32 devices in a mesh: gx: 2 (over x), gy: 4 (over y, core), gz: 4 (over z).
Axes of the slice: x: 2, y: 2, z: 4, core: 2. Of those that a mesh axis runs over, the one named last changes fastest.
Arguments:
- inputs: bfloat16 [384, 6144], P(('gx', 'gz'), 'gy'), may hold values from -6 to 6
- cotangent: bfloat16 [384, 6144], P(('gx', 'gz'), 'gy'), may hold values from -1.1953125 to 1.1953125
- up_weight: bfloat16 [6144, 24576], P('gy', ('gz', 'gx')), may hold values from -0.078125 to 0.078125
- down_weight: bfloat16 [24576, 6144], P(('gz', 'gx'), 'gy'), may hold values from -0.0390625 to 0.0390625
Outputs:
- grad_inputs: bfloat16 [384, 6144], P(('gx', 'gz'), 'gy')
- grad_up: float32 [6144, 24576], P('gy', ('gz', 'gx'))
- grad_down: float32 [24576, 6144], P(('gz', 'gx'), 'gy')
The draws below stay inside these ranges and needn't reach their ends.
All inputs are finite; a program needn't handle non-finite values.
Results may differ from the reference program's by a relative error of at most 0.0049.
Values may be sent and summed in bfloat16 or wider, within the bound.
No kernel may reach another device: no remote copies, remote signals or barrier semaphores. Data moves between devices by JAX's collectives and lax.ppermute only.
A program may use at most 192 MiB of HBM per device.

```python
import jax
import jax.numpy as jnp

D = 6144
FF = 24576
TOKENS = 384


def levels(rng, dims, cuts, low, top_value):
    level = 1.0
    for position, blocks in cuts:
        draws = jax.random.uniform(jax.random.fold_in(jax.random.fold_in(rng, 6), position), (blocks,), jnp.float32, low / len(cuts), top_value / len(cuts))
        level = level * jnp.repeat(jnp.exp(draws), dims[position] // blocks).reshape((-1,) + (1,) * (len(dims) - 1 - position))
    return level


def centred(key, shape, spread, most, cuts=(), dtype=jnp.bfloat16):
    array = spread * jax.random.normal(key, shape, jnp.float32)
    if cuts:
        array = array * levels(key, shape, cuts, -0.22, 0.18)
    return jnp.clip(array, -most, most).astype(dtype)


def setup_inputs(seed: int = 0) -> dict:
    key_list = jax.random.split(jax.random.key(seed), 5)
    inputs = centred(key_list[0], (TOKENS, D), 1.0, 6.0, ((0, 8), (1, 4)))
    cotangent = centred(key_list[1], (TOKENS, D), 0.2, 1.1953125, ((0, 8), (1, 4)))
    up_weight = centred(key_list[2], (D, FF), D ** -0.5, 0.078125, ((0, 4), (1, 8)))
    down_weight = centred(key_list[3], (FF, D), FF ** -0.5, 0.0390625, ((0, 8), (1, 4)))
    return dict(inputs=inputs, cotangent=cotangent, up_weight=up_weight, down_weight=down_weight)


def gelu_exact(value):
    return jax.nn.gelu(value, approximate=False)

def reference(inputs, cotangent, up_weight, down_weight):
    preact = jnp.dot(inputs, up_weight, preferred_element_type=jnp.float32)
    grad_hidden = jnp.dot(cotangent, down_weight.T, preferred_element_type=jnp.float32)
    activated, pullback = jax.vjp(gelu_exact, preact)
    grad_preact = pullback(grad_hidden)[0].astype(jnp.bfloat16)
    hidden = activated.astype(jnp.bfloat16)
    grad_down = jnp.dot(hidden.T, cotangent, preferred_element_type=jnp.float32)
    grad_up = jnp.dot(inputs.T, grad_preact, preferred_element_type=jnp.float32)
    grad_inputs = jnp.dot(grad_preact, up_weight.T, preferred_element_type=jnp.float32).astype(jnp.bfloat16)
    return (grad_inputs, grad_up, grad_down)
```

```python
import functools

import jax
import jax.numpy as jnp
from jax import lax
from jax.experimental import pallas as pl
from jax.experimental.pallas import tpu as pltpu
from jax.sharding import PartitionSpec as P

F32 = jnp.float32
BF16 = jnp.bfloat16
VMEM_LIMIT = 40 * 1024 * 1024


def gelu_exact(value):
    return jax.nn.gelu(value, approximate=False)


def activate(preact, grad_hidden):
    activated, pullback = jax.vjp(gelu_exact, preact)
    grad_preact = pullback(grad_hidden)[0]
    return (activated.astype(BF16), grad_preact.astype(BF16))


def contract(left, right, left_dim, right_dim):
    return lax.dot_general(
        left, right, (((left_dim,), (right_dim,)), ((), ())), preferred_element_type=F32
    )


def general_body(inputs, cotangent, up_weight, down_weight):
    all_inputs = lax.all_gather(inputs, ("gx", "gz"), axis=0, tiled=True)
    all_cotan = lax.all_gather(cotangent, ("gx", "gz"), axis=0, tiled=True)
    preact = lax.psum_scatter(
        contract(all_inputs, up_weight, 1, 0), "gy", scatter_dimension=0, tiled=True
    )
    grad_hidden = lax.psum_scatter(
        contract(all_cotan, down_weight, 1, 1), "gy", scatter_dimension=0, tiled=True
    )
    hidden, grad_preact = activate(preact, grad_hidden)
    hidden = lax.all_gather(hidden, "gy", axis=0, tiled=True)
    grad_preact = lax.all_gather(grad_preact, "gy", axis=0, tiled=True)
    grad_down = contract(hidden, all_cotan, 0, 0)
    grad_up = contract(all_inputs, grad_preact, 0, 0)
    grad_inputs = lax.psum_scatter(
        contract(grad_preact, up_weight, 1, 1), ("gx", "gz"), scatter_dimension=0, tiled=True
    ).astype(BF16)
    return (grad_inputs, grad_up, grad_down)


def params():
    return pltpu.CompilerParams(vmem_limit_bytes=VMEM_LIMIT)


def tile_of(width, most):
    tile = most
    while width % tile:
        tile //= 2
    return tile


def partial_kernel(core_ref, own_ref, other_ref, up_ref, down_ref, keep_ref, send_ref):
    first = core_ref[0] == 0
    rows = own_ref.shape[1]
    for which in range(2):
        own, other = own_ref[which], other_ref[which]
        acts = jnp.concatenate(
            [jnp.where(first, own, other), jnp.where(first, other, own)], axis=0
        )
        if which == 0:
            part = contract(acts, up_ref[...], 1, 0)
        else:
            part = contract(acts, down_ref[...], 1, 1)
        keep_ref[which] = part[:rows]
        send_ref[which] = part[rows:].astype(BF16)


def partial_sums(core, own, other, up, down, start, width):
    _, rows, depth = own.shape
    tile = tile_of(width, 512)
    first = start // tile
    block = pl.BlockSpec((2, rows, depth), lambda i, c: (0, 0, 0))
    return pl.pallas_call(
        partial_kernel,
        grid_spec=pltpu.PrefetchScalarGridSpec(
            num_scalar_prefetch=1,
            grid=(width // tile,),
            in_specs=[
                block,
                block,
                pl.BlockSpec((depth, tile), lambda i, c: (0, first + i)),
                pl.BlockSpec((tile, depth), lambda i, c: (first + i, 0)),
            ],
            out_specs=[
                pl.BlockSpec((2, rows, tile), lambda i, c: (0, 0, i)),
                pl.BlockSpec((2, rows, tile), lambda i, c: (0, 0, i)),
            ],
        ),
        out_shape=[
            jax.ShapeDtypeStruct((2, rows, width), F32),
            jax.ShapeDtypeStruct((2, rows, width), BF16),
        ],
        compiler_params=params(),
        cost_estimate=pl.CostEstimate(
            flops=8 * rows * depth * width,
            bytes_accessed=4 * depth * width + 12 * rows * width,
            transcendentals=0,
        ),
        name="partial_sums",
    )(core, own, other, up, down)


def back_kernel(core_ref, mine_ref, theirs_ref, up_ref, stay_ref, go_ref):
    first = core_ref[0] == 0
    rows = mine_ref.shape[1]
    grads = jnp.concatenate([mine_ref[1], theirs_ref[1]], axis=0)
    part = contract(grads, up_ref[...], 1, 1)
    stay_ref[...] = jnp.where(first, part[:rows], part[rows:])
    go_ref[...] = jnp.where(first, part[rows:], part[:rows]).astype(BF16)


def back(core, mine, theirs, up):
    _, rows, width = mine.shape
    depth = up.shape[0]
    tile = tile_of(depth, 256)
    block = pl.BlockSpec((2, rows, width), lambda i, c: (0, 0, 0))
    out = pl.BlockSpec((rows, tile), lambda i, c: (0, i))
    return pl.pallas_call(
        back_kernel,
        grid_spec=pltpu.PrefetchScalarGridSpec(
            num_scalar_prefetch=1,
            grid=(depth // tile,),
            in_specs=[block, block, pl.BlockSpec((tile, width), lambda i, c: (i, 0))],
            out_specs=[out, out],
        ),
        out_shape=[
            jax.ShapeDtypeStruct((rows, depth), F32),
            jax.ShapeDtypeStruct((rows, depth), BF16),
        ],
        compiler_params=params(),
        cost_estimate=pl.CostEstimate(
            flops=4 * rows * depth * width,
            bytes_accessed=2 * depth * width + 6 * rows * depth,
            transcendentals=0,
        ),
        name="back",
    )(core, mine, theirs, up)


def grads_kernel(groups, core_ref, *refs):
    blocks = refs[: 2 * groups]
    acts = refs[2 * groups : 4 * groups]
    up_out, down_out, inputs_t, cotan = refs[4 * groups :]
    first = core_ref[0] == 0

    @pl.when(pl.program_id(0) == 0)
    def _():
        stacked = [[], []]
        for group in range(groups):
            own, other = blocks[2 * group], blocks[2 * group + 1]
            for which in range(2):
                stacked[which].append(jnp.where(first, own[which], other[which]))
                stacked[which].append(jnp.where(first, other[which], own[which]))
        inputs_t[...] = jnp.concatenate(stacked[0], axis=0).T
        cotan[...] = jnp.concatenate(stacked[1], axis=0)

    hidden = jnp.concatenate([ref[0] for ref in acts], axis=0)
    grad = jnp.concatenate([ref[1] for ref in acts], axis=0)
    up_out[...] = contract(inputs_t[...], grad, 1, 0)
    down_out[...] = contract(hidden, cotan[...], 0, 0)


def weight_grads(core, blocks, acts):
    groups = len(blocks) // 2
    _, rows, depth = blocks[0].shape
    width = acts[0].shape[2]
    tokens = rows * len(blocks)
    tile = tile_of(width, 256)
    block = pl.BlockSpec((2, rows, depth), lambda i, c: (0, 0, 0))
    act = pl.BlockSpec((2, rows, tile), lambda i, c: (0, 0, i))
    return pl.pallas_call(
        functools.partial(grads_kernel, groups),
        grid_spec=pltpu.PrefetchScalarGridSpec(
            num_scalar_prefetch=1,
            grid=(width // tile,),
            in_specs=[block] * len(blocks) + [act] * len(acts),
            out_specs=[
                pl.BlockSpec((depth, tile), lambda i, c: (0, i)),
                pl.BlockSpec((tile, depth), lambda i, c: (i, 0)),
            ],
            scratch_shapes=[pltpu.VMEM((depth, tokens), BF16), pltpu.VMEM((tokens, depth), BF16)],
        ),
        out_shape=[
            jax.ShapeDtypeStruct((depth, width), F32),
            jax.ShapeDtypeStruct((width, depth), F32),
        ],
        compiler_params=params(),
        cost_estimate=pl.CostEstimate(
            flops=4 * tokens * depth * width,
            bytes_accessed=8 * depth * width + 4 * tokens * (depth + width),
            transcendentals=0,
        ),
        name="weight_grads",
    )(core, *blocks, *acts)


def swap(value, axis, size, bits):
    return lax.ppermute(value, axis, [(i, i ^ bits) for i in range(size)])


def cube_body(gz, inputs, cotangent, up_weight, down_weight):
    width = up_weight.shape[1]
    core = (lax.axis_index("gy") % 2).astype(jnp.int32).reshape(1)
    mine = jnp.stack([inputs, cotangent])
    blocks = []
    for d in range(gz):
        own = mine if d == 0 else swap(mine, "gz", gz, d)
        blocks += [own, swap(own, "gx", 2, 1)]

    acts = []
    total = None
    for d in range(gz):
        own, other = blocks[2 * d : 2 * d + 2]
        keep, send = partial_sums(core, own, other, up_weight, down_weight, 0, width)
        near = swap(send, "gy", 4, 1)
        chip = (keep + near.astype(F32)).astype(BF16)
        far = swap(chip, "gy", 4, 2)
        summed = (keep + near.astype(F32)) + far.astype(F32)
        act = jnp.stack(activate(summed[0], summed[1]))
        act_near = swap(act, "gy", 4, 1)
        acts += [act, act_near]
        stay, go = back(core, act, act_near, up_weight)
        stay = stay + swap(go, "gx", 2, 1).astype(F32)
        if d:
            stay = swap(stay.astype(BF16), "gz", gz, d).astype(F32)
        total = stay if total is None else total + stay

    grad_up, grad_down = weight_grads(core, blocks, acts)
    return (total.astype(BF16), grad_up, grad_down)


def solution(mesh):
    placed = (
        P(("gx", "gz"), "gy"),
        P(("gx", "gz"), "gy"),
        P("gy", ("gz", "gx")),
        P(("gz", "gx"), "gy"),
    )
    gx, gy, gz = (mesh.shape[axis] for axis in ("gx", "gy", "gz"))
    if gx == 2 and gy == 4 and gz & (gz - 1) == 0:
        body = functools.partial(cube_body, gz)
    else:
        body = general_body
    return jax.shard_map(
        body,
        mesh=mesh,
        in_specs=placed,
        out_specs=(P(("gx", "gz"), "gy"), P("gy", ("gz", "gx")), P(("gz", "gx"), "gy")),
        check_vma=False,
    )
```

```python
import math

import jax
import jax.numpy as jnp
from jax import lax
from jax.experimental import pallas as pl
from jax.experimental.pallas import tpu as pltpu
from jax.sharding import PartitionSpec as P

F32 = jnp.float32
BF16 = jnp.bfloat16
VMEM_LIMIT = 24 * 1024 * 1024
COST_PART = 16


def gelu_exact(value):
    return jax.nn.gelu(value, approximate=False)


def activate(preact, grad_hidden):
    activated, pullback = jax.vjp(gelu_exact, preact)
    grad_preact = pullback(grad_hidden)[0]
    return (activated.astype(BF16), grad_preact.astype(BF16))


def contract(left, right, left_dim, right_dim):
    return lax.dot_general(
        left, right, (((left_dim,), (right_dim,)), ((), ())), preferred_element_type=F32
    )


def general_body(inputs, cotangent, up_weight, down_weight):
    all_inputs = lax.all_gather(inputs, ("gx", "gz"), axis=0, tiled=True)
    all_cotan = lax.all_gather(cotangent, ("gx", "gz"), axis=0, tiled=True)
    preact = lax.psum_scatter(
        contract(all_inputs, up_weight, 1, 0), "gy", scatter_dimension=0, tiled=True
    )
    grad_hidden = lax.psum_scatter(
        contract(all_cotan, down_weight, 1, 1), "gy", scatter_dimension=0, tiled=True
    )
    hidden, grad_preact = activate(preact, grad_hidden)
    hidden = lax.all_gather(hidden, "gy", axis=0, tiled=True)
    grad_preact = lax.all_gather(grad_preact, "gy", axis=0, tiled=True)
    grad_down = contract(hidden, all_cotan, 0, 0)
    grad_up = contract(all_inputs, grad_preact, 0, 0)
    grad_inputs = lax.psum_scatter(
        contract(grad_preact, up_weight, 1, 1), ("gx", "gz"), scatter_dimension=0, tiled=True
    ).astype(BF16)
    return (grad_inputs, grad_up, grad_down)


def tile_of(width, most):
    tile = most
    while width % tile:
        tile //= 2
    return tile


def call(body, core, operands, in_specs, outs, out_specs, grid, cost, name, after=(), scratch=(), aliases=None):
    after = list(after)
    inner = len(operands) + 1

    def kernel(*refs):
        body(*refs[:inner], *refs[inner + len(after) :])

    flops, moved = cost
    return pl.pallas_call(
        kernel,
        grid_spec=pltpu.PrefetchScalarGridSpec(
            num_scalar_prefetch=1,
            grid=grid,
            in_specs=list(in_specs) + [pl.BlockSpec(memory_space=pl.ANY)] * len(after),
            out_specs=out_specs,
            scratch_shapes=list(scratch),
        ),
        out_shape=outs,
        input_output_aliases=aliases or {},
        compiler_params=pltpu.CompilerParams(vmem_limit_bytes=VMEM_LIMIT),
        cost_estimate=pl.CostEstimate(
            flops=flops // COST_PART, bytes_accessed=moved // COST_PART, transcendentals=0
        ),
        name=name,
    )(core, *operands, *after)


def whole(shape):
    return pl.BlockSpec(shape, lambda i, c: (0,) * len(shape))


def side_of(core_ref, side):
    return core_ref[0] if side == 0 else 1 - core_ref[0]


def partial_sums(core, units, up, down, side, start, width, dtype, after=()):
    _, rows, depth = units[0].shape
    tokens = rows * len(units)
    half = up.shape[1] // 2
    tile = tile_of(width, 256)

    def body(core_ref, *refs):
        *unit_refs, up_ref, down_ref, out_ref, acts = refs

        @pl.when(pl.program_id(0) == 0)
        def _():
            for n, ref in enumerate(unit_refs):
                acts[:, n * rows : (n + 1) * rows, :] = ref[...]

        out_ref[0] = contract(acts[0], up_ref[...], 1, 0).astype(dtype)
        out_ref[1] = contract(acts[1], down_ref[...], 1, 1).astype(dtype)

    def place(i, c):
        return side_of(c, side) * (half // tile) + start // tile + i

    return call(
        body,
        core,
        [*units, up, down],
        [whole(units[0].shape)] * len(units)
        + [
            pl.BlockSpec((depth, tile), lambda i, c: (0, place(i, c))),
            pl.BlockSpec((tile, depth), lambda i, c: (place(i, c), 0)),
        ],
        jax.ShapeDtypeStruct((2, tokens, width), dtype),
        pl.BlockSpec((2, tokens, tile), lambda i, c: (0, 0, i)),
        (width // tile,),
        (4 * tokens * depth * width, 4 * depth * width),
        "sums_send" if side else "sums_keep",
        after,
        [pltpu.VMEM((2, tokens, depth), BF16)],
    )


def activations(core, keep, near, far, after=()):
    _, tokens, width = keep.shape
    tile = tile_of(width, 256)
    block = pl.BlockSpec((2, tokens, tile), lambda i, c: (0, 0, i))

    def body(core_ref, keep_ref, near_ref, far_ref, act_ref):
        def total(which):
            return keep_ref[which] + near_ref[which].astype(F32) + far_ref[which].astype(F32)

        preact = total(0)
        cdf = 0.5 + 0.5 * lax.erf(preact * (0.5**0.5))
        pdf = jnp.exp(-0.5 * preact * preact) * ((0.5 / math.pi) ** 0.5)
        act_ref[0] = (preact * cdf).astype(BF16)
        act_ref[1] = (total(1) * (cdf + preact * pdf)).astype(BF16)

    return call(
        body,
        core,
        [keep, near, far],
        [block] * 3,
        jax.ShapeDtypeStruct(keep.shape, BF16),
        block,
        (width // tile,),
        (60 * tokens * width, 20 * tokens * width),
        "activations",
        after,
    )


def back(core, keep, near, up, start, before, leave, after=()):
    _, tokens, width = keep.shape
    depth, half = up.shape[0], up.shape[1] // 2
    tile = tile_of(depth, 512)
    act = pl.BlockSpec((1, tokens, width), lambda i, c: (1, 0, 0))

    def body(core_ref, keep_ref, near_ref, up_keep, up_near, *refs):
        part = contract(keep_ref[0], up_keep[...], 1, 1) + contract(near_ref[0], up_near[...], 1, 1)
        if before is not None:
            part = part + refs[0][...]
        outs = refs[(before is not None) :]
        if leave is None:
            outs[0][...] = part
        else:
            outs[0][...] = part[:leave]
            if leave < tokens:
                outs[1][...] = part[leave:].astype(BF16)

    def weights(side):
        return pl.BlockSpec(
            (tile, width), lambda i, c: (i, side_of(c, side) * (half // width) + start // width)
        )

    kinds = [(tokens if leave is None else leave, F32)]
    if leave is not None and leave < tokens:
        kinds.append((tokens - leave, BF16))
    return call(
        body,
        core,
        [keep, near, up, up] + ([] if before is None else [before]),
        [act, act, weights(0), weights(1)]
        + ([] if before is None else [pl.BlockSpec((tokens, tile), lambda i, c: (0, i))]),
        [jax.ShapeDtypeStruct((rows, depth), dtype) for rows, dtype in kinds],
        [pl.BlockSpec((rows, tile), lambda i, c: (0, i)) for rows, _ in kinds],
        (depth // tile,),
        (4 * tokens * depth * width, 4 * depth * width + 4 * tokens * depth),
        "back",
        after,
    )


def arrange(core, units, after=()):
    _, rows, depth = units[0].shape
    tokens = rows * len(units)

    def body(core_ref, *refs):
        *unit_refs, inputs_t, cotan = refs
        inputs_t[...] = jnp.concatenate([ref[0] for ref in unit_refs], axis=0).T
        cotan[...] = jnp.concatenate([ref[1] for ref in unit_refs], axis=0)

    return call(
        body,
        core,
        units,
        [whole(units[0].shape)] * len(units),
        [jax.ShapeDtypeStruct((depth, tokens), BF16), jax.ShapeDtypeStruct((tokens, depth), BF16)],
        [whole((depth, tokens)), whole((tokens, depth))],
        (1,),
        (0, 8 * tokens * depth),
        "arrange",
        after,
    )


def weight_grads(core, inputs_t, cotan, sides, acts, start, width, shape, outputs, after=()):
    depth, full = shape
    tokens = cotan.shape[0]
    half = full // 2
    tile = tile_of(width, 256)
    steps = width // tile
    groups = len(acts[0])

    def act_spec(order, array, offset):
        def index(i, c):
            return (0, 0, offset // tile + jnp.clip(i - order * steps, 0, steps - 1))

        return pl.BlockSpec((2, array.shape[1], tile), index)

    def body(core_ref, inputs_ref, cotan_ref, *refs):
        up_out, down_out, done = refs[-3:]
        done[...] = jnp.zeros_like(done)
        for order in range(len(sides)):
            mine = refs[order * groups : (order + 1) * groups]

            @pl.when(pl.program_id(0) // steps == order)
            def _(mine=mine):
                hidden = jnp.concatenate([ref[0] for ref in mine], axis=0)
                grad = jnp.concatenate([ref[1] for ref in mine], axis=0)
                up_out[...] = contract(inputs_ref[...], grad, 1, 0)
                down_out[...] = contract(hidden, cotan_ref[...], 0, 0)

    def place(i, c):
        which = side_of(c, sides[0])
        if len(sides) > 1:
            which = jnp.where(i // steps == 0, which, 1 - which)
        return which * (half // tile) + start // tile + i % steps

    operands = [inputs_t, cotan]
    specs = [whole(inputs_t.shape), whole(cotan.shape)]
    for order in range(len(sides)):
        for array, offset in acts[order]:
            operands.append(array)
            specs.append(act_spec(order, array, offset))
    aliases = None
    if outputs is not None:
        aliases = {len(operands) + 1: 0, len(operands) + 2: 1}
        operands += list(outputs)
        specs += [pl.BlockSpec(memory_space=pl.ANY)] * 2
    many = width * len(sides)
    return call(
        body,
        core,
        operands,
        specs,
        [
            jax.ShapeDtypeStruct((depth, full), F32),
            jax.ShapeDtypeStruct((full, depth), F32),
            jax.ShapeDtypeStruct((8, 128), F32),
        ],
        [
            pl.BlockSpec((depth, tile), lambda i, c: (0, place(i, c))),
            pl.BlockSpec((tile, depth), lambda i, c: (place(i, c), 0)),
            whole((8, 128)),
        ],
        (steps * len(sides),),
        (4 * tokens * depth * many, 8 * depth * many),
        "weight_grads",
        after,
        aliases=aliases,
    )


def swap(value, axis, size, bits):
    return lax.ppermute(value, axis, [(i, i ^ bits) for i in range(size)])


def cube_body(inputs, cotangent, up, down):
    rows = inputs.shape[0]
    half = up.shape[1] // 2
    width = half // 3 if half % 384 == 0 else half
    chunks = half // width
    core = (lax.axis_index("gy") % 2).astype(jnp.int32).reshape(1)

    unit = {(0, 0): jnp.stack([inputs, cotangent])}
    unit[0, 1] = swap(unit[0, 0], "gx", 2, 1)
    for d in (1, 2, 3):
        unit[d, 0] = swap(unit[0, 0], "gz", 4, d)
        unit[d, 1] = swap(unit[d, 0], "gx", 2, 1)
    groups = [
        [unit[0, 0]],
        [unit[1, 0], unit[0, 1], unit[1, 1]],
        [unit[2, 0], unit[3, 0], unit[2, 1], unit[3, 1]],
    ]

    def sums(piece, side, after):
        group, start, size = piece
        dtype = F32 if side == 0 else BF16
        weights = (up, down)
        if group == 0:
            weights = [pltpu.with_memory_space_constraint(array, pltpu.HBM) for array in weights]
        return partial_sums(core, groups[group], *weights, side, start, size, dtype, after)

    def over_cores(keep, near):
        return (keep + near.astype(F32)).astype(BF16)

    pieces = [(0, 0, half)] + [(g, j * width, width) for g in (1, 2) for j in range(chunks)]
    near, keep, chip, far, act, act_near = {}, {}, {}, {}, {}, {}

    def send(n, after):
        out = sums(pieces[n], 1, after)
        near[n] = swap(out, "gy", 4, 1)
        return out

    def hold(n, after):
        keep[n] = sums(pieces[n], 0, after)
        chip[n] = over_cores(keep[n], near[n])
        far[n] = swap(chip[n], "gy", 4, 2)
        return chip[n]

    def ready(n, after):
        act[n] = activations(core, keep[n], near[n], far[n], after)
        act_near[n] = swap(act[n], "gy", 4, 1)
        return act[n]

    one, two = 1, 1 + chunks
    last = send(0, ())
    last = hold(0, [last])
    last = ready(0, [last])
    last = send(one, [last])
    for j in range(chunks):
        if j + 1 < chunks:
            last = send(one + j + 1, [last])
        last = hold(one + j, [last])
    stay0, = back(core, act[0], act_near[0], up, 0, None, rows, [last])
    last = send(two, [stay0])
    for j in range(chunks):
        if j + 1 < chunks:
            last = send(two + j + 1, [last])
        last = hold(two + j, [last])
    inputs_t, cotan = arrange(core, groups[0] + groups[1] + groups[2], [last])
    last = ready(one, [inputs_t])
    part = None
    for j in range(chunks):
        n = one + j
        if j + 1 < chunks:
            last = ready(n + 1, [last])
        out = back(
            core, act[n], act_near[n], up, j * width, part, rows if j + 1 == chunks else None, [last]
        )
        last = part = out[0]
    stay1, go1 = out
    near1 = swap(go1, "gx", 2, 1).astype(F32)
    total = stay0 + near1[:rows]
    far1 = swap((stay1 + near1[rows:]).astype(BF16), "gz", 4, 1)

    outputs, part, last = None, None, [stay1]
    shape = up.shape

    def gradients(j, sides, after):
        acts = [
            [(array[0], j * width), (array[one + j], 0), (array[two + j], 0)]
            for array in (act, act_near)
        ]
        acts = [acts[side] for side in sides]
        return weight_grads(
            core, inputs_t, cotan, sides, acts, j * width, width, shape, outputs, after
        )

    for j in range(chunks):
        n = two + j
        last = [ready(n, last)]
        final = j + 1 == chunks
        if final:
            *outputs, done = gradients(j, (0,), last)
            last = [done]
        out = back(
            core, act[n], act_near[n], up, j * width, part, 2 * rows if final else None, last
        )
        part = out[0]
        *outputs, done = gradients(j, (1,) if final else (0, 1), [part])
        last = [done]
    stay2, go2 = out
    stay2 = (stay2 + swap(go2, "gx", 2, 1).astype(F32)).astype(BF16)
    far2 = swap(stay2[:rows], "gz", 4, 2)
    far3 = swap(stay2[rows:], "gz", 4, 3)
    total = total + far1.astype(F32) + far2.astype(F32) + far3.astype(F32)
    return (total.astype(BF16), *outputs)


def solution(mesh):
    placed = (
        P(("gx", "gz"), "gy"),
        P(("gx", "gz"), "gy"),
        P("gy", ("gz", "gx")),
        P(("gz", "gx"), "gy"),
    )
    cube = tuple(mesh.shape[axis] for axis in ("gx", "gy", "gz")) == (2, 4, 4)
    return jax.shard_map(
        cube_body if cube else general_body,
        mesh=mesh,
        in_specs=placed,
        out_specs=(P(("gx", "gz"), "gy"), P("gy", ("gz", "gx")), P(("gz", "gx"), "gy")),
        check_vma=False,
    )
```

```python
import math

import jax
import jax.numpy as jnp
from jax import lax
from jax.experimental import pallas as pl
from jax.experimental.pallas import tpu as pltpu
from jax.sharding import PartitionSpec as P

F32 = jnp.float32
BF16 = jnp.bfloat16
VMEM_LIMIT = 24 * 1024 * 1024
COST_PART = 1


def gelu_exact(value):
    return jax.nn.gelu(value, approximate=False)


def activate(preact, grad_hidden):
    activated, pullback = jax.vjp(gelu_exact, preact)
    grad_preact = pullback(grad_hidden)[0]
    return (activated.astype(BF16), grad_preact.astype(BF16))


def contract(left, right, left_dim, right_dim):
    return lax.dot_general(
        left, right, (((left_dim,), (right_dim,)), ((), ())), preferred_element_type=F32
    )


def general_body(inputs, cotangent, up_weight, down_weight):
    all_inputs = lax.all_gather(inputs, ("gx", "gz"), axis=0, tiled=True)
    all_cotan = lax.all_gather(cotangent, ("gx", "gz"), axis=0, tiled=True)
    preact = lax.psum_scatter(
        contract(all_inputs, up_weight, 1, 0), "gy", scatter_dimension=0, tiled=True
    )
    grad_hidden = lax.psum_scatter(
        contract(all_cotan, down_weight, 1, 1), "gy", scatter_dimension=0, tiled=True
    )
    hidden, grad_preact = activate(preact, grad_hidden)
    hidden = lax.all_gather(hidden, "gy", axis=0, tiled=True)
    grad_preact = lax.all_gather(grad_preact, "gy", axis=0, tiled=True)
    grad_down = contract(hidden, all_cotan, 0, 0)
    grad_up = contract(all_inputs, grad_preact, 0, 0)
    grad_inputs = lax.psum_scatter(
        contract(grad_preact, up_weight, 1, 1), ("gx", "gz"), scatter_dimension=0, tiled=True
    ).astype(BF16)
    return (grad_inputs, grad_up, grad_down)


def tile_of(width, most):
    tile = most
    while width % tile:
        tile //= 2
    return tile


def call(body, core, operands, in_specs, outs, out_specs, grid, cost, name, after=(), scratch=(), aliases=None):
    after = list(after)
    inner = len(operands) + 1

    def kernel(*refs):
        body(*refs[:inner], *refs[inner + len(after) :])

    flops, moved = cost
    return pl.pallas_call(
        kernel,
        grid_spec=pltpu.PrefetchScalarGridSpec(
            num_scalar_prefetch=1,
            grid=grid,
            in_specs=list(in_specs) + [pl.BlockSpec(memory_space=pl.ANY)] * len(after),
            out_specs=out_specs,
            scratch_shapes=list(scratch),
        ),
        out_shape=outs,
        input_output_aliases=aliases or {},
        compiler_params=pltpu.CompilerParams(vmem_limit_bytes=VMEM_LIMIT),
        cost_estimate=pl.CostEstimate(
            flops=flops // COST_PART, bytes_accessed=moved // COST_PART, transcendentals=0
        ),
        name=name,
    )(core, *operands, *after)


def whole(shape):
    return pl.BlockSpec(shape, lambda i, c: (0,) * len(shape))


def side_of(core_ref, side):
    return core_ref[0] if side == 0 else 1 - core_ref[0]


def partial_sums(core, units, up, down, side, start, width, apart, after=()):
    _, rows, depth = units[0].shape
    tokens = rows * len(units)
    half = up.shape[1] // 2
    tile = tile_of(width, 256)
    dtype = BF16 if side else F32

    def body(core_ref, *refs):
        *unit_refs, up_ref, down_ref = refs[: len(units) + 2]
        *out_refs, acts = refs[len(units) + 2 :]

        @pl.when(pl.program_id(0) == 0)
        def _():
            for n, ref in enumerate(unit_refs):
                acts[:, n * rows : (n + 1) * rows, :] = ref[...]

        preact = contract(acts[0], up_ref[...], 1, 0)
        grad_hidden = contract(acts[1], down_ref[...], 1, 1)
        if apart:
            out_refs[0][...] = preact.astype(dtype)
            out_refs[1][...] = grad_hidden.astype(dtype)
        else:
            out_refs[0][0] = preact.astype(dtype)
            out_refs[0][1] = grad_hidden.astype(dtype)

    def place(i, c):
        return side_of(c, side) * (half // tile) + start // tile + i

    if apart:
        outs = [jax.ShapeDtypeStruct((tokens, width), dtype)] * 2
        specs = [pl.BlockSpec((tokens, tile), lambda i, c: (0, i))] * 2
    else:
        outs = [jax.ShapeDtypeStruct((2, tokens, width), dtype)]
        specs = [pl.BlockSpec((2, tokens, tile), lambda i, c: (0, 0, i))]

    return call(
        body,
        core,
        [*units, up, down],
        [whole(units[0].shape)] * len(units)
        + [
            pl.BlockSpec((depth, tile), lambda i, c: (0, place(i, c))),
            pl.BlockSpec((tile, depth), lambda i, c: (place(i, c), 0)),
        ],
        outs,
        specs,
        (width // tile,),
        (4 * tokens * depth * width, 4 * depth * width),
        "sums_send" if side else "sums_keep",
        after,
        [pltpu.VMEM((2, tokens, depth), BF16)],
    )


def combine(core, keep, near, after):
    _, tokens, width = keep.shape
    tile = tile_of(width, 512)
    both = pl.BlockSpec((2, tokens, tile), lambda i, c: (0, 0, i))
    one = pl.BlockSpec((tokens, tile), lambda i, c: (0, i))

    def body(core_ref, keep_ref, preact_ref, grad_ref, chip_ref):
        chip_ref[0] = (keep_ref[0] + preact_ref[...].astype(F32)).astype(BF16)
        chip_ref[1] = (keep_ref[1] + grad_ref[...].astype(F32)).astype(BF16)

    return call(
        body,
        core,
        [keep, *near],
        [both, one, one],
        jax.ShapeDtypeStruct(keep.shape, BF16),
        both,
        (width // tile,),
        (4 * tokens * width, 16 * tokens * width),
        "combine",
        after,
    )


def activations(core, keep, near, far, start, after=()):
    _, tokens, width = far.shape
    tile = tile_of(width, 256)
    first = start // tile
    both = pl.BlockSpec((2, tokens, tile), lambda i, c: (0, 0, first + i))
    both_here = pl.BlockSpec((2, tokens, tile), lambda i, c: (0, 0, i))
    one = pl.BlockSpec((tokens, tile), lambda i, c: (0, first + i))

    def body(core_ref, keep_ref, *refs):
        *near_refs, far_ref, act_ref = refs

        def total(which):
            part = near_refs[which][...] if len(near) > 1 else near_refs[0][which]
            return keep_ref[which] + part.astype(F32) + far_ref[which].astype(F32)

        preact = total(0)
        cdf = 0.5 + 0.5 * lax.erf(preact * (0.5**0.5))
        pdf = jnp.exp(-0.5 * preact * preact) * ((0.5 / math.pi) ** 0.5)
        act_ref[0] = (preact * cdf).astype(BF16)
        act_ref[1] = (total(1) * (cdf + preact * pdf)).astype(BF16)

    return call(
        body,
        core,
        [keep, *near, far],
        [both] + [one if len(near) > 1 else both] * len(near) + [both_here],
        jax.ShapeDtypeStruct(far.shape, BF16),
        both_here,
        (width // tile,),
        (60 * tokens * width, 20 * tokens * width),
        "activations",
        after,
    )


def back(core, keep, near, up, start, before, leave, after=()):
    _, tokens, width = keep.shape
    depth, half = up.shape[0], up.shape[1] // 2
    tile = tile_of(depth, 512)
    act = pl.BlockSpec((1, tokens, width), lambda i, c: (1, 0, 0))

    def body(core_ref, keep_ref, near_ref, up_keep, up_near, *refs):
        part = contract(keep_ref[0], up_keep[...], 1, 1) + contract(near_ref[0], up_near[...], 1, 1)
        if before is not None:
            part = part + refs[0][...]
        outs = refs[(before is not None) :]
        if leave is None:
            outs[0][...] = part
        else:
            outs[0][...] = part[:leave]
            if leave < tokens:
                outs[1][...] = part[leave:].astype(BF16)

    def weights(side):
        return pl.BlockSpec(
            (tile, width), lambda i, c: (i, side_of(c, side) * (half // width) + start // width)
        )

    kinds = [(tokens if leave is None else leave, F32)]
    if leave is not None and leave < tokens:
        kinds.append((tokens - leave, BF16))
    return call(
        body,
        core,
        [keep, near, up, up] + ([] if before is None else [before]),
        [act, act, weights(0), weights(1)]
        + ([] if before is None else [pl.BlockSpec((tokens, tile), lambda i, c: (0, i))]),
        [jax.ShapeDtypeStruct((rows, depth), dtype) for rows, dtype in kinds],
        [pl.BlockSpec((rows, tile), lambda i, c: (0, i)) for rows, _ in kinds],
        (depth // tile,),
        (4 * tokens * depth * width, 4 * depth * width + 4 * tokens * depth),
        "back",
        after,
    )


def arrange(core, units, after=()):
    _, rows, depth = units[0].shape
    tokens = rows * len(units)

    def body(core_ref, *refs):
        *unit_refs, inputs_t, cotan = refs
        inputs_t[...] = jnp.concatenate([ref[0] for ref in unit_refs], axis=0).T
        cotan[...] = jnp.concatenate([ref[1] for ref in unit_refs], axis=0)

    return call(
        body,
        core,
        units,
        [whole(units[0].shape)] * len(units),
        [jax.ShapeDtypeStruct((depth, tokens), BF16), jax.ShapeDtypeStruct((tokens, depth), BF16)],
        [whole((depth, tokens)), whole((tokens, depth))],
        (1,),
        (0, 8 * tokens * depth),
        "arrange",
        after,
    )


def weight_grads(core, inputs_t, cotan, side, acts, start, width, shape, outputs, after=()):
    depth, full = shape
    tokens = cotan.shape[0]
    half = full // 2
    tile = tile_of(width, 256)
    groups = len(acts)

    def body(core_ref, inputs_ref, cotan_ref, *refs):
        up_out, down_out, done = refs[-3:]
        done[...] = jnp.zeros_like(done)
        hidden = jnp.concatenate([ref[0] for ref in refs[:groups]], axis=0)
        grad = jnp.concatenate([ref[1] for ref in refs[:groups]], axis=0)
        up_out[...] = contract(inputs_ref[...], grad, 1, 0)
        down_out[...] = contract(hidden, cotan_ref[...], 0, 0)

    def place(i, c):
        return side_of(c, side) * (half // tile) + start // tile + i

    operands = [inputs_t, cotan]
    specs = [whole(inputs_t.shape), whole(cotan.shape)]
    for array, offset in acts:
        first = offset // tile
        operands.append(array)
        specs.append(
            pl.BlockSpec((2, array.shape[1], tile), lambda i, c, first=first: (0, 0, first + i))
        )
    aliases = None
    if outputs is not None:
        aliases = {len(operands) + 1: 0, len(operands) + 2: 1}
        operands += list(outputs)
        specs += [pl.BlockSpec(memory_space=pl.ANY)] * 2
    return call(
        body,
        core,
        operands,
        specs,
        [
            jax.ShapeDtypeStruct((depth, full), F32),
            jax.ShapeDtypeStruct((full, depth), F32),
            jax.ShapeDtypeStruct((8, 128), F32),
        ],
        [
            pl.BlockSpec((depth, tile), lambda i, c: (0, place(i, c))),
            pl.BlockSpec((tile, depth), lambda i, c: (place(i, c), 0)),
            whole((8, 128)),
        ],
        (width // tile,),
        (4 * tokens * depth * width, 8 * depth * width),
        "weight_grads",
        after,
        aliases=aliases,
    )


def swap(value, axis, size, bits):
    return lax.ppermute(value, axis, [(i, i ^ bits) for i in range(size)])


def cube_body(inputs, cotangent, up, down):
    rows = inputs.shape[0]
    half = up.shape[1] // 2
    width = half // 3 if half % 384 == 0 else half
    chunks = half // width
    core = (lax.axis_index("gy") % 2).astype(jnp.int32).reshape(1)

    unit = {(0, 0): jnp.stack([inputs, cotangent])}
    unit[0, 1] = swap(unit[0, 0], "gx", 2, 1)
    for d in (1, 2, 3):
        unit[d, 0] = swap(unit[0, 0], "gz", 4, d)
        unit[d, 1] = swap(unit[d, 0], "gx", 2, 1)
    groups = [
        [unit[0, 0]],
        [unit[1, 0], unit[0, 1]],
        [unit[2, 0], unit[1, 1]],
        [unit[3, 0], unit[2, 1], unit[3, 1]],
    ]

    pieces = [(g, 0, half) for g in range(3)] + [(3, j * width, width) for j in range(chunks)]
    near, keep, far, act, act_near = {}, {}, {}, {}, {}

    def sums(group, side, after):
        weights = (up, down)
        if group == 0:
            weights = [pltpu.with_memory_space_constraint(array, pltpu.HBM) for array in weights]
        apart = side == 1 and group != 2
        return partial_sums(core, groups[group], *weights, side, 0, half, apart, after)

    def product(group, after, between=()):
        out = sums(group, 1, after)
        near[group] = [swap(array, "gy", 4, 1) for array in out]
        keep[group], = sums(group, 0, [out[0], *between])
        return [keep[group]]

    def cross(n, after=()):
        group, start, size = pieces[n]
        span = slice(start, start + size)
        parts = near[group] if len(near[group]) > 1 else near[group][0]
        if after:
            chip = combine(core, keep[group], parts, after)
        else:
            chip = jnp.stack([
                (keep[group][which, :, span] + parts[which][:, span].astype(F32)).astype(BF16)
                for which in range(2)
            ])
        far[n] = swap(chip, "gy", 4, 2)
        return [chip]

    def ready(n, after):
        group, start, _ = pieces[n]
        act[n] = activations(core, keep[group], near[group], far[n], start, after)
        act_near[n] = swap(act[n], "gy", 4, 1)
        return [act[n]]

    def inward(n, part, leave, after):
        group, start, _ = pieces[n]
        return back(core, act[n], act_near[n], up, start, part, leave, after)

    outputs = None

    def gradients(j, side, after):
        array = act_near if side else act
        acts = [(array[n], j * width) for n in range(3)] + [(array[3 + j], 0)]
        return weight_grads(
            core, inputs_t, cotan, side, acts, j * width, width, up.shape, outputs, after
        )

    def exchange(value):
        return swap(value, "gx", 2, 1).astype(F32)

    last = product(0, (), [unit[1, 0], unit[0, 1]])
    last = cross(0)
    last = product(1, last, [unit[2, 0]])
    last = ready(0, last)
    last = cross(1, last)
    last = product(2, last)
    total, = last = inward(0, None, rows, last)
    last = ready(1, [*last, unit[2, 1], unit[3, 1]])
    last = cross(2) + last
    last = product(3, last)
    stay1, go1 = inward(1, None, rows, last)
    last = ready(2, [stay1])
    for j in range(chunks):
        last = cross(3 + j) + last
    inputs_t, cotan = arrange(core, [u for group in groups for u in group], last)
    stay2, go2 = inward(2, None, rows, [inputs_t])
    total = total + exchange(go1)
    back1 = (stay1 + exchange(go2)).astype(BF16)
    far1 = swap(back1, "gz", 4, 1)

    part, last = None, [stay2]
    for j in range(chunks):
        n = 3 + j
        last = ready(n, last)
        if j + 1 < chunks:
            *outputs, done = gradients(j, 0, last)
            part, = inward(n, part, None, [done])
            *outputs, done = gradients(j, 1, [part] if j else [part, back1])
            last = [done]
        else:
            stay3, go3 = inward(n, part, rows, last)
            near3 = exchange(go3)
            *outputs, done = gradients(j, 0, [stay3])
            back2 = (stay2 + near3[:rows]).astype(BF16)
            back3 = (stay3 + near3[rows:]).astype(BF16)
            far2 = swap(back2, "gz", 4, 2)
            far3 = swap(back3, "gz", 4, 3)
            *outputs, done = gradients(j, 1, [done, back2, back3])
    total = total + far1.astype(F32) + far2.astype(F32) + far3.astype(F32)
    return (total.astype(BF16), *outputs)


def solution(mesh):
    placed = (
        P(("gx", "gz"), "gy"),
        P(("gx", "gz"), "gy"),
        P("gy", ("gz", "gx")),
        P(("gz", "gx"), "gy"),
    )
    cube = tuple(mesh.shape[axis] for axis in ("gx", "gy", "gz")) == (2, 4, 4)
    return jax.shard_map(
        cube_body if cube else general_body,
        mesh=mesh,
        in_specs=placed,
        out_specs=(P(("gx", "gz"), "gy"), P("gy", ("gz", "gx")), P(("gz", "gx"), "gy")),
        check_vma=False,
    )
```

```python
import math

import jax
import jax.numpy as jnp
from jax import lax
from jax.experimental import pallas as pl
from jax.experimental.pallas import tpu as pltpu
from jax.sharding import PartitionSpec as P

F32 = jnp.float32
BF16 = jnp.bfloat16
VMEM_LIMIT = 24 * 1024 * 1024
COST_PART = 1


def gelu_exact(value):
    return jax.nn.gelu(value, approximate=False)


def activate(preact, grad_hidden):
    activated, pullback = jax.vjp(gelu_exact, preact)
    grad_preact = pullback(grad_hidden)[0]
    return (activated.astype(BF16), grad_preact.astype(BF16))


def contract(left, right, left_dim, right_dim):
    return lax.dot_general(
        left, right, (((left_dim,), (right_dim,)), ((), ())), preferred_element_type=F32
    )


def general_body(inputs, cotangent, up_weight, down_weight):
    all_inputs = lax.all_gather(inputs, ("gx", "gz"), axis=0, tiled=True)
    all_cotan = lax.all_gather(cotangent, ("gx", "gz"), axis=0, tiled=True)
    preact = lax.psum_scatter(
        contract(all_inputs, up_weight, 1, 0), "gy", scatter_dimension=0, tiled=True
    )
    grad_hidden = lax.psum_scatter(
        contract(all_cotan, down_weight, 1, 1), "gy", scatter_dimension=0, tiled=True
    )
    hidden, grad_preact = activate(preact, grad_hidden)
    hidden = lax.all_gather(hidden, "gy", axis=0, tiled=True)
    grad_preact = lax.all_gather(grad_preact, "gy", axis=0, tiled=True)
    grad_down = contract(hidden, all_cotan, 0, 0)
    grad_up = contract(all_inputs, grad_preact, 0, 0)
    grad_inputs = lax.psum_scatter(
        contract(grad_preact, up_weight, 1, 1), ("gx", "gz"), scatter_dimension=0, tiled=True
    ).astype(BF16)
    return (grad_inputs, grad_up, grad_down)


def tile_of(width, most):
    tile = most
    while width % tile:
        tile //= 2
    return tile


def call(body, core, operands, in_specs, outs, out_specs, grid, cost, name, after=(), scratch=(), aliases=None):
    after = list(after)
    inner = len(operands) + 1

    def kernel(*refs):
        body(*refs[:inner], *refs[inner + len(after) :])

    flops, moved = cost
    return pl.pallas_call(
        kernel,
        grid_spec=pltpu.PrefetchScalarGridSpec(
            num_scalar_prefetch=1,
            grid=grid,
            in_specs=list(in_specs) + [pl.BlockSpec(memory_space=pl.ANY)] * len(after),
            out_specs=out_specs,
            scratch_shapes=list(scratch),
        ),
        out_shape=outs,
        input_output_aliases=aliases or {},
        compiler_params=pltpu.CompilerParams(vmem_limit_bytes=VMEM_LIMIT),
        cost_estimate=pl.CostEstimate(
            flops=flops // COST_PART, bytes_accessed=moved // COST_PART, transcendentals=0
        ),
        name=name,
    )(core, *operands, *after)


def whole(shape):
    return pl.BlockSpec(shape, lambda i, c: (0,) * len(shape))


def side_of(core_ref, side):
    return core_ref[0] if side == 0 else 1 - core_ref[0]


def partial_sums(core, units, up, down, side, apart, load, after=()):
    _, rows, depth = units[0].shape
    tokens = rows * len(units)
    width = up.shape[1] // 2 if load else up.shape[1]
    tile = tile_of(width, 256)
    dtype = BF16 if side else F32

    def body(core_ref, *refs):
        *unit_refs, up_ref, down_ref = refs[: len(units) + 2]
        *out_refs, acts = refs[len(units) + 2 :]

        @pl.when(pl.program_id(0) == 0)
        def _():
            for n, ref in enumerate(unit_refs):
                acts[:, n * rows : (n + 1) * rows, :] = ref[...]

        if load:
            out_refs[-2][...] = up_ref[...]
            out_refs[-1][...] = down_ref[...]
        preact = contract(acts[0], up_ref[...], 1, 0)
        grad_hidden = contract(acts[1], down_ref[...], 1, 1)
        if apart:
            out_refs[0][...] = preact.astype(dtype)
            out_refs[1][...] = grad_hidden.astype(dtype)
        else:
            out_refs[0][0] = preact.astype(dtype)
            out_refs[0][1] = grad_hidden.astype(dtype)

    def place(i, c):
        return side_of(c, side) * (width // tile) + i if load else i

    if apart:
        outs = [jax.ShapeDtypeStruct((tokens, width), dtype)] * 2
        specs = [pl.BlockSpec((tokens, tile), lambda i, c: (0, i))] * 2
    else:
        outs = [jax.ShapeDtypeStruct((2, tokens, width), dtype)]
        specs = [pl.BlockSpec((2, tokens, tile), lambda i, c: (0, 0, i))]
    if load:
        outs += [jax.ShapeDtypeStruct((depth, width), BF16), jax.ShapeDtypeStruct((width, depth), BF16)]
        specs += [
            pl.BlockSpec((depth, tile), lambda i, c: (0, i)),
            pl.BlockSpec((tile, depth), lambda i, c: (i, 0)),
        ]
        up, down = (pltpu.with_memory_space_constraint(array, pltpu.HBM) for array in (up, down))

    return call(
        body,
        core,
        [*units, up, down],
        [whole(units[0].shape)] * len(units)
        + [
            pl.BlockSpec((depth, tile), lambda i, c: (0, place(i, c))),
            pl.BlockSpec((tile, depth), lambda i, c: (place(i, c), 0)),
        ],
        outs,
        specs,
        (width // tile,),
        (4 * tokens * depth * width, 4 * depth * width),
        "sums_send" if side else "sums_keep",
        after,
        [pltpu.VMEM((2, tokens, depth), BF16)],
    )


def combine(core, keep, near, after):
    _, tokens, width = keep.shape
    tile = tile_of(width, 512)
    both = pl.BlockSpec((2, tokens, tile), lambda i, c: (0, 0, i))
    one = pl.BlockSpec((tokens, tile), lambda i, c: (0, i))

    def body(core_ref, keep_ref, preact_ref, grad_ref, chip_ref):
        chip_ref[0] = (keep_ref[0] + preact_ref[...].astype(F32)).astype(BF16)
        chip_ref[1] = (keep_ref[1] + grad_ref[...].astype(F32)).astype(BF16)

    return call(
        body,
        core,
        [keep, *near],
        [both, one, one],
        jax.ShapeDtypeStruct(keep.shape, BF16),
        both,
        (width // tile,),
        (4 * tokens * width, 16 * tokens * width),
        "combine",
        after,
    )


def activations(core, keep, near, far, start, after=()):
    _, tokens, width = far.shape
    tile = tile_of(width, 256)
    first = start // tile
    both = pl.BlockSpec((2, tokens, tile), lambda i, c: (0, 0, first + i))
    both_here = pl.BlockSpec((2, tokens, tile), lambda i, c: (0, 0, i))
    one = pl.BlockSpec((tokens, tile), lambda i, c: (0, first + i))

    def body(core_ref, keep_ref, *refs):
        *near_refs, far_ref, act_ref = refs

        def total(which):
            part = near_refs[which][...] if len(near) > 1 else near_refs[0][which]
            return keep_ref[which] + part.astype(F32) + far_ref[which].astype(F32)

        preact = total(0)
        cdf = 0.5 + 0.5 * lax.erf(preact * (0.5**0.5))
        pdf = jnp.exp(-0.5 * preact * preact) * ((0.5 / math.pi) ** 0.5)
        act_ref[0] = (preact * cdf).astype(BF16)
        act_ref[1] = (total(1) * (cdf + preact * pdf)).astype(BF16)

    return call(
        body,
        core,
        [keep, *near, far],
        [both] + [one if len(near) > 1 else both] * len(near) + [both_here],
        jax.ShapeDtypeStruct(far.shape, BF16),
        both_here,
        (width // tile,),
        (60 * tokens * width, 20 * tokens * width),
        "activations",
        after,
    )


def back(core, acts, ups, start, before, order, leave, after=()):
    width = acts[0][0].shape[2]
    tokens = sum(keep.shape[1] for keep, _ in acts)
    depth = ups[0].shape[0]
    tile = tile_of(depth, 512)
    groups = len(acts)

    def body(core_ref, *refs):
        part = None
        for side in range(2):
            mine = [ref[0] for ref in refs[side * groups : (side + 1) * groups]]
            mine = mine[0] if groups == 1 else jnp.concatenate(mine, axis=0)
            term = contract(mine, refs[2 * groups + side][...], 1, 1)
            part = term if part is None else part + term
        refs = refs[2 * groups + 2 :]
        if before is not None:
            part = part + refs[0][...]
        outs = refs[(before is not None) :]
        if leave is None:
            outs[0][...] = part
        else:
            rows = tokens // len(order)
            part = [part[n * rows : (n + 1) * rows] for n in order]
            outs[0][...] = jnp.concatenate(part[:leave], axis=0) if leave > 1 else part[0]
            outs[1][...] = jnp.concatenate(part[leave:], axis=0).astype(BF16)

    kinds = [(tokens, F32)]
    if leave is not None:
        rows = tokens // len(order)
        kinds = [(leave * rows, F32), (tokens - leave * rows, BF16)]
    operands = [which[side] for side in range(2) for which in acts]
    return call(
        body,
        core,
        [*operands, *ups] + ([] if before is None else [before]),
        [pl.BlockSpec((1, array.shape[1], width), lambda i, c: (1, 0, 0)) for array in operands]
        + [pl.BlockSpec((tile, width), lambda i, c: (i, start // width))] * 2
        + ([] if before is None else [pl.BlockSpec((tokens, tile), lambda i, c: (0, i))]),
        [jax.ShapeDtypeStruct((rows, depth), dtype) for rows, dtype in kinds],
        [pl.BlockSpec((rows, tile), lambda i, c: (0, i)) for rows, _ in kinds],
        (depth // tile,),
        (4 * tokens * depth * width, 4 * depth * width + 4 * tokens * depth),
        "back",
        after,
    )


def fold(core, stay, near, after=()):
    rows, depth = stay.shape

    def body(core_ref, stay_ref, near_ref, out_ref):
        out_ref[...] = (stay_ref[...] + near_ref[...].astype(F32)).astype(BF16)

    return call(
        body,
        core,
        [stay, near],
        [whole(stay.shape)] * 2,
        jax.ShapeDtypeStruct(stay.shape, BF16),
        whole(stay.shape),
        (1,),
        (rows * depth, 8 * rows * depth),
        "fold",
        after,
    )


def arrange(core, units, after=()):
    _, rows, depth = units[0].shape
    tokens = rows * len(units)

    def body(core_ref, *refs):
        *unit_refs, inputs_t, cotan = refs
        inputs_t[...] = jnp.concatenate([ref[0] for ref in unit_refs], axis=0).T
        cotan[...] = jnp.concatenate([ref[1] for ref in unit_refs], axis=0)

    return call(
        body,
        core,
        units,
        [whole(units[0].shape)] * len(units),
        [jax.ShapeDtypeStruct((depth, tokens), BF16), jax.ShapeDtypeStruct((tokens, depth), BF16)],
        [whole((depth, tokens)), whole((tokens, depth))],
        (1,),
        (0, 8 * tokens * depth),
        "arrange",
        after,
    )


def weight_grads(core, inputs_t, cotan, sides, acts, start, width, shape, outputs, after=()):
    depth, full = shape
    tokens = cotan.shape[0]
    half = full // 2
    tile = tile_of(width, 256)
    steps = width // tile
    groups = len(acts[0])

    def body(core_ref, inputs_ref, cotan_ref, *refs):
        up_out, down_out, done = refs[-3:]
        done[...] = jnp.zeros_like(done)
        for order in range(len(sides)):
            mine = refs[order * groups : (order + 1) * groups]

            @pl.when(pl.program_id(0) // steps == order)
            def _(mine=mine):
                hidden = jnp.concatenate([ref[0] for ref in mine], axis=0)
                grad = jnp.concatenate([ref[1] for ref in mine], axis=0)
                up_out[...] = contract(inputs_ref[...], grad, 1, 0)
                down_out[...] = contract(hidden, cotan_ref[...], 0, 0)

    def place(i, c):
        which = side_of(c, sides[0])
        if len(sides) > 1:
            which = jnp.where(i // steps == 0, which, 1 - which)
        return which * (half // tile) + start // tile + i % steps

    operands = [inputs_t, cotan]
    specs = [whole(inputs_t.shape), whole(cotan.shape)]
    for order in range(len(sides)):
        for array, offset in acts[order]:

            def index(i, c, order=order, first=offset // tile):
                return (0, 0, first + jnp.clip(i - order * steps, 0, steps - 1))

            operands.append(array)
            specs.append(pl.BlockSpec((2, array.shape[1], tile), index))
    aliases = None
    if outputs is not None:
        aliases = {len(operands) + 1: 0, len(operands) + 2: 1}
        operands += list(outputs)
        specs += [pl.BlockSpec(memory_space=pl.ANY)] * 2
    many = width * len(sides)
    return call(
        body,
        core,
        operands,
        specs,
        [
            jax.ShapeDtypeStruct((depth, full), F32),
            jax.ShapeDtypeStruct((full, depth), F32),
            jax.ShapeDtypeStruct((8, 128), F32),
        ],
        [
            pl.BlockSpec((depth, tile), lambda i, c: (0, place(i, c))),
            pl.BlockSpec((tile, depth), lambda i, c: (place(i, c), 0)),
            whole((8, 128)),
        ],
        (steps * len(sides),),
        (4 * tokens * depth * many, 8 * depth * many),
        "weight_grads",
        after,
        aliases=aliases,
    )


def swap(value, axis, size, bits):
    return lax.ppermute(value, axis, [(i, i ^ bits) for i in range(size)])


def cube_body(inputs, cotangent, up, down):
    rows = inputs.shape[0]
    half = up.shape[1] // 2
    width = half // 3 if half % 384 == 0 else half
    chunks = half // width
    core = (lax.axis_index("gy") % 2).astype(jnp.int32).reshape(1)

    unit = {(0, 0): jnp.stack([inputs, cotangent])}
    unit[0, 1] = swap(unit[0, 0], "gx", 2, 1)
    unit[1, 0] = swap(unit[0, 0], "gz", 4, 1)
    z = lax.axis_index("gz")
    middle = (z == 1) | (z == 2)
    across, outward = [(1, 2), (2, 1)], [(1, 0), (2, 3)]
    first = lax.ppermute(unit[0, 0], "gz", across)
    second = lax.ppermute(unit[1, 0], "gz", across)
    first_on = lax.ppermute(first, "gz", outward)
    second_on = lax.ppermute(second, "gz", outward)
    unit[2, 0] = jnp.where(middle, second, first_on)
    unit[3, 0] = jnp.where(middle, first, second_on)
    for d in (1, 2, 3):
        unit[d, 1] = swap(unit[d, 0], "gx", 2, 1)
    groups = [
        [unit[0, 0], unit[0, 1]],
        [unit[1, 0], unit[1, 1]],
        [unit[2, 0], unit[3, 0], unit[2, 1], unit[3, 1]],
    ]

    pieces = [(0, 0, half), (1, 0, half)] + [(2, j * width, width) for j in range(chunks)]
    near, keep, far, act, act_near, ups, downs = {}, {}, {}, {}, {}, {}, {}

    def sums(group, side, after):
        if group:
            return partial_sums(
                core, groups[group], ups[side], downs[side], side, side == 1, False, after
            )
        *out, ups[side], downs[side] = partial_sums(
            core, groups[group], up, down, side, side == 1, True, after
        )
        return out

    def product(group, after, between=()):
        out = sums(group, 1, after)
        near[group] = [swap(array, "gy", 4, 1) for array in out]
        keep[group], = sums(group, 0, [out[0], *between])
        return [keep[group]]

    def cross(n, after=()):
        group, start, size = pieces[n]
        span = slice(start, start + size)
        if after:
            chip = combine(core, keep[group], near[group], after)
        else:
            chip = jnp.stack([
                (keep[group][which, :, span] + near[group][which][:, span].astype(F32)).astype(BF16)
                for which in range(2)
            ])
        far[n] = swap(chip, "gy", 4, 2)
        return [chip]

    def ready(n, after):
        group, start, _ = pieces[n]
        act[n] = activations(core, keep[group], near[group], far[n], start, after)
        act_near[n] = swap(act[n], "gy", 4, 1)
        return [act[n]]

    def inward(many, start, part, order, leave, after):
        which = [(act[n], act_near[n]) for n in many]
        return back(core, which, (ups[0], ups[1]), start, part, order, leave, after)

    outputs = None

    def gradients(j, sides, after):
        acts = [
            [(array[n], j * width) for n in range(2)] + [(array[2 + j], 0)]
            for array in (act, act_near)
        ]
        acts = [acts[side] for side in sides]
        return weight_grads(
            core, inputs_t, cotan, sides, acts, j * width, width, up.shape, outputs, after
        )

    last = product(0, (), [unit[1, 0], first])
    last = cross(0, [unit[1, 1], first_on, second])
    last = product(1, last, [second_on])
    last = ready(0, last + [unit[2, 1]])
    last = cross(1, last + [])
    last = product(2, last)
    last = ready(1, last)
    for j in range(chunks):
        last = cross(2 + j) + last
    inputs_t, cotan = arrange(core, [u for group in groups for u in group], last)
    stay1, go1 = inward((0, 1), 0, None, (0, 2, 1, 3), 2, [inputs_t])
    near1 = swap(go1, "gx", 2, 1)

    part, last = None, [stay1]
    for j in range(chunks):
        n = 2 + j
        last = ready(n, last)
        if j == 0:
            total = stay1[:rows] + near1[:rows].astype(F32)
            back1 = fold(core, stay1[rows:], near1[rows:], last)
            far1 = swap(back1, "gz", 4, 1)
            last = [back1]
        if j + 1 < chunks:
            last = part, = inward((n,), j * width, part, None, None, last)
            *outputs, done = gradients(j, (0, 1), last)
            last = [done]
        else:
            stay2, go2 = inward((n,), j * width, part, (0, 1, 2, 3), 2, last)
            near2 = swap(go2, "gx", 2, 1)
            *outputs, done = gradients(j, (0,), [stay2])
            back2 = fold(core, stay2, near2, [done])
            far2 = swap(back2[:rows], "gz", 4, 2)
            far3 = swap(back2[rows:], "gz", 4, 3)
            *outputs, done = gradients(j, (1,), [back2])
    total = total + far1.astype(F32) + far2.astype(F32) + far3.astype(F32)
    return (total.astype(BF16), *outputs)


def solution(mesh):
    placed = (
        P(("gx", "gz"), "gy"),
        P(("gx", "gz"), "gy"),
        P("gy", ("gz", "gx")),
        P(("gz", "gx"), "gy"),
    )
    cube = tuple(mesh.shape[axis] for axis in ("gx", "gy", "gz")) == (2, 4, 4)
    return jax.shard_map(
        cube_body if cube else general_body,
        mesh=mesh,
        in_specs=placed,
        out_specs=(P(("gx", "gz"), "gy"), P("gy", ("gz", "gx")), P(("gz", "gx"), "gy")),
        check_vma=False,
    )
```

```python
import math

import jax
import jax.numpy as jnp
from jax import lax
from jax.experimental import pallas as pl
from jax.experimental.pallas import tpu as pltpu
from jax.sharding import PartitionSpec as P

F32 = jnp.float32
BF16 = jnp.bfloat16
VMEM_LIMIT = 24 * 1024 * 1024
COST_PART = 1


def gelu_exact(value):
    return jax.nn.gelu(value, approximate=False)


def activate(preact, grad_hidden):
    activated, pullback = jax.vjp(gelu_exact, preact)
    grad_preact = pullback(grad_hidden)[0]
    return (activated.astype(BF16), grad_preact.astype(BF16))


def contract(left, right, left_dim, right_dim):
    return lax.dot_general(
        left, right, (((left_dim,), (right_dim,)), ((), ())), preferred_element_type=F32
    )


def general_body(inputs, cotangent, up_weight, down_weight):
    all_inputs = lax.all_gather(inputs, ("gx", "gz"), axis=0, tiled=True)
    all_cotan = lax.all_gather(cotangent, ("gx", "gz"), axis=0, tiled=True)
    preact = lax.psum_scatter(
        contract(all_inputs, up_weight, 1, 0), "gy", scatter_dimension=0, tiled=True
    )
    grad_hidden = lax.psum_scatter(
        contract(all_cotan, down_weight, 1, 1), "gy", scatter_dimension=0, tiled=True
    )
    hidden, grad_preact = activate(preact, grad_hidden)
    hidden = lax.all_gather(hidden, "gy", axis=0, tiled=True)
    grad_preact = lax.all_gather(grad_preact, "gy", axis=0, tiled=True)
    grad_down = contract(hidden, all_cotan, 0, 0)
    grad_up = contract(all_inputs, grad_preact, 0, 0)
    grad_inputs = lax.psum_scatter(
        contract(grad_preact, up_weight, 1, 1), ("gx", "gz"), scatter_dimension=0, tiled=True
    ).astype(BF16)
    return (grad_inputs, grad_up, grad_down)


def tile_of(width, most):
    tile = most
    while width % tile:
        tile //= 2
    return tile


def call(body, core, operands, in_specs, outs, out_specs, grid, cost, name, after=(), scratch=(), aliases=None):
    after = list(after)
    inner = len(operands) + 1

    def kernel(*refs):
        body(*refs[:inner], *refs[inner + len(after) :])

    flops, moved = cost
    return pl.pallas_call(
        kernel,
        grid_spec=pltpu.PrefetchScalarGridSpec(
            num_scalar_prefetch=1,
            grid=grid,
            in_specs=list(in_specs) + [pl.BlockSpec(memory_space=pl.ANY)] * len(after),
            out_specs=out_specs,
            scratch_shapes=list(scratch),
        ),
        out_shape=outs,
        input_output_aliases=aliases or {},
        compiler_params=pltpu.CompilerParams(vmem_limit_bytes=VMEM_LIMIT),
        cost_estimate=pl.CostEstimate(
            flops=flops // COST_PART, bytes_accessed=moved // COST_PART, transcendentals=0
        ),
        name=name,
    )(core, *operands, *after)


def whole(shape):
    return pl.BlockSpec(shape, lambda i, c: (0,) * len(shape))


def side_of(core_ref, side):
    return core_ref[0] if side == 0 else 1 - core_ref[0]


def bring(core, up, down):
    depth, full = up.shape
    half = full // 2
    parts = 2

    def body(core_ref, up_ref, down_ref, *refs):
        *outs, sems = refs
        copies = []
        for side in range(2):
            begin = pl.multiple_of(side_of(core_ref, side) * half, half)
            up_out, down_out = outs[2 * side : 2 * side + 2]
            for part in range(parts):
                rows = pl.ds(part * (depth // parts), depth // parts)
                copies.append((up_ref.at[rows, pl.ds(begin, half)], up_out.at[rows]))
                size = half // parts
                rows = pl.ds(pl.multiple_of(begin + part * size, size), size)
                copies.append((down_ref.at[rows], down_out.at[pl.ds(part * size, size)]))
        copies = [
            pltpu.make_async_copy(source, target, sems.at[n])
            for n, (source, target) in enumerate(copies)
        ]
        for copy in copies:
            copy.start()
        for copy in copies:
            copy.wait()

    up, down = (pltpu.with_memory_space_constraint(array, pltpu.HBM) for array in (up, down))
    shapes = [(depth, half), (half, depth)] * 2
    return call(
        body,
        core,
        [up, down],
        [pl.BlockSpec(memory_space=pltpu.HBM)] * 2,
        [jax.ShapeDtypeStruct(shape, BF16) for shape in shapes],
        [pl.BlockSpec(memory_space=pl.ANY)] * 4,
        (1,),
        (0, 4 * depth * full),
        "bring",
        (),
        [pltpu.SemaphoreType.DMA((4 * parts,))],
    )


def partial_sums(core, units, up, down, side, apart, after=()):
    _, rows, depth = units[0].shape
    tokens = rows * len(units)
    width = up.shape[1]
    tile = tile_of(width, 256)
    dtype = BF16 if side else F32

    def body(core_ref, *refs):
        *unit_refs, up_ref, down_ref = refs[: len(units) + 2]
        *out_refs, acts = refs[len(units) + 2 :]

        @pl.when(pl.program_id(0) == 0)
        def _():
            for n, ref in enumerate(unit_refs):
                acts[:, n * rows : (n + 1) * rows, :] = ref[...]

        preact = contract(acts[0], up_ref[...], 1, 0)
        grad_hidden = contract(acts[1], down_ref[...], 1, 1)
        if apart:
            out_refs[0][...] = preact.astype(dtype)
            out_refs[1][...] = grad_hidden.astype(dtype)
        else:
            out_refs[0][0] = preact.astype(dtype)
            out_refs[0][1] = grad_hidden.astype(dtype)

    if apart:
        outs = [jax.ShapeDtypeStruct((tokens, width), dtype)] * 2
        specs = [pl.BlockSpec((tokens, tile), lambda i, c: (0, i))] * 2
    else:
        outs = [jax.ShapeDtypeStruct((2, tokens, width), dtype)]
        specs = [pl.BlockSpec((2, tokens, tile), lambda i, c: (0, 0, i))]
    return call(
        body,
        core,
        [*units, up, down],
        [whole(units[0].shape)] * len(units)
        + [
            pl.BlockSpec((depth, tile), lambda i, c: (0, i)),
            pl.BlockSpec((tile, depth), lambda i, c: (i, 0)),
        ],
        outs,
        specs,
        (width // tile,),
        (4 * tokens * depth * width, 4 * depth * width),
        "sums_send" if side else "sums_keep",
        after,
        [pltpu.VMEM((2, tokens, depth), BF16)],
    )


def combine(core, keep, near, after):
    _, tokens, width = keep.shape
    tile = tile_of(width, 512)
    both = pl.BlockSpec((2, tokens, tile), lambda i, c: (0, 0, i))
    one = pl.BlockSpec((tokens, tile), lambda i, c: (0, i))

    def body(core_ref, keep_ref, preact_ref, grad_ref, chip_ref):
        chip_ref[0] = (keep_ref[0] + preact_ref[...].astype(F32)).astype(BF16)
        chip_ref[1] = (keep_ref[1] + grad_ref[...].astype(F32)).astype(BF16)

    return call(
        body,
        core,
        [keep, *near],
        [both, one, one],
        jax.ShapeDtypeStruct(keep.shape, BF16),
        both,
        (width // tile,),
        (4 * tokens * width, 16 * tokens * width),
        "combine",
        after,
    )


def activations(core, keep, near, far, start, after=()):
    _, tokens, width = far.shape
    tile = tile_of(width, 256)
    first = start // tile
    both = pl.BlockSpec((2, tokens, tile), lambda i, c: (0, 0, first + i))
    both_here = pl.BlockSpec((2, tokens, tile), lambda i, c: (0, 0, i))
    one = pl.BlockSpec((tokens, tile), lambda i, c: (0, first + i))

    def body(core_ref, keep_ref, *refs):
        *near_refs, far_ref, act_ref = refs

        def total(which):
            part = near_refs[which][...] if len(near) > 1 else near_refs[0][which]
            return keep_ref[which] + part.astype(F32) + far_ref[which].astype(F32)

        preact = total(0)
        cdf = 0.5 + 0.5 * lax.erf(preact * (0.5**0.5))
        pdf = jnp.exp(-0.5 * preact * preact) * ((0.5 / math.pi) ** 0.5)
        act_ref[0] = (preact * cdf).astype(BF16)
        act_ref[1] = (total(1) * (cdf + preact * pdf)).astype(BF16)

    return call(
        body,
        core,
        [keep, *near, far],
        [both] + [one if len(near) > 1 else both] * len(near) + [both_here],
        jax.ShapeDtypeStruct(far.shape, BF16),
        both_here,
        (width // tile,),
        (60 * tokens * width, 20 * tokens * width),
        "activations",
        after,
    )


def back(core, acts, ups, start, before, order, leave, after=()):
    width = acts[0][0].shape[2]
    tokens = sum(keep.shape[1] for keep, _ in acts)
    depth = ups[0].shape[0]
    tile = tile_of(depth, 512)
    groups = len(acts)

    def body(core_ref, *refs):
        part = None
        for side in range(2):
            mine = [ref[0] for ref in refs[side * groups : (side + 1) * groups]]
            mine = mine[0] if groups == 1 else jnp.concatenate(mine, axis=0)
            term = contract(mine, refs[2 * groups + side][...], 1, 1)
            part = term if part is None else part + term
        refs = refs[2 * groups + 2 :]
        if before is not None:
            part = part + refs[0][...]
        outs = refs[(before is not None) :]
        if leave is None:
            outs[0][...] = part
        else:
            rows = tokens // len(order)
            part = [part[n * rows : (n + 1) * rows] for n in order]
            outs[0][...] = jnp.concatenate(part[:leave], axis=0) if leave > 1 else part[0]
            outs[1][...] = jnp.concatenate(part[leave:], axis=0).astype(BF16)

    kinds = [(tokens, F32)]
    if leave is not None:
        rows = tokens // len(order)
        kinds = [(leave * rows, F32), (tokens - leave * rows, BF16)]
    operands = [which[side] for side in range(2) for which in acts]
    return call(
        body,
        core,
        [*operands, *ups] + ([] if before is None else [before]),
        [pl.BlockSpec((1, array.shape[1], width), lambda i, c: (1, 0, 0)) for array in operands]
        + [pl.BlockSpec((tile, width), lambda i, c: (i, start // width))] * 2
        + ([] if before is None else [pl.BlockSpec((tokens, tile), lambda i, c: (0, i))]),
        [jax.ShapeDtypeStruct((rows, depth), dtype) for rows, dtype in kinds],
        [pl.BlockSpec((rows, tile), lambda i, c: (0, i)) for rows, _ in kinds],
        (depth // tile,),
        (4 * tokens * depth * width, 4 * depth * width + 4 * tokens * depth),
        "back",
        after,
    )


def fold(core, stay, near, dtype, after=()):
    rows, depth = stay.shape

    def body(core_ref, stay_ref, near_ref, out_ref):
        out_ref[...] = (stay_ref[...] + near_ref[...].astype(F32)).astype(dtype)

    return call(
        body,
        core,
        [stay, near],
        [whole(stay.shape)] * 2,
        jax.ShapeDtypeStruct(stay.shape, dtype),
        whole(stay.shape),
        (1,),
        (rows * depth, 8 * rows * depth),
        "fold",
        after,
    )


def arrange(core, units, after=()):
    _, rows, depth = units[0].shape
    tokens = rows * len(units)

    def body(core_ref, *refs):
        *unit_refs, inputs_t, cotan = refs
        inputs_t[...] = jnp.concatenate([ref[0] for ref in unit_refs], axis=0).T
        cotan[...] = jnp.concatenate([ref[1] for ref in unit_refs], axis=0)

    return call(
        body,
        core,
        units,
        [whole(units[0].shape)] * len(units),
        [jax.ShapeDtypeStruct((depth, tokens), BF16), jax.ShapeDtypeStruct((tokens, depth), BF16)],
        [whole((depth, tokens)), whole((tokens, depth))],
        (1,),
        (0, 8 * tokens * depth),
        "arrange",
        after,
    )


def weight_grads(core, inputs_t, cotan, sides, acts, start, width, shape, outputs, after=()):
    depth, full = shape
    tokens = cotan.shape[0]
    half = full // 2
    tile = tile_of(width, 256)
    steps = width // tile
    groups = len(acts[0])

    def body(core_ref, inputs_ref, cotan_ref, *refs):
        up_out, down_out, done = refs[-3:]
        done[...] = jnp.zeros_like(done)
        for order in range(len(sides)):
            mine = refs[order * groups : (order + 1) * groups]

            @pl.when(pl.program_id(0) // steps == order)
            def _(mine=mine):
                hidden = jnp.concatenate([ref[0] for ref in mine], axis=0)
                grad = jnp.concatenate([ref[1] for ref in mine], axis=0)
                up_out[...] = contract(inputs_ref[...], grad, 1, 0)
                down_out[...] = contract(hidden, cotan_ref[...], 0, 0)

    def place(i, c):
        which = side_of(c, sides[0])
        if len(sides) > 1:
            which = jnp.where(i // steps == 0, which, 1 - which)
        return which * (half // tile) + start // tile + i % steps

    operands = [inputs_t, cotan]
    specs = [whole(inputs_t.shape), whole(cotan.shape)]
    for order in range(len(sides)):
        for array, offset in acts[order]:

            def index(i, c, order=order, first=offset // tile):
                return (0, 0, first + jnp.clip(i - order * steps, 0, steps - 1))

            operands.append(array)
            specs.append(pl.BlockSpec((2, array.shape[1], tile), index))
    aliases = None
    if outputs is not None:
        aliases = {len(operands) + 1: 0, len(operands) + 2: 1}
        operands += list(outputs)
        specs += [pl.BlockSpec(memory_space=pl.ANY)] * 2
    many = width * len(sides)
    return call(
        body,
        core,
        operands,
        specs,
        [
            jax.ShapeDtypeStruct((depth, full), F32),
            jax.ShapeDtypeStruct((full, depth), F32),
            jax.ShapeDtypeStruct((8, 128), F32),
        ],
        [
            pl.BlockSpec((depth, tile), lambda i, c: (0, place(i, c))),
            pl.BlockSpec((tile, depth), lambda i, c: (place(i, c), 0)),
            whole((8, 128)),
        ],
        (steps * len(sides),),
        (4 * tokens * depth * many, 8 * depth * many),
        "weight_grads",
        after,
        aliases=aliases,
    )


def swap(value, axis, size, bits):
    return lax.ppermute(value, axis, [(i, i ^ bits) for i in range(size)])


def cube_body(inputs, cotangent, up, down):
    rows = inputs.shape[0]
    half = up.shape[1] // 2
    width = half // 3 if half % 384 == 0 else half
    chunks = half // width
    core = (lax.axis_index("gy") % 2).astype(jnp.int32).reshape(1)

    unit = {(0, 0): jnp.stack([inputs, cotangent])}
    unit[0, 1] = swap(unit[0, 0], "gx", 2, 1)
    unit[1, 0] = swap(unit[0, 0], "gz", 4, 1)
    z = lax.axis_index("gz")
    middle = (z == 1) | (z == 2)
    across, outward = [(1, 2), (2, 1)], [(1, 0), (2, 3)]
    first = lax.ppermute(unit[0, 0], "gz", across)
    second = lax.ppermute(unit[1, 0], "gz", across)
    first_on = lax.ppermute(first, "gz", outward)
    second_on = lax.ppermute(second, "gz", outward)
    unit[2, 0] = jnp.where(middle, second, first_on)
    unit[3, 0] = jnp.where(middle, first, second_on)
    for d in (1, 2, 3):
        unit[d, 1] = swap(unit[d, 0], "gx", 2, 1)
    groups = [
        [unit[0, 0], unit[0, 1]],
        [unit[1, 0], unit[1, 1]],
        [unit[2, 0], unit[3, 0], unit[2, 1], unit[3, 1]],
    ]

    pieces = [(0, 0, half), (1, 0, half)] + [(2, j * width, width) for j in range(chunks)]
    near, keep, far, act, act_near = {}, {}, {}, {}, {}
    *weights, = bring(core, up, down)
    ups, downs = weights[0::2], weights[1::2]

    def sums(group, side, after):
        return partial_sums(core, groups[group], ups[side], downs[side], side, side == 1, after)

    def product(group, after, between=()):
        out = sums(group, 1, after)
        near[group] = [swap(array, "gy", 4, 1) for array in out]
        keep[group], = sums(group, 0, [out[0], *between])
        return [keep[group]]

    def cross(n, after=()):
        group, start, size = pieces[n]
        span = slice(start, start + size)
        if after:
            chip = combine(core, keep[group], near[group], after)
        else:
            chip = jnp.stack([
                (keep[group][which, :, span] + near[group][which][:, span].astype(F32)).astype(BF16)
                for which in range(2)
            ])
        far[n] = swap(chip, "gy", 4, 2)
        return [chip]

    def ready(n, after):
        group, start, _ = pieces[n]
        act[n] = activations(core, keep[group], near[group], far[n], start, after)
        act_near[n] = swap(act[n], "gy", 4, 1)
        return [act[n]]

    def inward(many, start, part, order, leave, after):
        which = [(act[n], act_near[n]) for n in many]
        return back(core, which, (ups[0], ups[1]), start, part, order, leave, after)

    outputs = None

    def gradients(j, sides, after):
        acts = [
            [(array[n], j * width) for n in range(2)] + [(array[2 + j], 0)]
            for array in (act, act_near)
        ]
        acts = [acts[side] for side in sides]
        return weight_grads(
            core, inputs_t, cotan, sides, acts, j * width, width, up.shape, outputs, after
        )

    last = product(0, (), ())
    last = cross(0, [unit[1, 1], first_on, second])
    last = product(1, last, [second_on])
    last = ready(0, [*last, unit[2, 1]])
    last = cross(1, last)
    last = product(2, last)
    last = ready(1, last)
    for j in range(chunks):
        last = cross(2 + j) + last
    inputs_t, cotan = arrange(core, [u for group in groups for u in group], last)
    stay1, go1 = inward((0, 1), 0, None, (0, 2, 1, 3), 2, [inputs_t])
    near1 = swap(go1, "gx", 2, 1)

    part, last = None, [stay1]
    for j in range(chunks):
        n, final = 2 + j, j + 1 == chunks
        last = ready(n, last)
        if j:
            last = part, = inward((n - 1,), (j - 1) * width, part, None, None, last)
        if final:
            stay2, go2 = inward((n,), j * width, part, (0, 1, 2, 3), 2, last)
            near2 = swap(go2, "gx", 2, 1)
            last = [stay2]
        if j:
            *outputs, done = gradients(j - 1, (1,), last)
            last = [done]
        if final:
            back2 = fold(core, stay2, near2, BF16, last)
            far2 = swap(back2[:rows], "gz", 4, 2)
            far3 = swap(back2[rows:], "gz", 4, 3)
            last = [back2]
        *outputs, done = gradients(j, (0,), last)
        last = [done]
        if j == 0:
            total = fold(core, stay1[:rows], near1[:rows], F32, last)
            back1 = fold(core, stay1[rows:], near1[rows:], BF16, [total])
            far1 = swap(back1, "gz", 4, 1)
            last = [back1]
        elif j == 1 and not final:
            total = fold(core, total, far1, F32, last)
            last = [total]
    if chunks < 3:
        total = total + far1.astype(F32)
    *outputs, done = gradients(chunks - 1, (1,), last)
    total = total + far2.astype(F32) + far3.astype(F32)
    return (total.astype(BF16), *outputs)


def solution(mesh):
    placed = (
        P(("gx", "gz"), "gy"),
        P(("gx", "gz"), "gy"),
        P("gy", ("gz", "gx")),
        P(("gz", "gx"), "gy"),
    )
    cube = tuple(mesh.shape[axis] for axis in ("gx", "gy", "gz")) == (2, 4, 4)
    return jax.shard_map(
        cube_body if cube else general_body,
        mesh=mesh,
        in_specs=placed,
        out_specs=(P(("gx", "gz"), "gy"), P("gy", ("gz", "gx")), P(("gz", "gx"), "gy")),
        check_vma=False,
    )
```

```python
import math

import jax
import jax.numpy as jnp
from jax import lax
from jax.experimental import pallas as pl
from jax.experimental.pallas import tpu as pltpu
from jax.sharding import PartitionSpec as P

F32 = jnp.float32
BF16 = jnp.bfloat16
VMEM_LIMIT = 24 * 1024 * 1024
COST_PART = 1


def gelu_exact(value):
    return jax.nn.gelu(value, approximate=False)


def activate(preact, grad_hidden):
    activated, pullback = jax.vjp(gelu_exact, preact)
    grad_preact = pullback(grad_hidden)[0]
    return (activated.astype(BF16), grad_preact.astype(BF16))


def contract(left, right, left_dim, right_dim):
    return lax.dot_general(
        left, right, (((left_dim,), (right_dim,)), ((), ())), preferred_element_type=F32
    )


def general_body(inputs, cotangent, up_weight, down_weight):
    all_inputs = lax.all_gather(inputs, ("gx", "gz"), axis=0, tiled=True)
    all_cotan = lax.all_gather(cotangent, ("gx", "gz"), axis=0, tiled=True)
    preact = lax.psum_scatter(
        contract(all_inputs, up_weight, 1, 0), "gy", scatter_dimension=0, tiled=True
    )
    grad_hidden = lax.psum_scatter(
        contract(all_cotan, down_weight, 1, 1), "gy", scatter_dimension=0, tiled=True
    )
    hidden, grad_preact = activate(preact, grad_hidden)
    hidden = lax.all_gather(hidden, "gy", axis=0, tiled=True)
    grad_preact = lax.all_gather(grad_preact, "gy", axis=0, tiled=True)
    grad_down = contract(hidden, all_cotan, 0, 0)
    grad_up = contract(all_inputs, grad_preact, 0, 0)
    grad_inputs = lax.psum_scatter(
        contract(grad_preact, up_weight, 1, 1), ("gx", "gz"), scatter_dimension=0, tiled=True
    ).astype(BF16)
    return (grad_inputs, grad_up, grad_down)


def tile_of(width, most):
    tile = most
    while width % tile:
        tile //= 2
    return tile


def call(body, core, operands, in_specs, outs, out_specs, grid, cost, name, after=(), scratch=(), aliases=None):
    after = list(after)
    inner = len(operands) + 1

    def kernel(*refs):
        body(*refs[:inner], *refs[inner + len(after) :])

    flops, moved = cost
    return pl.pallas_call(
        kernel,
        grid_spec=pltpu.PrefetchScalarGridSpec(
            num_scalar_prefetch=1,
            grid=grid,
            in_specs=list(in_specs) + [pl.BlockSpec(memory_space=pl.ANY)] * len(after),
            out_specs=out_specs,
            scratch_shapes=list(scratch),
        ),
        out_shape=outs,
        input_output_aliases=aliases or {},
        compiler_params=pltpu.CompilerParams(vmem_limit_bytes=VMEM_LIMIT),
        cost_estimate=pl.CostEstimate(
            flops=flops // COST_PART, bytes_accessed=moved // COST_PART, transcendentals=0
        ),
        name=name,
    )(core, *operands, *after)


def whole(shape):
    return pl.BlockSpec(shape, lambda i, c: (0,) * len(shape))


def side_of(core_ref, side):
    return core_ref[0] if side == 0 else 1 - core_ref[0]


def bring(core, up, down):
    depth, full = up.shape
    half = full // 2
    parts = 2

    def body(core_ref, up_ref, down_ref, *refs):
        *outs, sems = refs
        copies = []
        for side in range(2):
            begin = pl.multiple_of(side_of(core_ref, side) * half, half)
            up_out, down_out = outs[2 * side : 2 * side + 2]
            for part in range(parts):
                rows = pl.ds(part * (depth // parts), depth // parts)
                copies.append((up_ref.at[rows, pl.ds(begin, half)], up_out.at[rows]))
                size = half // parts
                rows = pl.ds(pl.multiple_of(begin + part * size, size), size)
                copies.append((down_ref.at[rows], down_out.at[pl.ds(part * size, size)]))
        copies = [
            pltpu.make_async_copy(source, target, sems.at[n])
            for n, (source, target) in enumerate(copies)
        ]
        for copy in copies:
            copy.start()
        for copy in copies:
            copy.wait()

    up, down = (pltpu.with_memory_space_constraint(array, pltpu.HBM) for array in (up, down))
    shapes = [(depth, half), (half, depth)] * 2
    return call(
        body,
        core,
        [up, down],
        [pl.BlockSpec(memory_space=pltpu.HBM)] * 2,
        [pltpu.VMEM(shape, BF16) for shape in shapes],
        [pl.BlockSpec(memory_space=pltpu.VMEM)] * 4,
        (1,),
        (0, 4 * depth * full),
        "bring",
        (),
        [pltpu.SemaphoreType.DMA((4 * parts,))],
    )


def partial_sums(core, units, up, down, side, apart, start, width, after=()):
    _, rows, depth = units[0].shape
    tokens = rows * len(units)
    tile = tile_of(width, 256)
    first = start // tile
    dtype = BF16 if side else F32

    def body(core_ref, *refs):
        *unit_refs, up_ref, down_ref = refs[: len(units) + 2]
        *out_refs, acts = refs[len(units) + 2 :]

        @pl.when(pl.program_id(0) == 0)
        def _():
            for n, ref in enumerate(unit_refs):
                acts[:, n * rows : (n + 1) * rows, :] = ref[...]

        preact = contract(acts[0], up_ref[...], 1, 0)
        grad_hidden = contract(acts[1], down_ref[...], 1, 1)
        if apart:
            out_refs[0][...] = preact.astype(dtype)
            out_refs[1][...] = grad_hidden.astype(dtype)
        else:
            out_refs[0][0] = preact.astype(dtype)
            out_refs[0][1] = grad_hidden.astype(dtype)

    if apart:
        outs = [jax.ShapeDtypeStruct((tokens, width), dtype)] * 2
        specs = [pl.BlockSpec((tokens, tile), lambda i, c: (0, i))] * 2
    else:
        outs = [jax.ShapeDtypeStruct((2, tokens, width), dtype)]
        specs = [pl.BlockSpec((2, tokens, tile), lambda i, c: (0, 0, i))]
    return call(
        body,
        core,
        [*units, up, down],
        [whole(units[0].shape)] * len(units)
        + [
            pl.BlockSpec((depth, tile), lambda i, c: (0, first + i)),
            pl.BlockSpec((tile, depth), lambda i, c: (first + i, 0)),
        ],
        outs,
        specs,
        (width // tile,),
        (4 * tokens * depth * width, 4 * depth * width),
        "sums_send" if side else "sums_keep",
        after,
        [pltpu.VMEM((2, tokens, depth), BF16)],
    )


def combine(core, keep, near, start, after):
    _, tokens, width = keep.shape
    tile = tile_of(width, 256)
    both = pl.BlockSpec((2, tokens, tile), lambda i, c: (0, 0, i))
    one = pl.BlockSpec((tokens, tile), lambda i, c: (0, start // tile + i))

    def body(core_ref, keep_ref, preact_ref, grad_ref, chip_ref):
        chip_ref[0] = (keep_ref[0] + preact_ref[...].astype(F32)).astype(BF16)
        chip_ref[1] = (keep_ref[1] + grad_ref[...].astype(F32)).astype(BF16)

    return call(
        body,
        core,
        [keep, *near],
        [both, one, one],
        jax.ShapeDtypeStruct(keep.shape, BF16),
        both,
        (width // tile,),
        (4 * tokens * width, 16 * tokens * width),
        "combine",
        after,
    )


def activations(core, keep, near, far, row, start, near_start, after=()):
    _, tokens, width = far.shape
    tile = tile_of(width, 256)
    first, near_first, block = start // tile, near_start // tile, row // tokens
    both = pl.BlockSpec((2, tokens, tile), lambda i, c: (0, block, first + i))
    both_here = pl.BlockSpec((2, tokens, tile), lambda i, c: (0, 0, i))
    one = pl.BlockSpec((tokens, tile), lambda i, c: (block, near_first + i))

    def body(core_ref, keep_ref, *refs):
        *near_refs, far_ref, act_ref = refs

        def total(which):
            part = near_refs[which][...].astype(F32)
            return keep_ref[which] + part + far_ref[which].astype(F32)

        preact = total(0)
        cdf = 0.5 + 0.5 * lax.erf(preact * (0.5**0.5))
        pdf = jnp.exp(-0.5 * preact * preact) * ((0.5 / math.pi) ** 0.5)
        act_ref[0] = (preact * cdf).astype(BF16)
        act_ref[1] = (total(1) * (cdf + preact * pdf)).astype(BF16)

    return call(
        body,
        core,
        [keep, *near, far],
        [both, one, one, both_here],
        jax.ShapeDtypeStruct(far.shape, BF16),
        both_here,
        (width // tile,),
        (60 * tokens * width, 20 * tokens * width),
        "activations",
        after,
    )


def back(core, acts, ups, start, width, before, order, leave, after=()):
    tokens = sum(which[0].shape[1] for which in acts)
    depth = ups[0].shape[0]
    tile = tile_of(depth, 512)
    groups = len(acts)

    def body(core_ref, *refs):
        part = None
        for side in range(2):
            mine = [ref[0] for ref in refs[side * groups : (side + 1) * groups]]
            mine = mine[0] if groups == 1 else jnp.concatenate(mine, axis=0)
            term = contract(mine, refs[2 * groups + side][...], 1, 1)
            part = term if part is None else part + term
        refs = refs[2 * groups + 2 :]
        if before is not None:
            part = part + refs[0][...]
        outs = refs[(before is not None) :]
        if leave is None:
            outs[0][...] = part
        else:
            rows = tokens // len(order)
            part = [part[n * rows : (n + 1) * rows] for n in order]
            outs[0][...] = jnp.concatenate(part[:leave], axis=0) if leave > 1 else part[0]
            outs[1][...] = jnp.concatenate(part[leave:], axis=0).astype(BF16)

    kinds = [(tokens, F32)]
    if leave is not None:
        rows = tokens // len(order)
        kinds = [(leave * rows, F32), (tokens - leave * rows, BF16)]
    operands = [which[side] for side in range(2) for which in acts]
    firsts = [which[2] // width for side in range(2) for which in acts]
    return call(
        body,
        core,
        [*operands, *ups] + ([] if before is None else [before]),
        [
            pl.BlockSpec((1, array.shape[1], width), lambda i, c, first=first: (1, 0, first))
            for array, first in zip(operands, firsts)
        ]
        + [pl.BlockSpec((tile, width), lambda i, c: (i, start // width))] * 2
        + ([] if before is None else [pl.BlockSpec((tokens, tile), lambda i, c: (0, i))]),
        [jax.ShapeDtypeStruct((rows, depth), dtype) for rows, dtype in kinds],
        [pl.BlockSpec((rows, tile), lambda i, c: (0, i)) for rows, _ in kinds],
        (depth // tile,),
        (4 * tokens * depth * width, 4 * depth * width + 4 * tokens * depth),
        "back",
        after,
    )


def fold(core, stay, near, dtype, after=()):
    rows, depth = stay.shape

    def body(core_ref, stay_ref, near_ref, out_ref):
        out_ref[...] = (stay_ref[...] + near_ref[...].astype(F32)).astype(dtype)

    return call(
        body,
        core,
        [stay, near],
        [whole(stay.shape)] * 2,
        jax.ShapeDtypeStruct(stay.shape, dtype),
        whole(stay.shape),
        (1,),
        (rows * depth, 8 * rows * depth),
        "fold",
        after,
    )


def arrange(core, units, after=()):
    _, rows, depth = units[0].shape
    tokens = rows * len(units)

    def body(core_ref, *refs):
        *unit_refs, inputs_t, cotan = refs
        inputs_t[...] = jnp.concatenate([ref[0] for ref in unit_refs], axis=0).T
        cotan[...] = jnp.concatenate([ref[1] for ref in unit_refs], axis=0)

    return call(
        body,
        core,
        units,
        [whole(units[0].shape)] * len(units),
        [jax.ShapeDtypeStruct((depth, tokens), BF16), jax.ShapeDtypeStruct((tokens, depth), BF16)],
        [whole((depth, tokens)), whole((tokens, depth))],
        (1,),
        (0, 8 * tokens * depth),
        "arrange",
        after,
    )


def weight_grads(core, inputs_t, cotan, sides, acts, start, width, shape, outputs, after=()):
    depth, full = shape
    tokens = cotan.shape[0]
    half = full // 2
    tile = tile_of(width, 256)
    steps = width // tile
    groups = len(acts[0])

    def body(core_ref, inputs_ref, cotan_ref, *refs):
        up_out, down_out, done = refs[-3:]
        done[...] = jnp.zeros_like(done)
        for order in range(len(sides)):
            mine = refs[order * groups : (order + 1) * groups]

            @pl.when(pl.program_id(0) // steps == order)
            def _(mine=mine):
                hidden = jnp.concatenate([ref[0] for ref in mine], axis=0)
                grad = jnp.concatenate([ref[1] for ref in mine], axis=0)
                up_out[...] = contract(inputs_ref[...], grad, 1, 0)
                down_out[...] = contract(hidden, cotan_ref[...], 0, 0)

    def place(i, c):
        which = side_of(c, sides[0])
        if len(sides) > 1:
            which = jnp.where(i // steps == 0, which, 1 - which)
        return which * (half // tile) + start // tile + i % steps

    operands = [inputs_t, cotan]
    specs = [whole(inputs_t.shape), whole(cotan.shape)]
    for order in range(len(sides)):
        for array, offset in acts[order]:

            def index(i, c, order=order, first=offset // tile):
                return (0, 0, first + jnp.clip(i - order * steps, 0, steps - 1))

            operands.append(array)
            specs.append(pl.BlockSpec((2, array.shape[1], tile), index))
    aliases = None
    if outputs is not None:
        aliases = {len(operands) + 1: 0, len(operands) + 2: 1}
        operands += list(outputs)
        specs += [pl.BlockSpec(memory_space=pl.ANY)] * 2
    many = width * len(sides)
    return call(
        body,
        core,
        operands,
        specs,
        [
            jax.ShapeDtypeStruct((depth, full), F32),
            jax.ShapeDtypeStruct((full, depth), F32),
            jax.ShapeDtypeStruct((8, 128), F32),
        ],
        [
            pl.BlockSpec((depth, tile), lambda i, c: (0, place(i, c))),
            pl.BlockSpec((tile, depth), lambda i, c: (place(i, c), 0)),
            whole((8, 128)),
        ],
        (steps * len(sides),),
        (4 * tokens * depth * many, 8 * depth * many),
        "weight_grads",
        after,
        aliases=aliases,
    )


def swap(value, axis, size, bits):
    return lax.ppermute(value, axis, [(i, i ^ bits) for i in range(size)])


def cube_body(inputs, cotangent, up, down):
    rows = inputs.shape[0]
    half = up.shape[1] // 2
    width = half // 2
    core = (lax.axis_index("gy") % 2).astype(jnp.int32).reshape(1)

    unit = {(0, 0): jnp.stack([inputs, cotangent])}
    unit[0, 1] = swap(unit[0, 0], "gx", 2, 1)
    unit[1, 0] = swap(unit[0, 0], "gz", 4, 1)
    z = lax.axis_index("gz")
    middle = (z == 1) | (z == 2)
    across, outward = [(1, 2), (2, 1)], [(1, 0), (2, 3)]
    first = lax.ppermute(unit[0, 0], "gz", across)
    second = lax.ppermute(unit[1, 0], "gz", across)
    first_on = lax.ppermute(first, "gz", outward)
    second_on = lax.ppermute(second, "gz", outward)
    unit[2, 0] = jnp.where(middle, second, first_on)
    unit[3, 0] = jnp.where(middle, first, second_on)
    for d in (1, 2, 3):
        unit[d, 1] = swap(unit[d, 0], "gx", 2, 1)
    groups = [
        [unit[0, 0], unit[0, 1]],
        [unit[1, 0], unit[1, 1]],
        [unit[2, 0], unit[2, 1], unit[3, 0], unit[3, 1]],
    ]

    pair = 2 * rows
    pieces = [
        (0, 0, 0, width),
        (0, 0, width, width),
        (1, 0, 0, half),
        (2, 0, 0, half),
        (2, pair, 0, width),
        (2, pair, width, width),
    ]
    near, keep, far, act, act_near = {}, {}, {}, {}, {}
    *weights, = bring(core, up, down)
    ups, downs = weights[0::2], weights[1::2]

    def send(group, after=()):
        out = partial_sums(
            core, groups[group], ups[1], downs[1], 1, True, 0, half, after
        )
        near[group] = [swap(array, "gy", 4, 1) for array in out]
        return [out[0]]

    def hold(group, start, size, after):
        out, = partial_sums(
            core, groups[group], ups[0], downs[0], 0, False, start, size, after
        )
        keep[group, start] = out
        return [out]

    def kept(group, start):
        return (keep[group, start], 0) if (group, start) in keep else (keep[group, 0], start)

    def cross(n, after=()):
        group, row, start, size = pieces[n]
        array, column = kept(group, start)
        if after:
            chip = combine(core, array, near[group], start, after)
        else:
            chip = jnp.stack([
                (
                    array[which, row : row + pair, column : column + size]
                    + near[group][which][row : row + pair, start : start + size].astype(F32)
                ).astype(BF16)
                for which in range(2)
            ])
        far[n] = swap(chip, "gy", 4, 2)
        return [chip]

    def ready(n, after):
        group, row, start, _ = pieces[n]
        array, column = kept(group, start)
        act[n] = activations(core, array, near[group], far[n], row, column, start, after)
        act_near[n] = swap(act[n], "gy", 4, 1)
        return [act[n]]

    def inward(which, start, size, part, order, leave, after):
        acts = [(act[n], act_near[n], offset) for n, offset in which]
        return back(core, acts, ups, start, size, part, order, leave, after)

    outputs = None

    def gradients(j, sides, after):
        acts = [
            [(array[j], 0), (array[2], j * width), (array[3], j * width), (array[4 + j], 0)]
            for array in (act, act_near)
        ]
        acts = [acts[side] for side in sides]
        return weight_grads(
            core, inputs_t, cotan, sides, acts, j * width, width, up.shape, outputs, after
        )

    def finish(j, sides, after):
        nonlocal outputs
        *outputs, done = gradients(j, sides, after)
        return [done]

    last = send(0)
    last = hold(0, 0, width, last)
    last = cross(0) + last
    last = hold(0, width, width, last + [])
    last = cross(1, last + [])
    last = send(1, last + [unit[1, 1], second, first_on])
    last = hold(1, 0, half, [*last, second_on])
    last = ready(0, last)
    last = ready(1, [*last, unit[2, 1]])
    last = cross(2, last)
    last = send(2, last)
    last = hold(2, 0, half, last)
    last = ready(2, last)
    last = cross(3) + cross(4) + cross(5) + last
    inputs_t, cotan = arrange(core, [u for group in groups for u in group], last)
    part, = inward(((0, 0), (2, 0)), 0, width, None, None, None, [inputs_t])
    stay1, go1 = inward(((1, 0), (2, width)), width, width, part, (0, 2, 1, 3), 2, [part])
    near1 = swap(go1, "gx", 2, 1)

    last = ready(3, [stay1])
    total = fold(core, stay1[:rows], near1[:rows], F32, last)
    back1 = fold(core, stay1[rows:], near1[rows:], BF16, [total])
    far1 = swap(back1, "gz", 4, 1)
    stay2, go2 = inward(((3, 0),), 0, half, None, (0, 1), 1, [back1])
    near2 = swap(go2, "gx", 2, 1)

    last = ready(4, [stay2])
    last = finish(0, (0,), last)
    back2 = fold(core, stay2, near2, BF16, last)
    far2 = swap(back2, "gz", 4, 2)
    total = fold(core, total, far1, F32, [back2])
    last = ready(5, [total])
    part, = inward(((4, 0),), 0, width, None, None, None, last)
    stay3, go3 = inward(((5, 0),), width, width, part, (0, 1), 1, [part])
    near3 = swap(go3, "gx", 2, 1)
    last = finish(0, (1,), [stay3])
    back3 = fold(core, stay3, near3, BF16, last)
    far3 = swap(back3, "gz", 4, 3)
    finish(1, (0, 1), [back3])
    total = total + far2.astype(F32) + far3.astype(F32)
    return (total.astype(BF16), *outputs)


def solution(mesh):
    placed = (
        P(("gx", "gz"), "gy"),
        P(("gx", "gz"), "gy"),
        P("gy", ("gz", "gx")),
        P(("gz", "gx"), "gy"),
    )
    cube = tuple(mesh.shape[axis] for axis in ("gx", "gy", "gz")) == (2, 4, 4)
    return jax.shard_map(
        cube_body if cube else general_body,
        mesh=mesh,
        in_specs=placed,
        out_specs=(P(("gx", "gz"), "gy"), P("gy", ("gz", "gx")), P(("gz", "gx"), "gy")),
        check_vma=False,
    )
```

```python
import math

import jax
import jax.numpy as jnp
from jax import lax
from jax.experimental import pallas as pl
from jax.experimental.pallas import tpu as pltpu
from jax.sharding import PartitionSpec as P

F32 = jnp.float32
BF16 = jnp.bfloat16
VMEM_LIMIT = 10 * 1024 * 1024
GRADS_VMEM_LIMIT = 18 * 1024 * 1024
COST_PART = 1


def gelu_exact(value):
    return jax.nn.gelu(value, approximate=False)


def activate(preact, grad_hidden):
    activated, pullback = jax.vjp(gelu_exact, preact)
    grad_preact = pullback(grad_hidden)[0]
    return (activated.astype(BF16), grad_preact.astype(BF16))


def contract(left, right, left_dim, right_dim):
    return lax.dot_general(
        left, right, (((left_dim,), (right_dim,)), ((), ())), preferred_element_type=F32
    )


def general_body(inputs, cotangent, up_weight, down_weight):
    all_inputs = lax.all_gather(inputs, ("gx", "gz"), axis=0, tiled=True)
    all_cotan = lax.all_gather(cotangent, ("gx", "gz"), axis=0, tiled=True)
    preact = lax.psum_scatter(
        contract(all_inputs, up_weight, 1, 0), "gy", scatter_dimension=0, tiled=True
    )
    grad_hidden = lax.psum_scatter(
        contract(all_cotan, down_weight, 1, 1), "gy", scatter_dimension=0, tiled=True
    )
    hidden, grad_preact = activate(preact, grad_hidden)
    hidden = lax.all_gather(hidden, "gy", axis=0, tiled=True)
    grad_preact = lax.all_gather(grad_preact, "gy", axis=0, tiled=True)
    grad_down = contract(hidden, all_cotan, 0, 0)
    grad_up = contract(all_inputs, grad_preact, 0, 0)
    grad_inputs = lax.psum_scatter(
        contract(grad_preact, up_weight, 1, 1), ("gx", "gz"), scatter_dimension=0, tiled=True
    ).astype(BF16)
    return (grad_inputs, grad_up, grad_down)


def tile_of(width, most):
    tile = most
    while width % tile:
        tile //= 2
    return tile


def call(body, core, operands, in_specs, outs, out_specs, grid, cost, name, after=(), scratch=(), aliases=None, limit=VMEM_LIMIT):
    after = list(after)
    inner = len(operands) + 1

    def kernel(*refs):
        body(*refs[:inner], *refs[inner + len(after) :])

    flops, moved = cost
    return pl.pallas_call(
        kernel,
        grid_spec=pltpu.PrefetchScalarGridSpec(
            num_scalar_prefetch=1,
            grid=grid,
            in_specs=list(in_specs) + [pl.BlockSpec(memory_space=pl.ANY)] * len(after),
            out_specs=out_specs,
            scratch_shapes=list(scratch),
        ),
        out_shape=outs,
        input_output_aliases=aliases or {},
        compiler_params=pltpu.CompilerParams(vmem_limit_bytes=limit),
        cost_estimate=pl.CostEstimate(
            flops=flops // COST_PART, bytes_accessed=moved // COST_PART, transcendentals=0
        ),
        name=name,
    )(core, *operands, *after)


def whole(shape):
    return pl.BlockSpec(shape, lambda i, c: (0,) * len(shape))


def side_of(core_ref, side):
    return core_ref[0] if side == 0 else 1 - core_ref[0]


def bring(core, up, down):
    depth, full = up.shape
    half = full // 2
    parts = 2

    def body(core_ref, up_ref, down_ref, *refs):
        *outs, sems = refs
        copies = []
        for side in range(2):
            begin = pl.multiple_of(side_of(core_ref, side) * half, half)
            up_out, down_out = outs[2 * side : 2 * side + 2]
            for part in range(parts):
                rows = pl.ds(part * (depth // parts), depth // parts)
                copies.append((up_ref.at[rows, pl.ds(begin, half)], up_out.at[rows]))
                size = half // parts
                rows = pl.ds(pl.multiple_of(begin + part * size, size), size)
                copies.append((down_ref.at[rows], down_out.at[pl.ds(part * size, size)]))
        copies = [
            pltpu.make_async_copy(source, target, sems.at[n])
            for n, (source, target) in enumerate(copies)
        ]
        for copy in copies:
            copy.start()
        for copy in copies:
            copy.wait()

    up, down = (pltpu.with_memory_space_constraint(array, pltpu.HBM) for array in (up, down))
    shapes = [(depth, half), (half, depth)] * 2
    return call(
        body,
        core,
        [up, down],
        [pl.BlockSpec(memory_space=pltpu.HBM)] * 2,
        [pltpu.VMEM(shape, BF16) for shape in shapes],
        [pl.BlockSpec(memory_space=pltpu.VMEM)] * 4,
        (1,),
        (0, 4 * depth * full),
        "bring",
        (),
        [pltpu.SemaphoreType.DMA((4 * parts,))],
    )


def partial_sums(core, units, up, down, side, apart, start, width, after=()):
    _, rows, depth = units[0].shape
    tokens = rows * len(units)
    tile = tile_of(width, 256)
    first = start // tile
    dtype = BF16 if side else F32

    def body(core_ref, *refs):
        *unit_refs, up_ref, down_ref = refs[: len(units) + 2]
        *out_refs, acts = refs[len(units) + 2 :]

        @pl.when(pl.program_id(0) == 0)
        def _():
            for n, ref in enumerate(unit_refs):
                acts[:, n * rows : (n + 1) * rows, :] = ref[...]

        preact = contract(acts[0], up_ref[...], 1, 0)
        grad_hidden = contract(acts[1], down_ref[...], 1, 1)
        if apart:
            out_refs[0][...] = preact.astype(dtype)
            out_refs[1][...] = grad_hidden.astype(dtype)
        else:
            out_refs[0][0] = preact.astype(dtype)
            out_refs[0][1] = grad_hidden.astype(dtype)

    if apart:
        outs = [jax.ShapeDtypeStruct((tokens, width), dtype)] * 2
        specs = [pl.BlockSpec((tokens, tile), lambda i, c: (0, i))] * 2
    else:
        outs = [jax.ShapeDtypeStruct((2, tokens, width), dtype)]
        specs = [pl.BlockSpec((2, tokens, tile), lambda i, c: (0, 0, i))]
    return call(
        body,
        core,
        [*units, up, down],
        [whole(units[0].shape)] * len(units)
        + [
            pl.BlockSpec((depth, tile), lambda i, c: (0, first + i)),
            pl.BlockSpec((tile, depth), lambda i, c: (first + i, 0)),
        ],
        outs,
        specs,
        (width // tile,),
        (4 * tokens * depth * width, 4 * depth * width),
        "sums_send" if side else "sums_keep",
        after,
        [pltpu.VMEM((2, tokens, depth), BF16)],
    )


def combine(core, keep, near, row, tokens, column, start, width, after):
    tile = tile_of(width, 256)
    both = pl.BlockSpec((2, tokens, tile), lambda i, c: (0, row // tokens, column // tile + i))
    one = pl.BlockSpec((tokens, tile), lambda i, c: (row // tokens, start // tile + i))

    def body(core_ref, keep_ref, preact_ref, grad_ref, chip_ref):
        chip_ref[0] = (keep_ref[0] + preact_ref[...].astype(F32)).astype(BF16)
        chip_ref[1] = (keep_ref[1] + grad_ref[...].astype(F32)).astype(BF16)

    return call(
        body,
        core,
        [keep, *near],
        [both, one, one],
        jax.ShapeDtypeStruct((2, tokens, width), BF16),
        pl.BlockSpec((2, tokens, tile), lambda i, c: (0, 0, i)),
        (width // tile,),
        (4 * tokens * width, 16 * tokens * width),
        "combine",
        after,
    )


def activations(core, keep, near, far, row, start, near_start, after=()):
    _, tokens, width = far.shape
    tile = tile_of(width, 256)
    first, near_first, block = start // tile, near_start // tile, row // tokens
    both = pl.BlockSpec((2, tokens, tile), lambda i, c: (0, block, first + i))
    both_here = pl.BlockSpec((2, tokens, tile), lambda i, c: (0, 0, i))
    one = pl.BlockSpec((tokens, tile), lambda i, c: (block, near_first + i))

    def body(core_ref, keep_ref, *refs):
        *near_refs, far_ref, act_ref = refs

        def total(which):
            part = near_refs[which][...].astype(F32)
            return keep_ref[which] + part + far_ref[which].astype(F32)

        preact = total(0)
        cdf = 0.5 + 0.5 * lax.erf(preact * (0.5**0.5))
        pdf = jnp.exp(-0.5 * preact * preact) * ((0.5 / math.pi) ** 0.5)
        act_ref[0] = (preact * cdf).astype(BF16)
        act_ref[1] = (total(1) * (cdf + preact * pdf)).astype(BF16)

    return call(
        body,
        core,
        [keep, *near, far],
        [both, one, one, both_here],
        jax.ShapeDtypeStruct(far.shape, BF16),
        both_here,
        (width // tile,),
        (60 * tokens * width, 20 * tokens * width),
        "activations",
        after,
    )


def back(core, acts, ups, start, width, before, order, leave, after=()):
    tokens = sum(which[0].shape[1] for which in acts)
    depth = ups[0].shape[0]
    tile = tile_of(depth, 512)
    groups = len(acts)

    def body(core_ref, *refs):
        part = None
        for side in range(2):
            mine = [ref[0] for ref in refs[side * groups : (side + 1) * groups]]
            mine = mine[0] if groups == 1 else jnp.concatenate(mine, axis=0)
            term = contract(mine, refs[2 * groups + side][...], 1, 1)
            part = term if part is None else part + term
        refs = refs[2 * groups + 2 :]
        if before is not None:
            part = part + refs[0][...]
        outs = refs[(before is not None) :]
        if leave is None:
            outs[0][...] = part
        else:
            rows = tokens // len(order)
            part = [part[n * rows : (n + 1) * rows] for n in order]
            outs[0][...] = jnp.concatenate(part[:leave], axis=0) if leave > 1 else part[0]
            outs[1][...] = jnp.concatenate(part[leave:], axis=0).astype(BF16)

    kinds = [(tokens, F32)]
    if leave is not None:
        rows = tokens // len(order)
        kinds = [(leave * rows, F32), (tokens - leave * rows, BF16)]
    operands = [which[side] for side in range(2) for which in acts]
    firsts = [which[2] // width for side in range(2) for which in acts]
    return call(
        body,
        core,
        [*operands, *ups] + ([] if before is None else [before]),
        [
            pl.BlockSpec((1, array.shape[1], width), lambda i, c, first=first: (1, 0, first))
            for array, first in zip(operands, firsts)
        ]
        + [pl.BlockSpec((tile, width), lambda i, c: (i, start // width))] * 2
        + ([] if before is None else [pl.BlockSpec((tokens, tile), lambda i, c: (0, i))]),
        [jax.ShapeDtypeStruct((rows, depth), dtype) for rows, dtype in kinds],
        [pl.BlockSpec((rows, tile), lambda i, c: (0, i)) for rows, _ in kinds],
        (depth // tile,),
        (4 * tokens * depth * width, 4 * depth * width + 4 * tokens * depth),
        "back",
        after,
    )


def fold(core, stay, near, dtype, after=()):
    rows, depth = stay.shape

    def body(core_ref, stay_ref, near_ref, out_ref):
        out_ref[...] = (stay_ref[...] + near_ref[...].astype(F32)).astype(dtype)

    return call(
        body,
        core,
        [stay, near],
        [whole(stay.shape)] * 2,
        jax.ShapeDtypeStruct(stay.shape, dtype),
        whole(stay.shape),
        (1,),
        (rows * depth, 8 * rows * depth),
        "fold",
        after,
    )


def arrange(core, units, after=()):
    _, rows, depth = units[0].shape
    tokens = rows * len(units)

    def body(core_ref, *refs):
        *unit_refs, inputs_t, cotan = refs
        inputs_t[...] = jnp.concatenate([ref[0] for ref in unit_refs], axis=0).T
        cotan[...] = jnp.concatenate([ref[1] for ref in unit_refs], axis=0)

    return call(
        body,
        core,
        units,
        [whole(units[0].shape)] * len(units),
        [jax.ShapeDtypeStruct((depth, tokens), BF16), jax.ShapeDtypeStruct((tokens, depth), BF16)],
        [whole((depth, tokens)), whole((tokens, depth))],
        (1,),
        (0, 8 * tokens * depth),
        "arrange",
        after,
    )


def weight_grads(core, inputs_t, cotan, sides, acts, start, width, shape, outputs, after=()):
    depth, full = shape
    tokens = cotan.shape[0]
    half = full // 2
    tile = tile_of(width, 256)
    steps = width // tile
    groups = len(acts[0])

    def body(core_ref, inputs_ref, cotan_ref, *refs):
        up_out, down_out, done = refs[-3:]
        done[...] = jnp.zeros_like(done)
        for order in range(len(sides)):
            mine = refs[order * groups : (order + 1) * groups]

            @pl.when(pl.program_id(0) // steps == order)
            def _(mine=mine):
                hidden = jnp.concatenate([ref[0] for ref in mine], axis=0)
                grad = jnp.concatenate([ref[1] for ref in mine], axis=0)
                up_out[...] = contract(inputs_ref[...], grad, 1, 0)
                down_out[...] = contract(hidden, cotan_ref[...], 0, 0)

    def place(i, c):
        which = side_of(c, sides[0])
        if len(sides) > 1:
            which = jnp.where(i // steps == 0, which, 1 - which)
        return which * (half // tile) + start // tile + i % steps

    operands = [inputs_t, cotan]
    specs = [whole(inputs_t.shape), whole(cotan.shape)]
    for order in range(len(sides)):
        for array, offset in acts[order]:

            def index(i, c, order=order, first=offset // tile):
                return (0, 0, first + jnp.clip(i - order * steps, 0, steps - 1))

            operands.append(array)
            specs.append(pl.BlockSpec((2, array.shape[1], tile), index))
    aliases = None
    if outputs is not None:
        aliases = {len(operands) + 1: 0, len(operands) + 2: 1}
        operands += list(outputs)
        specs += [pl.BlockSpec(memory_space=pl.ANY)] * 2
    many = width * len(sides)
    return call(
        body,
        core,
        operands,
        specs,
        [
            jax.ShapeDtypeStruct((depth, full), F32),
            jax.ShapeDtypeStruct((full, depth), F32),
            jax.ShapeDtypeStruct((8, 128), F32),
        ],
        [
            pl.BlockSpec((depth, tile), lambda i, c: (0, place(i, c))),
            pl.BlockSpec((tile, depth), lambda i, c: (place(i, c), 0)),
            whole((8, 128)),
        ],
        (steps * len(sides),),
        (4 * tokens * depth * many, 8 * depth * many),
        "weight_grads",
        after,
        aliases=aliases,
        limit=GRADS_VMEM_LIMIT,
    )


def swap(value, axis, size, bits):
    return lax.ppermute(value, axis, [(i, i ^ bits) for i in range(size)])


def cube_body(inputs, cotangent, up, down):
    rows = inputs.shape[0]
    half = up.shape[1] // 2
    width = half // 2
    core = (lax.axis_index("gy") % 2).astype(jnp.int32).reshape(1)

    unit = {(0, 0): jnp.stack([inputs, cotangent])}
    unit[0, 1] = swap(unit[0, 0], "gx", 2, 1)
    unit[1, 0] = swap(unit[0, 0], "gz", 4, 1)
    z = lax.axis_index("gz")
    middle = (z == 1) | (z == 2)
    across, outward = [(1, 2), (2, 1)], [(1, 0), (2, 3)]
    first = lax.ppermute(unit[0, 0], "gz", across)
    second = lax.ppermute(unit[1, 0], "gz", across)
    first_on = lax.ppermute(first, "gz", outward)
    second_on = lax.ppermute(second, "gz", outward)
    unit[2, 0] = jnp.where(middle, second, first_on)
    unit[3, 0] = jnp.where(middle, first, second_on)
    for d in (1, 2, 3):
        unit[d, 1] = swap(unit[d, 0], "gx", 2, 1)
    groups = [
        [unit[0, 0], unit[0, 1]],
        [unit[1, 0], unit[1, 1]],
        [unit[2, 0], unit[2, 1], unit[3, 0], unit[3, 1]],
    ]

    pair = 2 * rows
    pieces = [
        (0, 0, 0, width),
        (0, 0, width, width),
        (1, 0, 0, half),
        (2, 0, 0, half),
        (2, pair, 0, width),
        (2, pair, width, width),
    ]
    near, keep, far, act, act_near = {}, {}, {}, {}, {}
    *weights, = bring(core, up, down)
    ups, downs = weights[0::2], weights[1::2]

    def send(group, after=()):
        out = partial_sums(
            core, groups[group], ups[1], downs[1], 1, True, 0, half, after
        )
        near[group] = [swap(array, "gy", 4, 1) for array in out]
        return [out[0]]

    def hold(group, start, size, after):
        out, = partial_sums(
            core, groups[group], ups[0], downs[0], 0, False, start, size, after
        )
        keep[group, start] = out
        return [out]

    def kept(group, start):
        return (keep[group, start], 0) if (group, start) in keep else (keep[group, 0], start)

    def cross(n, after=()):
        group, row, start, size = pieces[n]
        array, column = kept(group, start)
        if after:
            chip = combine(core, array, near[group], row, pair, column, start, size, after)
        else:
            chip = jnp.stack([
                (
                    array[which, row : row + pair, column : column + size]
                    + near[group][which][row : row + pair, start : start + size].astype(F32)
                ).astype(BF16)
                for which in range(2)
            ])
        far[n] = swap(chip, "gy", 4, 2)
        return [chip]

    def ready(n, after):
        group, row, start, _ = pieces[n]
        array, column = kept(group, start)
        act[n] = activations(core, array, near[group], far[n], row, column, start, after)
        act_near[n] = swap(act[n], "gy", 4, 1)
        return [act[n]]

    def inward(which, start, size, part, order, leave, after):
        acts = [(act[n], act_near[n], offset) for n, offset in which]
        return back(core, acts, ups, start, size, part, order, leave, after)

    outputs = None

    def gradients(j, sides, after):
        acts = [
            [(array[j], 0), (array[2], j * width), (array[3], j * width), (array[4 + j], 0)]
            for array in (act, act_near)
        ]
        acts = [acts[side] for side in sides]
        return weight_grads(
            core, inputs_t, cotan, sides, acts, j * width, width, up.shape, outputs, after
        )

    def finish(j, sides, after):
        nonlocal outputs
        *outputs, done = gradients(j, sides, after)
        return [done]

    last = send(0)
    last = hold(0, 0, width, last)
    last = cross(0) + last
    last = hold(0, width, width, last + [])
    last = cross(1, last + [])
    last = send(1, last + [unit[1, 1], second, first_on])
    last = hold(1, 0, half, [*last, second_on])
    last = ready(0, last)
    last = ready(1, [*last, unit[2, 1]])
    last = cross(2, last)
    last = send(2, last)
    last = hold(2, 0, half, last)
    last = ready(2, last)
    last = cross(3) + last
    inputs_t, cotan = arrange(core, [u for group in groups for u in group], last)
    part, = inward(((0, 0), (2, 0)), 0, width, None, None, None, [inputs_t])
    stay1, go1 = inward(((1, 0), (2, width)), width, width, part, (0, 2, 1, 3), 2, [part])
    near1 = swap(go1, "gx", 2, 1)

    last = ready(3, [stay1])
    last = cross(4, last)
    total = fold(core, stay1[:rows], near1[:rows], F32, last)
    back1 = fold(core, stay1[rows:], near1[rows:], BF16, [total])
    far1 = swap(back1, "gz", 4, 1)
    stay2, go2 = inward(((3, 0),), 0, half, None, (0, 1), 1, [back1])
    near2 = swap(go2, "gx", 2, 1)

    last = ready(4, [stay2])
    last = cross(5, last)
    last = finish(0, (0,), last)
    back2 = fold(core, stay2, near2, BF16, last)
    far2 = swap(back2, "gz", 4, 2)
    part, = inward(((4, 0),), 0, width, None, None, None, [back2])
    last = finish(0, (1,), [part])
    total = fold(core, total, far1, F32, last)
    last = ready(5, [total])
    stay3, go3 = inward(((5, 0),), width, width, part, (0, 1), 1, last)
    near3 = swap(go3, "gx", 2, 1)
    last = finish(1, (0,), [stay3])
    back3 = fold(core, stay3, near3, BF16, last)
    far3 = swap(back3, "gz", 4, 3)
    finish(1, (1,), [back3])
    total = total + far2.astype(F32) + far3.astype(F32)
    return (total.astype(BF16), *outputs)


def solution(mesh):
    placed = (
        P(("gx", "gz"), "gy"),
        P(("gx", "gz"), "gy"),
        P("gy", ("gz", "gx")),
        P(("gz", "gx"), "gy"),
    )
    cube = tuple(mesh.shape[axis] for axis in ("gx", "gy", "gz")) == (2, 4, 4)
    return jax.shard_map(
        cube_body if cube else general_body,
        mesh=mesh,
        in_specs=placed,
        out_specs=(P(("gx", "gz"), "gy"), P("gy", ("gz", "gx")), P(("gz", "gx"), "gy")),
        check_vma=False,
    )
```

```python
import math

import jax
import jax.numpy as jnp
from jax import lax
from jax.experimental import pallas as pl
from jax.experimental.pallas import tpu as pltpu
from jax.sharding import PartitionSpec as P

F32 = jnp.float32
BF16 = jnp.bfloat16
VMEM_LIMIT = 10 * 1024 * 1024
GRADS_VMEM_LIMIT = 18 * 1024 * 1024
COST_PART = 1


def gelu_exact(value):
    return jax.nn.gelu(value, approximate=False)


def activate(preact, grad_hidden):
    activated, pullback = jax.vjp(gelu_exact, preact)
    grad_preact = pullback(grad_hidden)[0]
    return (activated.astype(BF16), grad_preact.astype(BF16))


def contract(left, right, left_dim, right_dim):
    return lax.dot_general(
        left, right, (((left_dim,), (right_dim,)), ((), ())), preferred_element_type=F32
    )


def general_body(inputs, cotangent, up_weight, down_weight):
    all_inputs = lax.all_gather(inputs, ("gx", "gz"), axis=0, tiled=True)
    all_cotan = lax.all_gather(cotangent, ("gx", "gz"), axis=0, tiled=True)
    preact = lax.psum_scatter(
        contract(all_inputs, up_weight, 1, 0), "gy", scatter_dimension=0, tiled=True
    )
    grad_hidden = lax.psum_scatter(
        contract(all_cotan, down_weight, 1, 1), "gy", scatter_dimension=0, tiled=True
    )
    hidden, grad_preact = activate(preact, grad_hidden)
    hidden = lax.all_gather(hidden, "gy", axis=0, tiled=True)
    grad_preact = lax.all_gather(grad_preact, "gy", axis=0, tiled=True)
    grad_down = contract(hidden, all_cotan, 0, 0)
    grad_up = contract(all_inputs, grad_preact, 0, 0)
    grad_inputs = lax.psum_scatter(
        contract(grad_preact, up_weight, 1, 1), ("gx", "gz"), scatter_dimension=0, tiled=True
    ).astype(BF16)
    return (grad_inputs, grad_up, grad_down)


def tile_of(width, most):
    tile = most
    while width % tile:
        tile //= 2
    return tile


def call(body, core, operands, in_specs, outs, out_specs, grid, cost, name, after=(), scratch=(), aliases=None, limit=VMEM_LIMIT):
    after = list(after)
    inner = len(operands) + 1

    def kernel(*refs):
        body(*refs[:inner], *refs[inner + len(after) :])

    flops, moved = cost
    return pl.pallas_call(
        kernel,
        grid_spec=pltpu.PrefetchScalarGridSpec(
            num_scalar_prefetch=1,
            grid=grid,
            in_specs=list(in_specs) + [pl.BlockSpec(memory_space=pl.ANY)] * len(after),
            out_specs=out_specs,
            scratch_shapes=list(scratch),
        ),
        out_shape=outs,
        input_output_aliases=aliases or {},
        compiler_params=pltpu.CompilerParams(vmem_limit_bytes=limit),
        cost_estimate=pl.CostEstimate(
            flops=flops // COST_PART, bytes_accessed=moved // COST_PART, transcendentals=0
        ),
        name=name,
    )(core, *operands, *after)


def whole(shape):
    return pl.BlockSpec(shape, lambda i, c: (0,) * len(shape))


def side_of(core_ref, side):
    return core_ref[0] if side == 0 else 1 - core_ref[0]


def halves(core_ref, side, up_ref, down_ref, up_out, down_out, sems, parts):
    half = up_out.shape[1]
    size = half // parts
    pairs = []
    for part in range(parts):
        begin = pl.multiple_of(side_of(core_ref, side) * half + part * size, size)
        here = pl.ds(part * size, size)
        pairs.append((
            pltpu.make_async_copy(up_ref.at[:, pl.ds(begin, size)], up_out.at[:, here], sems.at[0, part]),
            pltpu.make_async_copy(down_ref.at[pl.ds(begin, size)], down_out.at[here], sems.at[1, part]),
        ))
    return pairs


def half_outs(up):
    depth, half = up.shape[0], up.shape[1] // 2
    return [pltpu.VMEM((depth, half), BF16), pltpu.VMEM((half, depth), BF16)]


def bring(core, side, up, down):
    def body(core_ref, up_ref, down_ref, up_out, down_out, sems):
        pairs = halves(core_ref, side, up_ref, down_ref, up_out, down_out, sems, 1)
        for copy in pairs[0]:
            copy.start()
        for copy in pairs[0]:
            copy.wait()

    return call(
        body,
        core,
        [pltpu.with_memory_space_constraint(array, pltpu.HBM) for array in (up, down)],
        [pl.BlockSpec(memory_space=pltpu.HBM)] * 2,
        half_outs(up),
        [pl.BlockSpec(memory_space=pltpu.VMEM)] * 2,
        (1,),
        (0, 2 * up.size),
        "bring",
        (),
        [pltpu.SemaphoreType.DMA((2, 1))],
    )


def bring_and_sum(core, units, side, up, down, after=()):
    _, rows, depth = units[0].shape
    tokens = rows * len(units)
    half = up.shape[1] // 2
    parts = 3 if half % 384 == 0 else 1
    size = half // parts

    def body(core_ref, *refs):
        unit_refs = refs[: len(units)]
        up_ref, down_ref, out, up_out, down_out, acts, sems = refs[len(units) :]
        pairs = halves(core_ref, side, up_ref, down_ref, up_out, down_out, sems, parts)
        for pair in pairs:
            for copy in pair:
                copy.start()
        for n, ref in enumerate(unit_refs):
            acts[:, n * rows : (n + 1) * rows, :] = ref[...]
        for part, pair in enumerate(pairs):
            for copy in pair:
                copy.wait()
            here = slice(part * size, (part + 1) * size)
            out[0, :, here] = contract(acts[0], up_out[:, here], 1, 0)
            out[1, :, here] = contract(acts[1], down_out[here, :], 1, 1)

    return call(
        body,
        core,
        [*units] + [pltpu.with_memory_space_constraint(array, pltpu.HBM) for array in (up, down)],
        [whole(units[0].shape)] * len(units) + [pl.BlockSpec(memory_space=pltpu.HBM)] * 2,
        [jax.ShapeDtypeStruct((2, tokens, half), F32)] + half_outs(up),
        [whole((2, tokens, half))] + [pl.BlockSpec(memory_space=pltpu.VMEM)] * 2,
        (1,),
        (4 * tokens * depth * half, 2 * up.size),
        "bring_and_sum",
        after,
        [pltpu.VMEM((2, tokens, depth), BF16), pltpu.SemaphoreType.DMA((2, parts))],
    )


def partial_sums(core, units, up, down, side, apart, start, width, after=()):
    _, rows, depth = units[0].shape
    tokens = rows * len(units)
    tile = tile_of(width, 256)
    first = start // tile
    dtype = BF16 if side else F32

    def body(core_ref, *refs):
        *unit_refs, up_ref, down_ref = refs[: len(units) + 2]
        *out_refs, acts = refs[len(units) + 2 :]

        @pl.when(pl.program_id(0) == 0)
        def _():
            for n, ref in enumerate(unit_refs):
                acts[:, n * rows : (n + 1) * rows, :] = ref[...]

        preact = contract(acts[0], up_ref[...], 1, 0)
        grad_hidden = contract(acts[1], down_ref[...], 1, 1)
        if apart:
            out_refs[0][...] = preact.astype(dtype)
            out_refs[1][...] = grad_hidden.astype(dtype)
        else:
            out_refs[0][0] = preact.astype(dtype)
            out_refs[0][1] = grad_hidden.astype(dtype)

    if apart:
        outs = [jax.ShapeDtypeStruct((tokens, width), dtype)] * 2
        specs = [pl.BlockSpec((tokens, tile), lambda i, c: (0, i))] * 2
    else:
        outs = [jax.ShapeDtypeStruct((2, tokens, width), dtype)]
        specs = [pl.BlockSpec((2, tokens, tile), lambda i, c: (0, 0, i))]
    return call(
        body,
        core,
        [*units, up, down],
        [whole(units[0].shape)] * len(units)
        + [
            pl.BlockSpec((depth, tile), lambda i, c: (0, first + i)),
            pl.BlockSpec((tile, depth), lambda i, c: (first + i, 0)),
        ],
        outs,
        specs,
        (width // tile,),
        (4 * tokens * depth * width, 4 * depth * width),
        "sums_send" if side else "sums_keep",
        after,
        [pltpu.VMEM((2, tokens, depth), BF16)],
    )


def combine(core, keep, near, row, tokens, column, start, width, after):
    tile = tile_of(width, 256)
    both = pl.BlockSpec((2, tokens, tile), lambda i, c: (0, row // tokens, column // tile + i))
    one = pl.BlockSpec((tokens, tile), lambda i, c: (row // tokens, start // tile + i))

    def body(core_ref, keep_ref, preact_ref, grad_ref, chip_ref):
        chip_ref[0] = (keep_ref[0] + preact_ref[...].astype(F32)).astype(BF16)
        chip_ref[1] = (keep_ref[1] + grad_ref[...].astype(F32)).astype(BF16)

    return call(
        body,
        core,
        [keep, *near],
        [both, one, one],
        jax.ShapeDtypeStruct((2, tokens, width), BF16),
        pl.BlockSpec((2, tokens, tile), lambda i, c: (0, 0, i)),
        (width // tile,),
        (4 * tokens * width, 16 * tokens * width),
        "combine",
        after,
    )


def activations(core, keep, near, far, row, start, near_start, after=()):
    _, tokens, width = far.shape
    tile = tile_of(width, 256)
    first, near_first, block = start // tile, near_start // tile, row // tokens
    both = pl.BlockSpec((2, tokens, tile), lambda i, c: (0, block, first + i))
    both_here = pl.BlockSpec((2, tokens, tile), lambda i, c: (0, 0, i))
    one = pl.BlockSpec((tokens, tile), lambda i, c: (block, near_first + i))

    def body(core_ref, keep_ref, *refs):
        *near_refs, far_ref, act_ref = refs

        def total(which):
            part = near_refs[which][...].astype(F32)
            return keep_ref[which] + part + far_ref[which].astype(F32)

        preact = total(0)
        cdf = 0.5 + 0.5 * lax.erf(preact * (0.5**0.5))
        pdf = jnp.exp(-0.5 * preact * preact) * ((0.5 / math.pi) ** 0.5)
        act_ref[0] = (preact * cdf).astype(BF16)
        act_ref[1] = (total(1) * (cdf + preact * pdf)).astype(BF16)

    return call(
        body,
        core,
        [keep, *near, far],
        [both, one, one, both_here],
        jax.ShapeDtypeStruct(far.shape, BF16),
        both_here,
        (width // tile,),
        (60 * tokens * width, 20 * tokens * width),
        "activations",
        after,
    )


def back(core, acts, ups, start, width, before, order, leave, after=()):
    tokens = sum(which[0].shape[1] for which in acts)
    depth = ups[0].shape[0]
    tile = tile_of(depth, 512)
    groups = len(acts)

    def body(core_ref, *refs):
        part = None
        for side in range(2):
            mine = [ref[0] for ref in refs[side * groups : (side + 1) * groups]]
            mine = mine[0] if groups == 1 else jnp.concatenate(mine, axis=0)
            term = contract(mine, refs[2 * groups + side][...], 1, 1)
            part = term if part is None else part + term
        refs = refs[2 * groups + 2 :]
        if before is not None:
            part = part + refs[0][...]
        outs = refs[(before is not None) :]
        if leave is None:
            outs[0][...] = part
        else:
            rows = tokens // len(order)
            part = [part[n * rows : (n + 1) * rows] for n in order]
            outs[0][...] = jnp.concatenate(part[:leave], axis=0) if leave > 1 else part[0]
            outs[1][...] = jnp.concatenate(part[leave:], axis=0).astype(BF16)

    kinds = [(tokens, F32)]
    if leave is not None:
        rows = tokens // len(order)
        kinds = [(leave * rows, F32), (tokens - leave * rows, BF16)]
    operands = [which[side] for side in range(2) for which in acts]
    firsts = [which[2] // width for side in range(2) for which in acts]
    return call(
        body,
        core,
        [*operands, *ups] + ([] if before is None else [before]),
        [
            pl.BlockSpec((1, array.shape[1], width), lambda i, c, first=first: (1, 0, first))
            for array, first in zip(operands, firsts)
        ]
        + [pl.BlockSpec((tile, width), lambda i, c: (i, start // width))] * 2
        + ([] if before is None else [pl.BlockSpec((tokens, tile), lambda i, c: (0, i))]),
        [jax.ShapeDtypeStruct((rows, depth), dtype) for rows, dtype in kinds],
        [pl.BlockSpec((rows, tile), lambda i, c: (0, i)) for rows, _ in kinds],
        (depth // tile,),
        (4 * tokens * depth * width, 4 * depth * width + 4 * tokens * depth),
        "back",
        after,
    )


def fold(core, stay, near, dtype, after=()):
    rows, depth = stay.shape

    def body(core_ref, stay_ref, near_ref, out_ref):
        out_ref[...] = (stay_ref[...] + near_ref[...].astype(F32)).astype(dtype)

    return call(
        body,
        core,
        [stay, near],
        [whole(stay.shape)] * 2,
        jax.ShapeDtypeStruct(stay.shape, dtype),
        whole(stay.shape),
        (1,),
        (rows * depth, 8 * rows * depth),
        "fold",
        after,
    )


def arrange(core, units, after=()):
    _, rows, depth = units[0].shape
    tokens = rows * len(units)

    def body(core_ref, *refs):
        *unit_refs, inputs_t, cotan = refs
        inputs_t[...] = jnp.concatenate([ref[0] for ref in unit_refs], axis=0).T
        cotan[...] = jnp.concatenate([ref[1] for ref in unit_refs], axis=0)

    return call(
        body,
        core,
        units,
        [whole(units[0].shape)] * len(units),
        [jax.ShapeDtypeStruct((depth, tokens), BF16), jax.ShapeDtypeStruct((tokens, depth), BF16)],
        [whole((depth, tokens)), whole((tokens, depth))],
        (1,),
        (0, 8 * tokens * depth),
        "arrange",
        after,
    )


def weight_grads(core, inputs_t, cotan, sides, acts, start, width, shape, outputs, after=()):
    depth, full = shape
    tokens = cotan.shape[0]
    half = full // 2
    tile = tile_of(width, 256)
    steps = width // tile
    groups = len(acts[0])

    def body(core_ref, inputs_ref, cotan_ref, *refs):
        up_out, down_out, done = refs[-3:]
        done[...] = jnp.zeros_like(done)
        for order in range(len(sides)):
            mine = refs[order * groups : (order + 1) * groups]

            @pl.when(pl.program_id(0) // steps == order)
            def _(mine=mine):
                hidden = jnp.concatenate([ref[0] for ref in mine], axis=0)
                grad = jnp.concatenate([ref[1] for ref in mine], axis=0)
                up_out[...] = contract(inputs_ref[...], grad, 1, 0)
                down_out[...] = contract(hidden, cotan_ref[...], 0, 0)

    def place(i, c):
        which = side_of(c, sides[0])
        if len(sides) > 1:
            which = jnp.where(i // steps == 0, which, 1 - which)
        return which * (half // tile) + start // tile + i % steps

    operands = [inputs_t, cotan]
    specs = [whole(inputs_t.shape), whole(cotan.shape)]
    for order in range(len(sides)):
        for array, offset in acts[order]:

            def index(i, c, order=order, first=offset // tile):
                return (0, 0, first + jnp.clip(i - order * steps, 0, steps - 1))

            operands.append(array)
            specs.append(pl.BlockSpec((2, array.shape[1], tile), index))
    aliases = None
    if outputs is not None:
        aliases = {len(operands) + 1: 0, len(operands) + 2: 1}
        operands += list(outputs)
        specs += [pl.BlockSpec(memory_space=pl.ANY)] * 2
    many = width * len(sides)
    return call(
        body,
        core,
        operands,
        specs,
        [
            jax.ShapeDtypeStruct((depth, full), F32),
            jax.ShapeDtypeStruct((full, depth), F32),
            jax.ShapeDtypeStruct((8, 128), F32),
        ],
        [
            pl.BlockSpec((depth, tile), lambda i, c: (0, place(i, c))),
            pl.BlockSpec((tile, depth), lambda i, c: (place(i, c), 0)),
            whole((8, 128)),
        ],
        (steps * len(sides),),
        (4 * tokens * depth * many, 8 * depth * many),
        "weight_grads",
        after,
        aliases=aliases,
        limit=GRADS_VMEM_LIMIT,
    )


def swap(value, axis, size, bits):
    return lax.ppermute(value, axis, [(i, i ^ bits) for i in range(size)])


def cube_body(inputs, cotangent, up, down):
    rows = inputs.shape[0]
    half = up.shape[1] // 2
    width = half // 2
    core = (lax.axis_index("gy") % 2).astype(jnp.int32).reshape(1)

    unit = {(0, 0): jnp.stack([inputs, cotangent])}
    unit[0, 1] = swap(unit[0, 0], "gx", 2, 1)
    unit[1, 0] = swap(unit[0, 0], "gz", 4, 1)
    z = lax.axis_index("gz")
    middle = (z == 1) | (z == 2)
    across, outward = [(1, 2), (2, 1)], [(1, 0), (2, 3)]
    first = lax.ppermute(unit[0, 0], "gz", across)
    second = lax.ppermute(unit[1, 0], "gz", across)
    first_on = lax.ppermute(first, "gz", outward)
    second_on = lax.ppermute(second, "gz", outward)
    unit[2, 0] = jnp.where(middle, second, first_on)
    unit[3, 0] = jnp.where(middle, first, second_on)
    for d in (1, 2, 3):
        unit[d, 1] = swap(unit[d, 0], "gx", 2, 1)
    groups = [
        [unit[0, 0], unit[0, 1]],
        [unit[1, 0], unit[1, 1]],
        [unit[2, 0], unit[2, 1], unit[3, 0], unit[3, 1]],
    ]

    pair = 2 * rows
    pieces = [
        (0, 0, 0, half),
        (1, 0, 0, half),
        (2, 0, 0, half),
        (2, pair, 0, width),
        (2, pair, width, width),
    ]
    near, keep, far, act, act_near = {}, {}, {}, {}, {}
    ups, downs = {}, {}
    ups[1], downs[1] = bring(core, 1, up, down)

    def send(group, after=()):
        out = partial_sums(
            core, groups[group], ups[1], downs[1], 1, True, 0, half, after
        )
        near[group] = [swap(array, "gy", 4, 1) for array in out]
        return [out[0]]

    def hold(group, start, size, after):
        if group:
            out, = partial_sums(
                core, groups[group], ups[0], downs[0], 0, False, start, size, after
            )
        else:
            out, ups[0], downs[0] = bring_and_sum(core, groups[group], 0, up, down, after)
        keep[group, start] = out
        return [out]

    def kept(group, start):
        return (keep[group, start], 0) if (group, start) in keep else (keep[group, 0], start)

    def cross(n, after=()):
        group, row, start, size = pieces[n]
        array, column = kept(group, start)
        if after:
            chip = combine(core, array, near[group], row, pair, column, start, size, after)
        else:
            chip = jnp.stack([
                (
                    array[which, row : row + pair, column : column + size]
                    + near[group][which][row : row + pair, start : start + size].astype(F32)
                ).astype(BF16)
                for which in range(2)
            ])
        far[n] = swap(chip, "gy", 4, 2)
        return [chip]

    def ready(n, after):
        group, row, start, _ = pieces[n]
        array, column = kept(group, start)
        act[n] = activations(core, array, near[group], far[n], row, column, start, after)
        act_near[n] = swap(act[n], "gy", 4, 1)
        return [act[n]]

    def inward(which, start, size, part, order, leave, after):
        acts = [(act[n], act_near[n], offset) for n, offset in which]
        return back(core, acts, (ups[0], ups[1]), start, size, part, order, leave, after)

    outputs = None

    def gradients(j, sides, after):
        acts = [
            [(array[n], j * width) for n in range(3)] + [(array[3 + j], 0)]
            for array in (act, act_near)
        ]
        acts = [acts[side] for side in sides]
        return weight_grads(
            core, inputs_t, cotan, sides, acts, j * width, width, up.shape, outputs, after
        )

    def finish(j, sides, after):
        nonlocal outputs
        *outputs, done = gradients(j, sides, after)
        return [done]

    last = send(0)
    last = hold(0, 0, half, last)
    last = cross(0, [*last, unit[1, 1], first_on, second])
    last = send(1, last)
    last = hold(1, 0, half, [*last, second_on])
    last = ready(0, [*last, unit[2, 1]])
    last = cross(1, last)
    last = send(2, last)
    last = hold(2, 0, half, last)
    last = ready(1, last)
    last = cross(2) + last
    inputs_t, cotan = arrange(core, [u for group in groups for u in group], last)
    stay1, go1 = inward(((0, 0), (1, 0)), 0, half, None, (0, 2, 1, 3), 2, [inputs_t])
    near1 = swap(go1, "gx", 2, 1)

    last = ready(2, [stay1])
    last = cross(3, last)
    total = fold(core, stay1[:rows], near1[:rows], F32, last)
    back1 = fold(core, stay1[rows:], near1[rows:], BF16, [total])
    far1 = swap(back1, "gz", 4, 1)
    stay2, go2 = inward(((2, 0),), 0, half, None, (0, 1), 1, [back1])
    near2 = swap(go2, "gx", 2, 1)

    last = ready(3, [stay2])
    last = cross(4, last)
    last = finish(0, (0,), last)
    back2 = fold(core, stay2, near2, BF16, last)
    far2 = swap(back2, "gz", 4, 2)
    part, = inward(((3, 0),), 0, width, None, None, None, [back2])
    last = finish(0, (1,), [part])
    total = fold(core, total, far1, F32, last)
    last = ready(4, [total])
    stay3, go3 = inward(((4, 0),), width, width, part, (0, 1), 1, last)
    near3 = swap(go3, "gx", 2, 1)
    last = finish(1, (0,), [stay3])
    back3 = fold(core, stay3, near3, BF16, last)
    far3 = swap(back3, "gz", 4, 3)
    finish(1, (1,), [back3])
    total = total + far2.astype(F32) + far3.astype(F32)
    return (total.astype(BF16), *outputs)


def solution(mesh):
    placed = (
        P(("gx", "gz"), "gy"),
        P(("gx", "gz"), "gy"),
        P("gy", ("gz", "gx")),
        P(("gz", "gx"), "gy"),
    )
    cube = tuple(mesh.shape[axis] for axis in ("gx", "gy", "gz")) == (2, 4, 4)
    return jax.shard_map(
        cube_body if cube else general_body,
        mesh=mesh,
        in_specs=placed,
        out_specs=(P(("gx", "gz"), "gy"), P("gy", ("gz", "gx")), P(("gz", "gx"), "gy")),
        check_vma=False,
    )
```

```python
import math

import jax
import jax.numpy as jnp
from jax import lax
from jax.experimental import pallas as pl
from jax.experimental.pallas import tpu as pltpu
from jax.sharding import PartitionSpec as P

F32 = jnp.float32
BF16 = jnp.bfloat16
VMEM_LIMIT = 10 * 1024 * 1024
GRADS_VMEM_LIMIT = 18 * 1024 * 1024
COST_PART = 1


def gelu_exact(value):
    return jax.nn.gelu(value, approximate=False)


def activate(preact, grad_hidden):
    activated, pullback = jax.vjp(gelu_exact, preact)
    grad_preact = pullback(grad_hidden)[0]
    return (activated.astype(BF16), grad_preact.astype(BF16))


def contract(left, right, left_dim, right_dim):
    return lax.dot_general(
        left, right, (((left_dim,), (right_dim,)), ((), ())), preferred_element_type=F32
    )


def general_body(inputs, cotangent, up_weight, down_weight):
    all_inputs = lax.all_gather(inputs, ("gx", "gz"), axis=0, tiled=True)
    all_cotan = lax.all_gather(cotangent, ("gx", "gz"), axis=0, tiled=True)
    preact = lax.psum_scatter(
        contract(all_inputs, up_weight, 1, 0), "gy", scatter_dimension=0, tiled=True
    )
    grad_hidden = lax.psum_scatter(
        contract(all_cotan, down_weight, 1, 1), "gy", scatter_dimension=0, tiled=True
    )
    hidden, grad_preact = activate(preact, grad_hidden)
    hidden = lax.all_gather(hidden, "gy", axis=0, tiled=True)
    grad_preact = lax.all_gather(grad_preact, "gy", axis=0, tiled=True)
    grad_down = contract(hidden, all_cotan, 0, 0)
    grad_up = contract(all_inputs, grad_preact, 0, 0)
    grad_inputs = lax.psum_scatter(
        contract(grad_preact, up_weight, 1, 1), ("gx", "gz"), scatter_dimension=0, tiled=True
    ).astype(BF16)
    return (grad_inputs, grad_up, grad_down)


def tile_of(width, most):
    tile = most
    while width % tile:
        tile //= 2
    return tile


def call(body, core, operands, in_specs, outs, out_specs, grid, cost, name, after=(), scratch=(), aliases=None, limit=VMEM_LIMIT):
    after = list(after)
    inner = len(operands) + 1

    def kernel(*refs):
        body(*refs[:inner], *refs[inner + len(after) :])

    flops, moved = cost
    return pl.pallas_call(
        kernel,
        grid_spec=pltpu.PrefetchScalarGridSpec(
            num_scalar_prefetch=1,
            grid=grid,
            in_specs=list(in_specs) + [pl.BlockSpec(memory_space=pl.ANY)] * len(after),
            out_specs=out_specs,
            scratch_shapes=list(scratch),
        ),
        out_shape=outs,
        input_output_aliases=aliases or {},
        compiler_params=pltpu.CompilerParams(vmem_limit_bytes=limit),
        cost_estimate=pl.CostEstimate(
            flops=flops // COST_PART, bytes_accessed=moved // COST_PART, transcendentals=0
        ),
        name=name,
    )(core, *operands, *after)


def whole(shape):
    return pl.BlockSpec(shape, lambda i, c: (0,) * len(shape))


def side_of(core_ref, side):
    return core_ref[0] if side == 0 else 1 - core_ref[0]


def halves(core_ref, side, up_ref, down_ref, up_out, down_out, sems, parts):
    half = up_out.shape[1]
    size = half // parts
    pairs = []
    for part in range(parts):
        begin = pl.multiple_of(side_of(core_ref, side) * half + part * size, size)
        here = pl.ds(part * size, size)
        pairs.append((
            pltpu.make_async_copy(up_ref.at[:, pl.ds(begin, size)], up_out.at[:, here], sems.at[0, part]),
            pltpu.make_async_copy(down_ref.at[pl.ds(begin, size)], down_out.at[here], sems.at[1, part]),
        ))
    return pairs


def half_outs(up):
    depth, half = up.shape[0], up.shape[1] // 2
    return [pltpu.VMEM((depth, half), BF16), pltpu.VMEM((half, depth), BF16)]


def bring(core, side, up, down):
    def body(core_ref, up_ref, down_ref, up_out, down_out, sems):
        pairs = halves(core_ref, side, up_ref, down_ref, up_out, down_out, sems, 1)
        for copy in pairs[0]:
            copy.start()
        for copy in pairs[0]:
            copy.wait()

    return call(
        body,
        core,
        [pltpu.with_memory_space_constraint(array, pltpu.HBM) for array in (up, down)],
        [pl.BlockSpec(memory_space=pltpu.HBM)] * 2,
        half_outs(up),
        [pl.BlockSpec(memory_space=pltpu.VMEM)] * 2,
        (1,),
        (0, 2 * up.size),
        "bring",
        (),
        [pltpu.SemaphoreType.DMA((2, 1))],
    )


def bring_and_sum(core, units, side, up, down, after=()):
    _, rows, depth = units[0].shape
    tokens = rows * len(units)
    half = up.shape[1] // 2
    parts = 3 if half % 384 == 0 else 1
    size = half // parts

    def body(core_ref, *refs):
        unit_refs = refs[: len(units)]
        up_ref, down_ref, out, up_out, down_out, acts, sems = refs[len(units) :]
        pairs = halves(core_ref, side, up_ref, down_ref, up_out, down_out, sems, parts)
        for pair in pairs:
            for copy in pair:
                copy.start()
        for n, ref in enumerate(unit_refs):
            acts[:, n * rows : (n + 1) * rows, :] = ref[...]
        for part, pair in enumerate(pairs):
            for copy in pair:
                copy.wait()
            here = slice(part * size, (part + 1) * size)
            out[0, :, here] = contract(acts[0], up_out[:, here], 1, 0)
            out[1, :, here] = contract(acts[1], down_out[here, :], 1, 1)

    return call(
        body,
        core,
        [*units] + [pltpu.with_memory_space_constraint(array, pltpu.HBM) for array in (up, down)],
        [whole(units[0].shape)] * len(units) + [pl.BlockSpec(memory_space=pltpu.HBM)] * 2,
        [jax.ShapeDtypeStruct((2, tokens, half), F32)] + half_outs(up),
        [whole((2, tokens, half))] + [pl.BlockSpec(memory_space=pltpu.VMEM)] * 2,
        (1,),
        (4 * tokens * depth * half, 2 * up.size),
        "bring_and_sum",
        after,
        [pltpu.VMEM((2, tokens, depth), BF16), pltpu.SemaphoreType.DMA((2, parts))],
    )


def partial_sums(core, units, up, down, side, apart, start, width, after=()):
    _, rows, depth = units[0].shape
    tokens = rows * len(units)
    tile = tile_of(width, 256)
    first = start // tile
    dtype = BF16 if side else F32

    def body(core_ref, *refs):
        *unit_refs, up_ref, down_ref = refs[: len(units) + 2]
        *out_refs, acts = refs[len(units) + 2 :]

        @pl.when(pl.program_id(0) == 0)
        def _():
            for n, ref in enumerate(unit_refs):
                acts[:, n * rows : (n + 1) * rows, :] = ref[...]

        preact = contract(acts[0], up_ref[...], 1, 0)
        grad_hidden = contract(acts[1], down_ref[...], 1, 1)
        if apart:
            out_refs[0][...] = preact.astype(dtype)
            out_refs[1][...] = grad_hidden.astype(dtype)
        else:
            out_refs[0][0] = preact.astype(dtype)
            out_refs[0][1] = grad_hidden.astype(dtype)

    if apart:
        outs = [jax.ShapeDtypeStruct((tokens, width), dtype)] * 2
        specs = [pl.BlockSpec((tokens, tile), lambda i, c: (0, i))] * 2
    else:
        outs = [jax.ShapeDtypeStruct((2, tokens, width), dtype)]
        specs = [pl.BlockSpec((2, tokens, tile), lambda i, c: (0, 0, i))]
    return call(
        body,
        core,
        [*units, up, down],
        [whole(units[0].shape)] * len(units)
        + [
            pl.BlockSpec((depth, tile), lambda i, c: (0, first + i)),
            pl.BlockSpec((tile, depth), lambda i, c: (first + i, 0)),
        ],
        outs,
        specs,
        (width // tile,),
        (4 * tokens * depth * width, 4 * depth * width),
        "sums_send" if side else "sums_keep",
        after,
        [pltpu.VMEM((2, tokens, depth), BF16)],
    )


def combine(core, keep, near, row, tokens, column, start, width, after):
    tile = tile_of(width, 256)
    both = pl.BlockSpec((2, tokens, tile), lambda i, c: (0, row // tokens, column // tile + i))
    one = pl.BlockSpec((tokens, tile), lambda i, c: (row // tokens, start // tile + i))

    def body(core_ref, keep_ref, preact_ref, grad_ref, chip_ref):
        chip_ref[0] = (keep_ref[0] + preact_ref[...].astype(F32)).astype(BF16)
        chip_ref[1] = (keep_ref[1] + grad_ref[...].astype(F32)).astype(BF16)

    return call(
        body,
        core,
        [keep, *near],
        [both, one, one],
        jax.ShapeDtypeStruct((2, tokens, width), BF16),
        pl.BlockSpec((2, tokens, tile), lambda i, c: (0, 0, i)),
        (width // tile,),
        (4 * tokens * width, 16 * tokens * width),
        "combine",
        after,
    )


def activations(core, keep, near, far, row, start, near_start, after=()):
    _, tokens, width = far.shape
    tile = tile_of(width, 256)
    first, near_first, block = start // tile, near_start // tile, row // tokens
    both = pl.BlockSpec((2, tokens, tile), lambda i, c: (0, block, first + i))
    both_here = pl.BlockSpec((2, tokens, tile), lambda i, c: (0, 0, i))
    one = pl.BlockSpec((tokens, tile), lambda i, c: (block, near_first + i))

    def body(core_ref, keep_ref, *refs):
        *near_refs, far_ref, act_ref = refs

        def total(which):
            part = near_refs[which][...].astype(F32)
            return keep_ref[which] + part + far_ref[which].astype(F32)

        preact = total(0)
        cdf = 0.5 + 0.5 * lax.erf(preact * (0.5**0.5))
        pdf = jnp.exp(-0.5 * preact * preact) * ((0.5 / math.pi) ** 0.5)
        act_ref[0] = (preact * cdf).astype(BF16)
        act_ref[1] = (total(1) * (cdf + preact * pdf)).astype(BF16)

    return call(
        body,
        core,
        [keep, *near, far],
        [both, one, one, both_here],
        jax.ShapeDtypeStruct(far.shape, BF16),
        both_here,
        (width // tile,),
        (60 * tokens * width, 20 * tokens * width),
        "activations",
        after,
    )


def back(core, acts, ups, start, width, before, row, order, leave, after=()):
    tokens = sum(which[0].shape[1] for which in acts)
    depth = ups[0].shape[0]
    tile = tile_of(depth, 512)
    groups = len(acts)

    def body(core_ref, *refs):
        part = None
        for side in range(2):
            mine = [ref[0] for ref in refs[side * groups : (side + 1) * groups]]
            mine = mine[0] if groups == 1 else jnp.concatenate(mine, axis=0)
            term = contract(mine, refs[2 * groups + side][...], 1, 1)
            part = term if part is None else part + term
        refs = refs[2 * groups + 2 :]
        if before is not None:
            part = part + refs[0][...]
        outs = refs[(before is not None) :]
        if leave is None:
            outs[0][...] = part
        else:
            rows = tokens // len(order)
            part = [part[n * rows : (n + 1) * rows] for n in order]
            outs[0][...] = jnp.concatenate(part[:leave], axis=0) if leave > 1 else part[0]
            outs[1][...] = jnp.concatenate(part[leave:], axis=0).astype(BF16)

    kinds = [(tokens, F32)]
    if leave is not None:
        rows = tokens // len(order)
        kinds = [(leave * rows, F32), (tokens - leave * rows, BF16)]
    operands = [which[side] for side in range(2) for which in acts]
    firsts = [which[2] // width for side in range(2) for which in acts]
    return call(
        body,
        core,
        [*operands, *ups] + ([] if before is None else [before]),
        [
            pl.BlockSpec((1, array.shape[1], width), lambda i, c, first=first: (1, 0, first))
            for array, first in zip(operands, firsts)
        ]
        + [pl.BlockSpec((tile, width), lambda i, c: (i, start // width))] * 2
        + ([] if before is None else [pl.BlockSpec((tokens, tile), lambda i, c: (row // tokens, i))]),
        [jax.ShapeDtypeStruct((rows, depth), dtype) for rows, dtype in kinds],
        [pl.BlockSpec((rows, tile), lambda i, c: (0, i)) for rows, _ in kinds],
        (depth // tile,),
        (4 * tokens * depth * width, 4 * depth * width + 4 * tokens * depth),
        "back",
        after,
    )


def fold(core, stay, near, dtype, after=()):
    rows, depth = stay.shape

    def body(core_ref, stay_ref, near_ref, out_ref):
        out_ref[...] = (stay_ref[...] + near_ref[...].astype(F32)).astype(dtype)

    return call(
        body,
        core,
        [stay, near],
        [whole(stay.shape)] * 2,
        jax.ShapeDtypeStruct(stay.shape, dtype),
        whole(stay.shape),
        (1,),
        (rows * depth, 8 * rows * depth),
        "fold",
        after,
    )


def arrange(core, units, after=()):
    _, rows, depth = units[0].shape
    tokens = rows * len(units)

    def body(core_ref, *refs):
        *unit_refs, inputs_t, cotan = refs
        inputs_t[...] = jnp.concatenate([ref[0] for ref in unit_refs], axis=0).T
        cotan[...] = jnp.concatenate([ref[1] for ref in unit_refs], axis=0)

    return call(
        body,
        core,
        units,
        [whole(units[0].shape)] * len(units),
        [jax.ShapeDtypeStruct((depth, tokens), BF16), jax.ShapeDtypeStruct((tokens, depth), BF16)],
        [whole((depth, tokens)), whole((tokens, depth))],
        (1,),
        (0, 8 * tokens * depth),
        "arrange",
        after,
    )


def weight_grads(core, inputs_t, cotan, sides, acts, start, width, shape, outputs, after=()):
    depth, full = shape
    tokens = cotan.shape[0]
    half = full // 2
    tile = tile_of(width, 256)
    steps = width // tile
    groups = len(acts[0])

    def body(core_ref, inputs_ref, cotan_ref, *refs):
        up_out, down_out, done = refs[-3:]
        done[...] = jnp.zeros_like(done)
        for order in range(len(sides)):
            mine = refs[order * groups : (order + 1) * groups]

            @pl.when(pl.program_id(0) // steps == order)
            def _(mine=mine):
                hidden = jnp.concatenate([ref[0] for ref in mine], axis=0)
                grad = jnp.concatenate([ref[1] for ref in mine], axis=0)
                up_out[...] = contract(inputs_ref[...], grad, 1, 0)
                down_out[...] = contract(hidden, cotan_ref[...], 0, 0)

    def place(i, c):
        which = side_of(c, sides[0])
        if len(sides) > 1:
            which = jnp.where(i // steps == 0, which, 1 - which)
        return which * (half // tile) + start // tile + i % steps

    operands = [inputs_t, cotan]
    specs = [whole(inputs_t.shape), whole(cotan.shape)]
    for order in range(len(sides)):
        for array, offset in acts[order]:

            def index(i, c, order=order, first=offset // tile):
                return (0, 0, first + jnp.clip(i - order * steps, 0, steps - 1))

            operands.append(array)
            specs.append(pl.BlockSpec((2, array.shape[1], tile), index))
    aliases = None
    if outputs is not None:
        aliases = {len(operands) + 1: 0, len(operands) + 2: 1}
        operands += list(outputs)
        specs += [pl.BlockSpec(memory_space=pl.ANY)] * 2
    many = width * len(sides)
    return call(
        body,
        core,
        operands,
        specs,
        [
            jax.ShapeDtypeStruct((depth, full), F32),
            jax.ShapeDtypeStruct((full, depth), F32),
            jax.ShapeDtypeStruct((8, 128), F32),
        ],
        [
            pl.BlockSpec((depth, tile), lambda i, c: (0, place(i, c))),
            pl.BlockSpec((tile, depth), lambda i, c: (place(i, c), 0)),
            whole((8, 128)),
        ],
        (steps * len(sides),),
        (4 * tokens * depth * many, 8 * depth * many),
        "weight_grads",
        after,
        aliases=aliases,
        limit=GRADS_VMEM_LIMIT,
    )


def swap(value, axis, size, bits):
    return lax.ppermute(value, axis, [(i, i ^ bits) for i in range(size)])


def cube_body(inputs, cotangent, up, down):
    rows = inputs.shape[0]
    half = up.shape[1] // 2
    width = half // 2
    core = (lax.axis_index("gy") % 2).astype(jnp.int32).reshape(1)

    unit = {(0, 0): jnp.stack([inputs, cotangent])}
    unit[0, 1] = swap(unit[0, 0], "gx", 2, 1)
    unit[1, 0] = swap(unit[0, 0], "gz", 4, 1)
    z = lax.axis_index("gz")
    middle = (z == 1) | (z == 2)
    across, outward = [(1, 2), (2, 1)], [(1, 0), (2, 3)]
    first = lax.ppermute(unit[0, 0], "gz", across)
    ups, downs = {}, {}
    ups[1], downs[1] = bring(core, 1, up, down)
    second = lax.ppermute(unit[1, 0], "gz", across)
    first_on = lax.ppermute(first, "gz", outward)
    second_on = lax.ppermute(second, "gz", outward)
    unit[2, 0] = jnp.where(middle, second, first_on)
    unit[3, 0] = jnp.where(middle, first, second_on)
    for d in (1, 2, 3):
        unit[d, 1] = swap(unit[d, 0], "gx", 2, 1)
    groups = [
        [unit[0, 0], unit[0, 1]],
        [unit[1, 0], unit[1, 1]],
        [unit[2, 0], unit[2, 1], unit[3, 0], unit[3, 1]],
    ]

    pair = 2 * rows
    pieces = [
        (0, 0, pair, 0, half),
        (1, 0, pair, 0, half),
        (2, 0, 2 * pair, 0, width),
        (2, 0, pair, width, width),
        (2, pair, pair, width, width),
    ]
    near, keep, far, act, act_near = {}, {}, {}, {}, {}

    def send(group, after=()):
        out = partial_sums(
            core, groups[group], ups[1], downs[1], 1, True, 0, half, after
        )
        near[group] = [swap(array, "gy", 4, 1) for array in out]
        return [out[0]]

    def hold(group, start, size, after):
        if group:
            out, = partial_sums(
                core, groups[group], ups[0], downs[0], 0, False, start, size, after
            )
        else:
            out, ups[0], downs[0] = bring_and_sum(core, groups[group], 0, up, down, after)
        keep[group, start] = out
        return [out]

    def kept(group, start):
        return (keep[group, start], 0) if (group, start) in keep else (keep[group, 0], start)

    def cross(n, after=()):
        group, row, count, start, size = pieces[n]
        array, column = kept(group, start)
        if after:
            chip = combine(core, array, near[group], row, count, column, start, size, after)
        else:
            chip = jnp.stack([
                (
                    array[which, row : row + count, column : column + size]
                    + near[group][which][row : row + count, start : start + size].astype(F32)
                ).astype(BF16)
                for which in range(2)
            ])
        far[n] = swap(chip, "gy", 4, 2)
        return [chip]

    def ready(n, after):
        group, row, _, start, _ = pieces[n]
        array, column = kept(group, start)
        act[n] = activations(core, array, near[group], far[n], row, column, start, after)
        act_near[n] = swap(act[n], "gy", 4, 1)
        return [act[n]]

    def inward(which, start, size, part, row, order, leave, after):
        acts = [(act[n], act_near[n], offset) for n, offset in which]
        return back(core, acts, (ups[0], ups[1]), start, size, part, row, order, leave, after)

    outputs = None

    def gradients(j, sides, after):
        acts = [
            [(array[n], j * width) for n in range(2)]
            + ([(array[3], 0), (array[4], 0)] if j else [(array[2], 0)])
            for array in (act, act_near)
        ]
        acts = [acts[side] for side in sides]
        return weight_grads(
            core, inputs_t, cotan, sides, acts, j * width, width, up.shape, outputs, after
        )

    def finish(j, sides, after):
        nonlocal outputs
        *outputs, done = gradients(j, sides, after)
        return [done]

    last = send(0)
    last = hold(0, 0, half, last)
    last = cross(0, [*last, unit[1, 1]])
    last = send(1, [*last, first_on, second])
    last = hold(1, 0, half, [*last, second_on])
    last = ready(0, [*last, unit[2, 1]])
    last = cross(1, last)
    last = send(2, last)
    last = hold(2, 0, half, last)
    last = ready(1, last)
    last = cross(2) + last
    inputs_t, cotan = arrange(core, [u for group in groups for u in group], last)
    stay1, go1 = inward(((0, 0), (1, 0)), 0, half, None, 0, (0, 2, 1, 3), 2, [inputs_t])
    near1 = swap(go1, "gx", 2, 1)

    last = ready(2, [stay1])
    last = cross(3, last)
    last = finish(0, (0,), last)
    last = ready(3, last)
    last = cross(4, last)
    total = fold(core, stay1[:rows], near1[:rows], F32, last)
    back1 = fold(core, stay1[rows:], near1[rows:], BF16, [total])
    far1 = swap(back1, "gz", 4, 1)
    part, = inward(((2, 0),), 0, width, None, 0, None, None, [back1])
    last = finish(0, (1,), [part])
    stay2, go2 = inward(((3, 0),), width, width, part, 0, (0, 1), 1, last)
    near2 = swap(go2, "gx", 2, 1)
    total = fold(core, total, far1, F32, [stay2])
    last = ready(4, [total])
    stay3, go3 = inward(((4, 0),), width, width, part, pair, (0, 1), 1, last)
    near3 = swap(go3, "gx", 2, 1)
    back2 = fold(core, stay2, near2, BF16, [stay3])
    far2 = swap(back2, "gz", 4, 2)
    last = finish(1, (0,), [back2])
    back3 = fold(core, stay3, near3, BF16, last)
    far3 = swap(back3, "gz", 4, 3)
    finish(1, (1,), [back3])
    total = total + far2.astype(F32) + far3.astype(F32)
    return (total.astype(BF16), *outputs)


def solution(mesh):
    placed = (
        P(("gx", "gz"), "gy"),
        P(("gx", "gz"), "gy"),
        P("gy", ("gz", "gx")),
        P(("gz", "gx"), "gy"),
    )
    cube = tuple(mesh.shape[axis] for axis in ("gx", "gy", "gz")) == (2, 4, 4)
    return jax.shard_map(
        cube_body if cube else general_body,
        mesh=mesh,
        in_specs=placed,
        out_specs=(P(("gx", "gz"), "gy"), P("gy", ("gz", "gx")), P(("gz", "gx"), "gy")),
        check_vma=False,
    )
```

```python
import math

import jax
import jax.numpy as jnp
from jax import lax
from jax.experimental import pallas as pl
from jax.experimental.pallas import tpu as pltpu
from jax.sharding import PartitionSpec as P

F32 = jnp.float32
BF16 = jnp.bfloat16
VMEM_LIMIT = 10 * 1024 * 1024
GRADS_VMEM_LIMIT = 18 * 1024 * 1024
COST_PART = 1


def gelu_exact(value):
    return jax.nn.gelu(value, approximate=False)


def activate(preact, grad_hidden):
    activated, pullback = jax.vjp(gelu_exact, preact)
    grad_preact = pullback(grad_hidden)[0]
    return (activated.astype(BF16), grad_preact.astype(BF16))


def contract(left, right, left_dim, right_dim):
    return lax.dot_general(
        left, right, (((left_dim,), (right_dim,)), ((), ())), preferred_element_type=F32
    )


def general_body(inputs, cotangent, up_weight, down_weight):
    all_inputs = lax.all_gather(inputs, ("gx", "gz"), axis=0, tiled=True)
    all_cotan = lax.all_gather(cotangent, ("gx", "gz"), axis=0, tiled=True)
    preact = lax.psum_scatter(
        contract(all_inputs, up_weight, 1, 0), "gy", scatter_dimension=0, tiled=True
    )
    grad_hidden = lax.psum_scatter(
        contract(all_cotan, down_weight, 1, 1), "gy", scatter_dimension=0, tiled=True
    )
    hidden, grad_preact = activate(preact, grad_hidden)
    hidden = lax.all_gather(hidden, "gy", axis=0, tiled=True)
    grad_preact = lax.all_gather(grad_preact, "gy", axis=0, tiled=True)
    grad_down = contract(hidden, all_cotan, 0, 0)
    grad_up = contract(all_inputs, grad_preact, 0, 0)
    grad_inputs = lax.psum_scatter(
        contract(grad_preact, up_weight, 1, 1), ("gx", "gz"), scatter_dimension=0, tiled=True
    ).astype(BF16)
    return (grad_inputs, grad_up, grad_down)


def tile_of(width, most):
    tile = most
    while width % tile:
        tile //= 2
    return tile


def call(body, core, operands, in_specs, outs, out_specs, grid, cost, name, after=(), scratch=(), aliases=None, limit=VMEM_LIMIT):
    after = list(after)
    inner = len(operands) + 1

    def kernel(*refs):
        body(*refs[:inner], *refs[inner + len(after) :])

    flops, moved = cost
    return pl.pallas_call(
        kernel,
        grid_spec=pltpu.PrefetchScalarGridSpec(
            num_scalar_prefetch=1,
            grid=grid,
            in_specs=list(in_specs) + [pl.BlockSpec(memory_space=pl.ANY)] * len(after),
            out_specs=out_specs,
            scratch_shapes=list(scratch),
        ),
        out_shape=outs,
        input_output_aliases=aliases or {},
        compiler_params=pltpu.CompilerParams(vmem_limit_bytes=limit),
        cost_estimate=pl.CostEstimate(
            flops=flops // COST_PART, bytes_accessed=moved // COST_PART, transcendentals=0
        ),
        name=name,
    )(core, *operands, *after)


def whole(shape):
    return pl.BlockSpec(shape, lambda i, c: (0,) * len(shape))


def side_of(core_ref, side):
    return core_ref[0] if side == 0 else 1 - core_ref[0]


def halves(core_ref, side, up_ref, down_ref, up_out, down_out, sems, parts):
    half = up_out.shape[1]
    size = half // parts
    pairs = []
    for part in range(parts):
        begin = pl.multiple_of(side_of(core_ref, side) * half + part * size, size)
        here = pl.ds(part * size, size)
        pairs.append((
            pltpu.make_async_copy(up_ref.at[:, pl.ds(begin, size)], up_out.at[:, here], sems.at[0, part]),
            pltpu.make_async_copy(down_ref.at[pl.ds(begin, size)], down_out.at[here], sems.at[1, part]),
        ))
    return pairs


def half_outs(up):
    depth, half = up.shape[0], up.shape[1] // 2
    return [pltpu.VMEM((depth, half), BF16), pltpu.VMEM((half, depth), BF16)]


def bring(core, side, up, down):
    def body(core_ref, up_ref, down_ref, up_out, down_out, sems):
        pairs = halves(core_ref, side, up_ref, down_ref, up_out, down_out, sems, 1)
        for copy in pairs[0]:
            copy.start()
        for copy in pairs[0]:
            copy.wait()

    return call(
        body,
        core,
        [pltpu.with_memory_space_constraint(array, pltpu.HBM) for array in (up, down)],
        [pl.BlockSpec(memory_space=pltpu.HBM)] * 2,
        half_outs(up),
        [pl.BlockSpec(memory_space=pltpu.VMEM)] * 2,
        (1,),
        (0, 2 * up.size),
        "bring",
        (),
        [pltpu.SemaphoreType.DMA((2, 1))],
    )


def bring_and_sum(core, units, side, up, down, after=()):
    _, rows, depth = units[0].shape
    tokens = rows * len(units)
    half = up.shape[1] // 2
    parts = 3 if half % 384 == 0 else 1
    size = half // parts

    def body(core_ref, *refs):
        unit_refs = refs[: len(units)]
        up_ref, down_ref, out, up_out, down_out, acts, sems = refs[len(units) :]
        pairs = halves(core_ref, side, up_ref, down_ref, up_out, down_out, sems, parts)
        for pair in pairs:
            for copy in pair:
                copy.start()
        for n, ref in enumerate(unit_refs):
            acts[:, n * rows : (n + 1) * rows, :] = ref[...]
        for part, pair in enumerate(pairs):
            for copy in pair:
                copy.wait()
            here = slice(part * size, (part + 1) * size)
            out[0, :, here] = contract(acts[0], up_out[:, here], 1, 0)
            out[1, :, here] = contract(acts[1], down_out[here, :], 1, 1)

    return call(
        body,
        core,
        [*units] + [pltpu.with_memory_space_constraint(array, pltpu.HBM) for array in (up, down)],
        [whole(units[0].shape)] * len(units) + [pl.BlockSpec(memory_space=pltpu.HBM)] * 2,
        [jax.ShapeDtypeStruct((2, tokens, half), F32)] + half_outs(up),
        [whole((2, tokens, half))] + [pl.BlockSpec(memory_space=pltpu.VMEM)] * 2,
        (1,),
        (4 * tokens * depth * half, 2 * up.size),
        "bring_and_sum",
        after,
        [pltpu.VMEM((2, tokens, depth), BF16), pltpu.SemaphoreType.DMA((2, parts))],
    )


def partial_sums(core, units, up, down, side, apart, start, width, after=()):
    _, rows, depth = units[0].shape
    tokens = rows * len(units)
    tile = tile_of(width, 256)
    first = start // tile
    dtype = BF16 if side else F32

    def body(core_ref, *refs):
        *unit_refs, up_ref, down_ref = refs[: len(units) + 2]
        *out_refs, acts = refs[len(units) + 2 :]

        @pl.when(pl.program_id(0) == 0)
        def _():
            for n, ref in enumerate(unit_refs):
                acts[:, n * rows : (n + 1) * rows, :] = ref[...]

        preact = contract(acts[0], up_ref[...], 1, 0)
        grad_hidden = contract(acts[1], down_ref[...], 1, 1)
        if apart:
            out_refs[0][...] = preact.astype(dtype)
            out_refs[1][...] = grad_hidden.astype(dtype)
        else:
            out_refs[0][0] = preact.astype(dtype)
            out_refs[0][1] = grad_hidden.astype(dtype)

    if apart:
        outs = [jax.ShapeDtypeStruct((tokens, width), dtype)] * 2
        specs = [pl.BlockSpec((tokens, tile), lambda i, c: (0, i))] * 2
    else:
        outs = [jax.ShapeDtypeStruct((2, tokens, width), dtype)]
        specs = [pl.BlockSpec((2, tokens, tile), lambda i, c: (0, 0, i))]
    return call(
        body,
        core,
        [*units, up, down],
        [whole(units[0].shape)] * len(units)
        + [
            pl.BlockSpec((depth, tile), lambda i, c: (0, first + i)),
            pl.BlockSpec((tile, depth), lambda i, c: (first + i, 0)),
        ],
        outs,
        specs,
        (width // tile,),
        (4 * tokens * depth * width, 4 * depth * width),
        "sums_send" if side else "sums_keep",
        after,
        [pltpu.VMEM((2, tokens, depth), BF16)],
    )


def combine(core, keep, near, row, tokens, column, start, width, after):
    tile = tile_of(width, 256)
    both = pl.BlockSpec((2, tokens, tile), lambda i, c: (0, row // tokens, column // tile + i))
    one = pl.BlockSpec((tokens, tile), lambda i, c: (row // tokens, start // tile + i))

    def body(core_ref, keep_ref, preact_ref, grad_ref, chip_ref):
        chip_ref[0] = (keep_ref[0] + preact_ref[...].astype(F32)).astype(BF16)
        chip_ref[1] = (keep_ref[1] + grad_ref[...].astype(F32)).astype(BF16)

    return call(
        body,
        core,
        [keep, *near],
        [both, one, one],
        jax.ShapeDtypeStruct((2, tokens, width), BF16),
        pl.BlockSpec((2, tokens, tile), lambda i, c: (0, 0, i)),
        (width // tile,),
        (4 * tokens * width, 16 * tokens * width),
        "combine",
        after,
    )


def activations(core, keep, near, far, row, start, near_start, after=()):
    _, tokens, width = far.shape
    tile = tile_of(width, 256)
    first, near_first, block = start // tile, near_start // tile, row // tokens
    both = pl.BlockSpec((2, tokens, tile), lambda i, c: (0, block, first + i))
    both_here = pl.BlockSpec((2, tokens, tile), lambda i, c: (0, 0, i))
    one = pl.BlockSpec((tokens, tile), lambda i, c: (block, near_first + i))

    def body(core_ref, keep_ref, *refs):
        *near_refs, far_ref, act_ref = refs

        def total(which):
            part = near_refs[which][...].astype(F32)
            return keep_ref[which] + part + far_ref[which].astype(F32)

        preact = total(0)
        cdf = 0.5 + 0.5 * lax.erf(preact * (0.5**0.5))
        pdf = jnp.exp(-0.5 * preact * preact) * ((0.5 / math.pi) ** 0.5)
        act_ref[0] = (preact * cdf).astype(BF16)
        act_ref[1] = (total(1) * (cdf + preact * pdf)).astype(BF16)

    return call(
        body,
        core,
        [keep, *near, far],
        [both, one, one, both_here],
        jax.ShapeDtypeStruct(far.shape, BF16),
        both_here,
        (width // tile,),
        (60 * tokens * width, 20 * tokens * width),
        "activations",
        after,
    )


def back(core, acts, ups, start, width, before, row, order, leave, after=()):
    tokens = sum(which[0].shape[1] for which in acts)
    depth = ups[0].shape[0]
    tile = tile_of(depth, 512)
    groups = len(acts)

    def body(core_ref, *refs):
        part = None
        for side in range(2):
            mine = [ref[0] for ref in refs[side * groups : (side + 1) * groups]]
            mine = mine[0] if groups == 1 else jnp.concatenate(mine, axis=0)
            term = contract(mine, refs[2 * groups + side][:, start : start + width], 1, 1)
            part = term if part is None else part + term
        refs = refs[2 * groups + 2 :]
        if before is not None:
            part = part + refs[0][...]
        outs = refs[(before is not None) :]
        if leave is None:
            outs[0][...] = part
        else:
            rows = tokens // len(order)
            part = [part[n * rows : (n + 1) * rows] for n in order]
            outs[0][...] = jnp.concatenate(part[:leave], axis=0) if leave > 1 else part[0]
            outs[1][...] = jnp.concatenate(part[leave:], axis=0).astype(BF16)

    kinds = [(tokens, F32)]
    if leave is not None:
        rows = tokens // len(order)
        kinds = [(leave * rows, F32), (tokens - leave * rows, BF16)]
    operands = [which[side] for side in range(2) for which in acts]
    firsts = [which[2] // width for side in range(2) for which in acts]
    return call(
        body,
        core,
        [*operands, *ups] + ([] if before is None else [before]),
        [
            pl.BlockSpec((1, array.shape[1], width), lambda i, c, first=first: (1, 0, first))
            for array, first in zip(operands, firsts)
        ]
        + [pl.BlockSpec((tile, ups[0].shape[1]), lambda i, c: (i, 0))] * 2
        + ([] if before is None else [pl.BlockSpec((tokens, tile), lambda i, c: (row // tokens, i))]),
        [jax.ShapeDtypeStruct((rows, depth), dtype) for rows, dtype in kinds],
        [pl.BlockSpec((rows, tile), lambda i, c: (0, i)) for rows, _ in kinds],
        (depth // tile,),
        (4 * tokens * depth * width, 4 * depth * width + 4 * tokens * depth),
        "back",
        after,
    )


def fold(core, stay, near, dtype, after=()):
    rows, depth = stay.shape

    def body(core_ref, stay_ref, near_ref, out_ref):
        out_ref[...] = (stay_ref[...] + near_ref[...].astype(F32)).astype(dtype)

    return call(
        body,
        core,
        [stay, near],
        [whole(stay.shape)] * 2,
        jax.ShapeDtypeStruct(stay.shape, dtype),
        whole(stay.shape),
        (1,),
        (rows * depth, 8 * rows * depth),
        "fold",
        after,
    )


def arrange(core, units, after=()):
    _, rows, depth = units[0].shape
    tokens = rows * len(units)

    def body(core_ref, *refs):
        *unit_refs, inputs_t, cotan = refs
        inputs_t[...] = jnp.concatenate([ref[0] for ref in unit_refs], axis=0).T
        cotan[...] = jnp.concatenate([ref[1] for ref in unit_refs], axis=0)

    return call(
        body,
        core,
        units,
        [whole(units[0].shape)] * len(units),
        [jax.ShapeDtypeStruct((depth, tokens), BF16), jax.ShapeDtypeStruct((tokens, depth), BF16)],
        [whole((depth, tokens)), whole((tokens, depth))],
        (1,),
        (0, 8 * tokens * depth),
        "arrange",
        after,
    )


def weight_grads(core, inputs_t, cotan, sides, acts, start, width, shape, outputs, after=()):
    depth, full = shape
    tokens = cotan.shape[0]
    half = full // 2
    tile = tile_of(width, 256)
    steps = width // tile
    groups = len(acts[0])

    def body(core_ref, inputs_ref, cotan_ref, *refs):
        up_out, down_out, done = refs[-3:]
        done[...] = jnp.zeros_like(done)
        for order in range(len(sides)):
            mine = refs[order * groups : (order + 1) * groups]

            @pl.when(pl.program_id(0) // steps == order)
            def _(mine=mine):
                hidden = jnp.concatenate([ref[0] for ref in mine], axis=0)
                grad = jnp.concatenate([ref[1] for ref in mine], axis=0)
                up_out[...] = contract(inputs_ref[...], grad, 1, 0)
                down_out[...] = contract(hidden, cotan_ref[...], 0, 0)

    def place(i, c):
        which = side_of(c, sides[0])
        if len(sides) > 1:
            which = jnp.where(i // steps == 0, which, 1 - which)
        return which * (half // tile) + start // tile + i % steps

    operands = [inputs_t, cotan]
    specs = [whole(inputs_t.shape), whole(cotan.shape)]
    for order in range(len(sides)):
        for array, offset in acts[order]:

            def index(i, c, order=order, first=offset // tile):
                return (0, 0, first + jnp.clip(i - order * steps, 0, steps - 1))

            operands.append(array)
            specs.append(pl.BlockSpec((2, array.shape[1], tile), index))
    aliases = None
    if outputs is not None:
        aliases = {len(operands) + 1: 0, len(operands) + 2: 1}
        operands += list(outputs)
        specs += [pl.BlockSpec(memory_space=pl.ANY)] * 2
    many = width * len(sides)
    return call(
        body,
        core,
        operands,
        specs,
        [
            jax.ShapeDtypeStruct((depth, full), F32),
            jax.ShapeDtypeStruct((full, depth), F32),
            jax.ShapeDtypeStruct((8, 128), F32),
        ],
        [
            pl.BlockSpec((depth, tile), lambda i, c: (0, place(i, c))),
            pl.BlockSpec((tile, depth), lambda i, c: (place(i, c), 0)),
            whole((8, 128)),
        ],
        (steps * len(sides),),
        (4 * tokens * depth * many, 8 * depth * many),
        "weight_grads",
        after,
        aliases=aliases,
        limit=GRADS_VMEM_LIMIT,
    )


def swap(value, axis, size, bits):
    return lax.ppermute(value, axis, [(i, i ^ bits) for i in range(size)])


def cube_body(inputs, cotangent, up, down):
    rows = inputs.shape[0]
    half = up.shape[1] // 2
    width = half // 3 if half % 768 == 0 else half // 2
    spans = [(0, width), (width, half - width)]
    core = (lax.axis_index("gy") % 2).astype(jnp.int32).reshape(1)

    unit = {(0, 0): jnp.stack([inputs, cotangent])}
    unit[0, 1] = swap(unit[0, 0], "gx", 2, 1)
    unit[1, 0] = swap(unit[0, 0], "gz", 4, 1)
    z = lax.axis_index("gz")
    middle = (z == 1) | (z == 2)
    across, outward = [(1, 2), (2, 1)], [(1, 0), (2, 3)]
    first = lax.ppermute(unit[0, 0], "gz", across)
    ups, downs = {}, {}
    ups[1], downs[1] = bring(core, 1, up, down)
    second = lax.ppermute(unit[1, 0], "gz", across)
    first_on = lax.ppermute(first, "gz", outward)
    second_on = lax.ppermute(second, "gz", outward)
    unit[2, 0] = jnp.where(middle, second, first_on)
    unit[3, 0] = jnp.where(middle, first, second_on)
    for d in (1, 2, 3):
        unit[d, 1] = swap(unit[d, 0], "gx", 2, 1)
    groups = [
        [unit[0, 0], unit[0, 1]],
        [unit[1, 0], unit[1, 1]],
        [unit[2, 0], unit[2, 1], unit[3, 0], unit[3, 1]],
    ]

    pair = 2 * rows
    pieces = [
        (0, 0, pair, 0, half),
        (1, 0, pair, 0, half),
        (2, 0, 2 * pair, *spans[0]),
        (2, 0, pair, *spans[1]),
        (2, pair, pair, *spans[1]),
    ]
    near, keep, far, act, act_near = {}, {}, {}, {}, {}

    def send(group, after=()):
        out = partial_sums(
            core, groups[group], ups[1], downs[1], 1, True, 0, half, after
        )
        near[group] = [swap(array, "gy", 4, 1) for array in out]
        return [out[0]]

    def hold(group, start, size, after):
        if group:
            out, = partial_sums(
                core, groups[group], ups[0], downs[0], 0, False, start, size, after
            )
        else:
            out, ups[0], downs[0] = bring_and_sum(core, groups[group], 0, up, down, after)
        keep[group, start] = out
        return [out]

    def kept(group, start):
        return (keep[group, start], 0) if (group, start) in keep else (keep[group, 0], start)

    def cross(n, after=()):
        group, row, count, start, size = pieces[n]
        array, column = kept(group, start)
        if after:
            chip = combine(core, array, near[group], row, count, column, start, size, after)
        else:
            chip = jnp.stack([
                (
                    array[which, row : row + count, column : column + size]
                    + near[group][which][row : row + count, start : start + size].astype(F32)
                ).astype(BF16)
                for which in range(2)
            ])
        far[n] = swap(chip, "gy", 4, 2)
        return [chip]

    def ready(n, after):
        group, row, _, start, _ = pieces[n]
        array, column = kept(group, start)
        act[n] = activations(core, array, near[group], far[n], row, column, start, after)
        act_near[n] = swap(act[n], "gy", 4, 1)
        return [act[n]]

    def inward(which, start, size, part, row, order, leave, after):
        acts = [(act[n], act_near[n], offset) for n, offset in which]
        return back(core, acts, (ups[0], ups[1]), start, size, part, row, order, leave, after)

    outputs = None

    def gradients(j, sides, after):
        acts = [
            [(array[n], spans[j][0]) for n in range(2)]
            + ([(array[3], 0), (array[4], 0)] if j else [(array[2], 0)])
            for array in (act, act_near)
        ]
        acts = [acts[side] for side in sides]
        return weight_grads(
            core, inputs_t, cotan, sides, acts, *spans[j], up.shape, outputs, after
        )

    def finish(j, sides, after):
        nonlocal outputs
        *outputs, done = gradients(j, sides, after)
        return [done]

    last = send(0)
    last = hold(0, 0, half, last)
    last = cross(0, [*last, unit[1, 1]])
    last = send(1, [*last, first_on, second])
    last = hold(1, 0, half, [*last, second_on])
    last = ready(0, [*last, unit[2, 1]])
    last = cross(1, last)
    last = send(2, last)
    last = hold(2, 0, half, last)
    last = ready(1, last)
    last = cross(2) + last
    inputs_t, cotan = arrange(core, [u for group in groups for u in group], last)
    stay1, go1 = inward(((0, 0), (1, 0)), 0, half, None, 0, (0, 2, 1, 3), 2, [inputs_t])
    near1 = swap(go1, "gx", 2, 1)

    last = ready(2, [stay1])
    last = cross(3, last)
    last = finish(0, (0,), last)
    total = fold(core, stay1[:rows], near1[:rows], F32, last)
    back1 = fold(core, stay1[rows:], near1[rows:], BF16, [total])
    far1 = swap(back1, "gz", 4, 1)
    part, = inward(((2, 0),), *spans[0], None, 0, None, None, [back1])
    last = ready(3, [part])
    last = cross(4, last)
    last = finish(0, (1,), last)
    stay2, go2 = inward(((3, 0),), *spans[1], part, 0, (0, 1), 1, last)
    near2 = swap(go2, "gx", 2, 1)
    total = fold(core, total, far1, F32, [stay2])
    last = ready(4, [total])
    stay3, go3 = inward(((4, 0),), *spans[1], part, pair, (0, 1), 1, last)
    near3 = swap(go3, "gx", 2, 1)
    back2 = fold(core, stay2, near2, BF16, [stay3])
    far2 = swap(back2, "gz", 4, 2)
    last = finish(1, (0,), [back2])
    back3 = fold(core, stay3, near3, BF16, last)
    far3 = swap(back3, "gz", 4, 3)
    finish(1, (1,), [back3])
    total = total + far2.astype(F32) + far3.astype(F32)
    return (total.astype(BF16), *outputs)


def solution(mesh):
    placed = (
        P(("gx", "gz"), "gy"),
        P(("gx", "gz"), "gy"),
        P("gy", ("gz", "gx")),
        P(("gz", "gx"), "gy"),
    )
    cube = tuple(mesh.shape[axis] for axis in ("gx", "gy", "gz")) == (2, 4, 4)
    return jax.shard_map(
        cube_body if cube else general_body,
        mesh=mesh,
        in_specs=placed,
        out_specs=(P(("gx", "gz"), "gy"), P("gy", ("gz", "gx")), P(("gz", "gx"), "gy")),
        check_vma=False,
    )
```

```python
import math

import jax
import jax.numpy as jnp
from jax import lax
from jax.experimental import pallas as pl
from jax.experimental.pallas import tpu as pltpu
from jax.sharding import PartitionSpec as P

F32 = jnp.float32
BF16 = jnp.bfloat16
VMEM_LIMIT = 10 * 1024 * 1024
GRADS_VMEM_LIMIT = 18 * 1024 * 1024
COST_PART = 1


def gelu_exact(value):
    return jax.nn.gelu(value, approximate=False)


def activate(preact, grad_hidden):
    activated, pullback = jax.vjp(gelu_exact, preact)
    grad_preact = pullback(grad_hidden)[0]
    return (activated.astype(BF16), grad_preact.astype(BF16))


def contract(left, right, left_dim, right_dim):
    return lax.dot_general(
        left, right, (((left_dim,), (right_dim,)), ((), ())), preferred_element_type=F32
    )


def general_body(inputs, cotangent, up_weight, down_weight):
    all_inputs = lax.all_gather(inputs, ("gx", "gz"), axis=0, tiled=True)
    all_cotan = lax.all_gather(cotangent, ("gx", "gz"), axis=0, tiled=True)
    preact = lax.psum_scatter(
        contract(all_inputs, up_weight, 1, 0), "gy", scatter_dimension=0, tiled=True
    )
    grad_hidden = lax.psum_scatter(
        contract(all_cotan, down_weight, 1, 1), "gy", scatter_dimension=0, tiled=True
    )
    hidden, grad_preact = activate(preact, grad_hidden)
    hidden = lax.all_gather(hidden, "gy", axis=0, tiled=True)
    grad_preact = lax.all_gather(grad_preact, "gy", axis=0, tiled=True)
    grad_down = contract(hidden, all_cotan, 0, 0)
    grad_up = contract(all_inputs, grad_preact, 0, 0)
    grad_inputs = lax.psum_scatter(
        contract(grad_preact, up_weight, 1, 1), ("gx", "gz"), scatter_dimension=0, tiled=True
    ).astype(BF16)
    return (grad_inputs, grad_up, grad_down)


def tile_of(width, most):
    tile = most
    while width % tile:
        tile //= 2
    return tile


def call(body, core, operands, in_specs, outs, out_specs, grid, cost, name, after=(), scratch=(), aliases=None, limit=VMEM_LIMIT):
    after = list(after)
    inner = len(operands) + 1

    def kernel(*refs):
        body(*refs[:inner], *refs[inner + len(after) :])

    flops, moved = cost
    return pl.pallas_call(
        kernel,
        grid_spec=pltpu.PrefetchScalarGridSpec(
            num_scalar_prefetch=1,
            grid=grid,
            in_specs=list(in_specs) + [pl.BlockSpec(memory_space=pl.ANY)] * len(after),
            out_specs=out_specs,
            scratch_shapes=list(scratch),
        ),
        out_shape=outs,
        input_output_aliases=aliases or {},
        compiler_params=pltpu.CompilerParams(vmem_limit_bytes=limit),
        cost_estimate=pl.CostEstimate(
            flops=flops // COST_PART, bytes_accessed=moved // COST_PART, transcendentals=0
        ),
        name=name,
    )(core, *operands, *after)


def whole(shape):
    return pl.BlockSpec(shape, lambda i, c: (0,) * len(shape))


def side_of(core_ref, side):
    return core_ref[0] if side == 0 else 1 - core_ref[0]


def halves(core_ref, side, up_ref, down_ref, up_out, down_out, sems, parts):
    half = up_out.shape[1]
    size = half // parts
    pairs = []
    for part in range(parts):
        begin = pl.multiple_of(side_of(core_ref, side) * half + part * size, size)
        here = pl.ds(part * size, size)
        pairs.append((
            pltpu.make_async_copy(up_ref.at[:, pl.ds(begin, size)], up_out.at[:, here], sems.at[0, part]),
            pltpu.make_async_copy(down_ref.at[pl.ds(begin, size)], down_out.at[here], sems.at[1, part]),
        ))
    return pairs


def half_outs(up):
    depth, half = up.shape[0], up.shape[1] // 2
    return [pltpu.VMEM((depth, half), BF16), pltpu.VMEM((half, depth), BF16)]


def bring(core, side, up, down):
    def body(core_ref, up_ref, down_ref, up_out, down_out, sems):
        pairs = halves(core_ref, side, up_ref, down_ref, up_out, down_out, sems, 1)
        for copy in pairs[0]:
            copy.start()
        for copy in pairs[0]:
            copy.wait()

    return call(
        body,
        core,
        [pltpu.with_memory_space_constraint(array, pltpu.HBM) for array in (up, down)],
        [pl.BlockSpec(memory_space=pltpu.HBM)] * 2,
        half_outs(up),
        [pl.BlockSpec(memory_space=pltpu.VMEM)] * 2,
        (1,),
        (0, 2 * up.size),
        "bring",
        (),
        [pltpu.SemaphoreType.DMA((2, 1))],
    )


def bring_and_sum(core, units, side, up, down, after=()):
    _, rows, depth = units[0].shape
    tokens = rows * len(units)
    half = up.shape[1] // 2
    parts = 3 if half % 384 == 0 else 1
    size = half // parts

    def body(core_ref, *refs):
        unit_refs = refs[: len(units)]
        up_ref, down_ref, out, up_out, down_out, acts, sems = refs[len(units) :]
        pairs = halves(core_ref, side, up_ref, down_ref, up_out, down_out, sems, parts)
        for pair in pairs:
            for copy in pair:
                copy.start()
        for n, ref in enumerate(unit_refs):
            acts[:, n * rows : (n + 1) * rows, :] = ref[...]
        for part, pair in enumerate(pairs):
            for copy in pair:
                copy.wait()
            here = slice(part * size, (part + 1) * size)
            out[0, :, here] = contract(acts[0], up_out[:, here], 1, 0)
            out[1, :, here] = contract(acts[1], down_out[here, :], 1, 1)

    return call(
        body,
        core,
        [*units] + [pltpu.with_memory_space_constraint(array, pltpu.HBM) for array in (up, down)],
        [whole(units[0].shape)] * len(units) + [pl.BlockSpec(memory_space=pltpu.HBM)] * 2,
        [jax.ShapeDtypeStruct((2, tokens, half), F32)] + half_outs(up),
        [whole((2, tokens, half))] + [pl.BlockSpec(memory_space=pltpu.VMEM)] * 2,
        (1,),
        (4 * tokens * depth * half, 2 * up.size),
        "bring_and_sum",
        after,
        [pltpu.VMEM((2, tokens, depth), BF16), pltpu.SemaphoreType.DMA((2, parts))],
    )


def partial_sums(core, units, up, down, side, apart, start, width, after=()):
    _, rows, depth = units[0].shape
    tokens = rows * len(units)
    tile = tile_of(width, 256)
    first = start // tile
    dtype = BF16 if side else F32

    def body(core_ref, *refs):
        *unit_refs, up_ref, down_ref = refs[: len(units) + 2]
        *out_refs, acts = refs[len(units) + 2 :]

        @pl.when(pl.program_id(0) == 0)
        def _():
            for n, ref in enumerate(unit_refs):
                acts[:, n * rows : (n + 1) * rows, :] = ref[...]

        preact = contract(acts[0], up_ref[...], 1, 0)
        grad_hidden = contract(acts[1], down_ref[...], 1, 1)
        if apart:
            out_refs[0][...] = preact.astype(dtype)
            out_refs[1][...] = grad_hidden.astype(dtype)
        else:
            out_refs[0][0] = preact.astype(dtype)
            out_refs[0][1] = grad_hidden.astype(dtype)

    if apart:
        outs = [jax.ShapeDtypeStruct((tokens, width), dtype)] * 2
        specs = [pl.BlockSpec((tokens, tile), lambda i, c: (0, i))] * 2
    else:
        outs = [jax.ShapeDtypeStruct((2, tokens, width), dtype)]
        specs = [pl.BlockSpec((2, tokens, tile), lambda i, c: (0, 0, i))]
    return call(
        body,
        core,
        [*units, up, down],
        [whole(units[0].shape)] * len(units)
        + [
            pl.BlockSpec((depth, tile), lambda i, c: (0, first + i)),
            pl.BlockSpec((tile, depth), lambda i, c: (first + i, 0)),
        ],
        outs,
        specs,
        (width // tile,),
        (4 * tokens * depth * width, 4 * depth * width),
        "sums_send" if side else "sums_keep",
        after,
        [pltpu.VMEM((2, tokens, depth), BF16)],
    )


def combine(core, keep, near, row, tokens, column, start, width, after):
    tile = tile_of(width, 256)
    both = pl.BlockSpec((2, tokens, tile), lambda i, c: (0, row // tokens, column // tile + i))
    one = pl.BlockSpec((tokens, tile), lambda i, c: (row // tokens, start // tile + i))

    def body(core_ref, keep_ref, preact_ref, grad_ref, chip_ref):
        chip_ref[0] = (keep_ref[0] + preact_ref[...].astype(F32)).astype(BF16)
        chip_ref[1] = (keep_ref[1] + grad_ref[...].astype(F32)).astype(BF16)

    return call(
        body,
        core,
        [keep, *near],
        [both, one, one],
        jax.ShapeDtypeStruct((2, tokens, width), BF16),
        pl.BlockSpec((2, tokens, tile), lambda i, c: (0, 0, i)),
        (width // tile,),
        (4 * tokens * width, 16 * tokens * width),
        "combine",
        after,
    )


def activations(core, keep, near, far, row, start, near_start, after=()):
    _, tokens, width = far.shape
    tile = tile_of(width, 256)
    first, near_first, block = start // tile, near_start // tile, row // tokens
    both = pl.BlockSpec((2, tokens, tile), lambda i, c: (0, block, first + i))
    both_here = pl.BlockSpec((2, tokens, tile), lambda i, c: (0, 0, i))
    one = pl.BlockSpec((tokens, tile), lambda i, c: (block, near_first + i))

    def body(core_ref, keep_ref, *refs):
        *near_refs, far_ref, act_ref = refs

        def total(which):
            part = near_refs[which][...].astype(F32)
            return keep_ref[which] + part + far_ref[which].astype(F32)

        preact = total(0)
        cdf = 0.5 + 0.5 * lax.erf(preact * (0.5**0.5))
        pdf = jnp.exp(-0.5 * preact * preact) * ((0.5 / math.pi) ** 0.5)
        act_ref[0] = (preact * cdf).astype(BF16)
        act_ref[1] = (total(1) * (cdf + preact * pdf)).astype(BF16)

    return call(
        body,
        core,
        [keep, *near, far],
        [both, one, one, both_here],
        jax.ShapeDtypeStruct(far.shape, BF16),
        both_here,
        (width // tile,),
        (60 * tokens * width, 20 * tokens * width),
        "activations",
        after,
    )


def back(core, acts, ups, start, width, before, row, order, leave, after=()):
    tokens = sum(which[0].shape[1] for which in acts)
    depth = ups[0].shape[0]
    tile = tile_of(depth, 512)
    groups = len(acts)

    def body(core_ref, *refs):
        part = None
        for side in range(2):
            mine = [ref[0] for ref in refs[side * groups : (side + 1) * groups]]
            mine = mine[0] if groups == 1 else jnp.concatenate(mine, axis=0)
            term = contract(mine, refs[2 * groups + side][:, start : start + width], 1, 1)
            part = term if part is None else part + term
        refs = refs[2 * groups + 2 :]
        if before is not None:
            part = part + refs[0][...]
        outs = refs[(before is not None) :]
        if leave is None:
            outs[0][...] = part
        else:
            rows = tokens // len(order)
            part = [part[n * rows : (n + 1) * rows] for n in order]
            outs[0][...] = jnp.concatenate(part[:leave], axis=0) if leave > 1 else part[0]
            outs[1][...] = jnp.concatenate(part[leave:], axis=0).astype(BF16)

    kinds = [(tokens, F32)]
    if leave is not None:
        rows = tokens // len(order)
        kinds = [(leave * rows, F32), (tokens - leave * rows, BF16)]
    operands = [which[side] for side in range(2) for which in acts]
    firsts = [which[2] // width for side in range(2) for which in acts]
    return call(
        body,
        core,
        [*operands, *ups] + ([] if before is None else [before]),
        [
            pl.BlockSpec((1, array.shape[1], width), lambda i, c, first=first: (1, 0, first))
            for array, first in zip(operands, firsts)
        ]
        + [pl.BlockSpec((tile, ups[0].shape[1]), lambda i, c: (i, 0))] * 2
        + ([] if before is None else [pl.BlockSpec((tokens, tile), lambda i, c: (row // tokens, i))]),
        [jax.ShapeDtypeStruct((rows, depth), dtype) for rows, dtype in kinds],
        [pl.BlockSpec((rows, tile), lambda i, c: (0, i)) for rows, _ in kinds],
        (depth // tile,),
        (4 * tokens * depth * width, 4 * depth * width + 4 * tokens * depth),
        "back",
        after,
    )


def fold(core, stay, near, dtype, after=()):
    rows, depth = stay.shape

    def body(core_ref, stay_ref, near_ref, out_ref):
        out_ref[...] = (stay_ref[...] + near_ref[...].astype(F32)).astype(dtype)

    return call(
        body,
        core,
        [stay, near],
        [whole(stay.shape)] * 2,
        jax.ShapeDtypeStruct(stay.shape, dtype),
        whole(stay.shape),
        (1,),
        (rows * depth, 8 * rows * depth),
        "fold",
        after,
    )


def arrange(core, units, after=()):
    _, rows, depth = units[0].shape
    tokens = rows * len(units)

    def body(core_ref, *refs):
        *unit_refs, inputs_t, cotan = refs
        inputs_t[...] = jnp.concatenate([ref[0] for ref in unit_refs], axis=0).T
        cotan[...] = jnp.concatenate([ref[1] for ref in unit_refs], axis=0)

    return call(
        body,
        core,
        units,
        [whole(units[0].shape)] * len(units),
        [jax.ShapeDtypeStruct((depth, tokens), BF16), jax.ShapeDtypeStruct((tokens, depth), BF16)],
        [whole((depth, tokens)), whole((tokens, depth))],
        (1,),
        (0, 8 * tokens * depth),
        "arrange",
        after,
    )


def weight_grads(core, inputs_t, cotan, sides, acts, start, width, shape, outputs, after=()):
    depth, full = shape
    tokens = cotan.shape[0]
    half = full // 2
    tile = tile_of(width, 256)
    steps = width // tile
    groups = len(acts[0])

    def body(core_ref, inputs_ref, cotan_ref, *refs):
        up_out, down_out, done = refs[-3:]
        done[...] = jnp.zeros_like(done)
        for order in range(len(sides)):
            mine = refs[order * groups : (order + 1) * groups]

            @pl.when(pl.program_id(0) // steps == order)
            def _(mine=mine):
                hidden = jnp.concatenate([ref[0] for ref in mine], axis=0)
                grad = jnp.concatenate([ref[1] for ref in mine], axis=0)
                up_out[...] = contract(inputs_ref[...], grad, 1, 0)
                down_out[...] = contract(hidden, cotan_ref[...], 0, 0)

    def place(i, c):
        which = side_of(c, sides[0])
        if len(sides) > 1:
            which = jnp.where(i // steps == 0, which, 1 - which)
        return which * (half // tile) + start // tile + i % steps

    operands = [inputs_t, cotan]
    specs = [whole(inputs_t.shape), whole(cotan.shape)]
    for order in range(len(sides)):
        for array, offset in acts[order]:

            def index(i, c, order=order, first=offset // tile):
                return (0, 0, first + jnp.clip(i - order * steps, 0, steps - 1))

            operands.append(array)
            specs.append(pl.BlockSpec((2, array.shape[1], tile), index))
    aliases = None
    if outputs is not None:
        aliases = {len(operands) + 1: 0, len(operands) + 2: 1}
        operands += list(outputs)
        specs += [pl.BlockSpec(memory_space=pl.ANY)] * 2
    many = width * len(sides)
    return call(
        body,
        core,
        operands,
        specs,
        [
            jax.ShapeDtypeStruct((depth, full), F32),
            jax.ShapeDtypeStruct((full, depth), F32),
            jax.ShapeDtypeStruct((8, 128), F32),
        ],
        [
            pl.BlockSpec((depth, tile), lambda i, c: (0, place(i, c))),
            pl.BlockSpec((tile, depth), lambda i, c: (place(i, c), 0)),
            whole((8, 128)),
        ],
        (steps * len(sides),),
        (4 * tokens * depth * many, 8 * depth * many),
        "weight_grads",
        after,
        aliases=aliases,
        limit=GRADS_VMEM_LIMIT,
    )


def swap(value, axis, size, bits):
    return lax.ppermute(value, axis, [(i, i ^ bits) for i in range(size)])


def cube_body(inputs, cotangent, up, down):
    rows = inputs.shape[0]
    half = up.shape[1] // 2
    width = half // 3 if half % 768 == 0 else half // 2
    spans = [(0, width), (width, half - width)]
    core = (lax.axis_index("gy") % 2).astype(jnp.int32).reshape(1)

    unit = {(0, 0): jnp.stack([inputs, cotangent])}
    unit[0, 1] = swap(unit[0, 0], "gx", 2, 1)
    unit[1, 0] = swap(unit[0, 0], "gz", 4, 1)
    z = lax.axis_index("gz")
    middle = (z == 1) | (z == 2)
    across, outward = [(1, 2), (2, 1)], [(1, 0), (2, 3)]
    first = lax.ppermute(unit[0, 0], "gz", across)
    ups, downs = {}, {}
    ups[1], downs[1] = bring(core, 1, up, down)
    second = lax.ppermute(unit[1, 0], "gz", across)
    first_on = lax.ppermute(first, "gz", outward)
    second_on = lax.ppermute(second, "gz", outward)
    unit[2, 0] = jnp.where(middle, second, first_on)
    unit[3, 0] = jnp.where(middle, first, second_on)
    for d in (1, 2, 3):
        unit[d, 1] = swap(unit[d, 0], "gx", 2, 1)
    groups = [
        [unit[0, 0], unit[0, 1]],
        [unit[1, 0], unit[1, 1]],
        [unit[2, 0], unit[2, 1], unit[3, 0], unit[3, 1]],
    ]

    pair = 2 * rows
    pieces = [
        (0, 0, pair, 0, half),
        (1, 0, pair, 0, half),
        (2, 0, 2 * pair, *spans[0]),
        (2, 0, pair, *spans[1]),
        (2, pair, pair, *spans[1]),
    ]
    near, keep, far, act, act_near = {}, {}, {}, {}, {}

    def send(group, after=()):
        out = partial_sums(
            core, groups[group], ups[1], downs[1], 1, True, 0, half, after
        )
        near[group] = [swap(array, "gy", 4, 1) for array in out]
        return [out[0]]

    def hold(group, start, size, after):
        if group:
            out, = partial_sums(
                core, groups[group], ups[0], downs[0], 0, False, start, size, after
            )
        else:
            out, ups[0], downs[0] = bring_and_sum(core, groups[group], 0, up, down, after)
        keep[group, start] = out
        return [out]

    def kept(group, start):
        return (keep[group, start], 0) if (group, start) in keep else (keep[group, 0], start)

    def cross(n, after=()):
        group, row, count, start, size = pieces[n]
        array, column = kept(group, start)
        if after:
            chip = combine(core, array, near[group], row, count, column, start, size, after)
        else:
            chip = jnp.stack([
                (
                    array[which, row : row + count, column : column + size]
                    + near[group][which][row : row + count, start : start + size].astype(F32)
                ).astype(BF16)
                for which in range(2)
            ])
        far[n] = swap(chip, "gy", 4, 2)
        return [chip]

    def ready(n, after):
        group, row, _, start, _ = pieces[n]
        array, column = kept(group, start)
        act[n] = activations(core, array, near[group], far[n], row, column, start, after)
        act_near[n] = swap(act[n], "gy", 4, 1)
        return [act[n]]

    def inward(which, start, size, part, row, order, leave, after):
        acts = [(act[n], act_near[n], offset) for n, offset in which]
        return back(core, acts, (ups[0], ups[1]), start, size, part, row, order, leave, after)

    outputs = None

    def gradients(j, sides, after):
        acts = [
            [(array[n], spans[j][0]) for n in range(2)]
            + ([(array[3], 0), (array[4], 0)] if j else [(array[2], 0)])
            for array in (act, act_near)
        ]
        acts = [acts[side] for side in sides]
        return weight_grads(
            core, inputs_t, cotan, sides, acts, *spans[j], up.shape, outputs, after
        )

    def finish(j, sides, after):
        nonlocal outputs
        *outputs, done = gradients(j, sides, after)
        return [done]

    last = send(0)
    last = hold(0, 0, half, last)
    last = cross(0, [*last, unit[1, 1]])
    last = send(1, [*last, first_on, second])
    last = hold(1, 0, half, [*last, second_on])
    last = ready(0, [*last, unit[2, 1]])
    last = cross(1, last)
    last = send(2, last)
    last = hold(2, 0, half, last)
    last = ready(1, last)
    last = cross(2) + last
    inputs_t, cotan = arrange(core, [u for group in groups for u in group], last)
    stay1, go1 = inward(((0, 0), (1, 0)), 0, half, None, 0, (0, 2, 1, 3), 2, [inputs_t])
    near1 = swap(go1, "gx", 2, 1)

    last = ready(2, [stay1])
    last = cross(3, last)
    last = finish(0, (0,), last)
    total = fold(core, stay1[:rows], near1[:rows], F32, last)
    back1 = fold(core, stay1[rows:], near1[rows:], BF16, [total])
    far1 = swap(back1, "gz", 4, 1)
    part, = inward(((2, 0),), *spans[0], None, 0, None, None, [back1])
    last = cross(4, [part])
    last = finish(0, (1,), last)
    last = ready(3, last)
    stay2, go2 = inward(((3, 0),), *spans[1], part, 0, (0, 1), 1, last)
    near2 = swap(go2, "gx", 2, 1)
    total = fold(core, total, far1, F32, [stay2])
    last = ready(4, [total])
    stay3, go3 = inward(((4, 0),), *spans[1], part, pair, (0, 1), 1, last)
    near3 = swap(go3, "gx", 2, 1)
    back2 = fold(core, stay2, near2, BF16, [stay3])
    far2 = swap(back2, "gz", 4, 2)
    last = finish(1, (0,), [back2])
    back3 = fold(core, stay3, near3, BF16, last)
    far3 = swap(back3, "gz", 4, 3)
    finish(1, (1,), [back3])
    total = total + far2.astype(F32) + far3.astype(F32)
    return (total.astype(BF16), *outputs)


def solution(mesh):
    placed = (
        P(("gx", "gz"), "gy"),
        P(("gx", "gz"), "gy"),
        P("gy", ("gz", "gx")),
        P(("gz", "gx"), "gy"),
    )
    cube = tuple(mesh.shape[axis] for axis in ("gx", "gy", "gz")) == (2, 4, 4)
    return jax.shard_map(
        cube_body if cube else general_body,
        mesh=mesh,
        in_specs=placed,
        out_specs=(P(("gx", "gz"), "gy"), P("gy", ("gz", "gx")), P(("gz", "gx"), "gy")),
        check_vma=False,
    )
```

```python
import math

import jax
import jax.numpy as jnp
from jax import lax
from jax.experimental import pallas as pl
from jax.experimental.pallas import tpu as pltpu
from jax.sharding import PartitionSpec as P

F32 = jnp.float32
BF16 = jnp.bfloat16
VMEM_LIMIT = 10 * 1024 * 1024
GRADS_VMEM_LIMIT = 18 * 1024 * 1024
COST_PART = 1


def gelu_exact(value):
    return jax.nn.gelu(value, approximate=False)


def activate(preact, grad_hidden):
    activated, pullback = jax.vjp(gelu_exact, preact)
    grad_preact = pullback(grad_hidden)[0]
    return (activated.astype(BF16), grad_preact.astype(BF16))


def contract(left, right, left_dim, right_dim):
    return lax.dot_general(
        left, right, (((left_dim,), (right_dim,)), ((), ())), preferred_element_type=F32
    )


def general_body(inputs, cotangent, up_weight, down_weight):
    all_inputs = lax.all_gather(inputs, ("gx", "gz"), axis=0, tiled=True)
    all_cotan = lax.all_gather(cotangent, ("gx", "gz"), axis=0, tiled=True)
    preact = lax.psum_scatter(
        contract(all_inputs, up_weight, 1, 0), "gy", scatter_dimension=0, tiled=True
    )
    grad_hidden = lax.psum_scatter(
        contract(all_cotan, down_weight, 1, 1), "gy", scatter_dimension=0, tiled=True
    )
    hidden, grad_preact = activate(preact, grad_hidden)
    hidden = lax.all_gather(hidden, "gy", axis=0, tiled=True)
    grad_preact = lax.all_gather(grad_preact, "gy", axis=0, tiled=True)
    grad_down = contract(hidden, all_cotan, 0, 0)
    grad_up = contract(all_inputs, grad_preact, 0, 0)
    grad_inputs = lax.psum_scatter(
        contract(grad_preact, up_weight, 1, 1), ("gx", "gz"), scatter_dimension=0, tiled=True
    ).astype(BF16)
    return (grad_inputs, grad_up, grad_down)


def tile_of(width, most):
    tile = most
    while width % tile:
        tile //= 2
    return tile


def call(body, core, operands, in_specs, outs, out_specs, grid, cost, name, after=(), scratch=(), aliases=None, limit=VMEM_LIMIT):
    after = list(after)
    inner = len(operands) + 1

    def kernel(*refs):
        body(*refs[:inner], *refs[inner + len(after) :])

    flops, moved = cost
    return pl.pallas_call(
        kernel,
        grid_spec=pltpu.PrefetchScalarGridSpec(
            num_scalar_prefetch=1,
            grid=grid,
            in_specs=list(in_specs) + [pl.BlockSpec(memory_space=pl.ANY)] * len(after),
            out_specs=out_specs,
            scratch_shapes=list(scratch),
        ),
        out_shape=outs,
        input_output_aliases=aliases or {},
        compiler_params=pltpu.CompilerParams(vmem_limit_bytes=limit),
        cost_estimate=pl.CostEstimate(
            flops=flops // COST_PART, bytes_accessed=moved // COST_PART, transcendentals=0
        ),
        name=name,
    )(core, *operands, *after)


def whole(shape):
    return pl.BlockSpec(shape, lambda i, c: (0,) * len(shape))


def side_of(core_ref, side):
    return core_ref[0] if side == 0 else 1 - core_ref[0]


def halves(core_ref, side, up_ref, down_ref, up_out, down_out, sems, parts):
    half = up_out.shape[1]
    size = half // parts
    pairs = []
    for part in range(parts):
        begin = pl.multiple_of(side_of(core_ref, side) * half + part * size, size)
        here = pl.ds(part * size, size)
        pairs.append((
            pltpu.make_async_copy(up_ref.at[:, pl.ds(begin, size)], up_out.at[:, here], sems.at[0, part]),
            pltpu.make_async_copy(down_ref.at[pl.ds(begin, size)], down_out.at[here], sems.at[1, part]),
        ))
    return pairs


def half_outs(up):
    depth, half = up.shape[0], up.shape[1] // 2
    return [pltpu.VMEM((depth, half), BF16), pltpu.VMEM((half, depth), BF16)]


def bring_and_sum(core, units, side, up, down, after=()):
    _, rows, depth = units[0].shape
    tokens = rows * len(units)
    half = up.shape[1] // 2
    parts = 3 if half % 384 == 0 else 1
    size = half // parts
    if side:
        kinds = [jax.ShapeDtypeStruct((tokens, half), BF16)] * 2
    else:
        kinds = [jax.ShapeDtypeStruct((2, tokens, half), F32)]

    def body(core_ref, *refs):
        unit_refs = refs[: len(units)]
        up_ref, down_ref, *outs, up_out, down_out, acts, sems = refs[len(units) :]
        pairs = halves(core_ref, side, up_ref, down_ref, up_out, down_out, sems, parts)
        for pair in pairs:
            for copy in pair:
                copy.start()
        for n, ref in enumerate(unit_refs):
            acts[:, n * rows : (n + 1) * rows, :] = ref[...]
        for part, pair in enumerate(pairs):
            for copy in pair:
                copy.wait()
            here = slice(part * size, (part + 1) * size)
            preact = contract(acts[0], up_out[:, here], 1, 0)
            grad_hidden = contract(acts[1], down_out[here, :], 1, 1)
            if side:
                outs[0][:, here] = preact.astype(BF16)
                outs[1][:, here] = grad_hidden.astype(BF16)
            else:
                outs[0][0, :, here] = preact
                outs[0][1, :, here] = grad_hidden

    return call(
        body,
        core,
        [*units] + [pltpu.with_memory_space_constraint(array, pltpu.HBM) for array in (up, down)],
        [whole(units[0].shape)] * len(units) + [pl.BlockSpec(memory_space=pltpu.HBM)] * 2,
        kinds + half_outs(up),
        [whole(kind.shape) for kind in kinds] + [pl.BlockSpec(memory_space=pltpu.VMEM)] * 2,
        (1,),
        (4 * tokens * depth * half, 2 * up.size),
        "bring_and_sum",
        after,
        [pltpu.VMEM((2, tokens, depth), BF16), pltpu.SemaphoreType.DMA((2, parts))],
    )


def partial_sums(core, units, up, down, side, apart, start, width, after=()):
    _, rows, depth = units[0].shape
    tokens = rows * len(units)
    tile = tile_of(width, 256)
    first = start // tile
    dtype = BF16 if side else F32

    def body(core_ref, *refs):
        *unit_refs, up_ref, down_ref = refs[: len(units) + 2]
        *out_refs, acts = refs[len(units) + 2 :]

        @pl.when(pl.program_id(0) == 0)
        def _():
            for n, ref in enumerate(unit_refs):
                acts[:, n * rows : (n + 1) * rows, :] = ref[...]

        preact = contract(acts[0], up_ref[...], 1, 0)
        grad_hidden = contract(acts[1], down_ref[...], 1, 1)
        if apart:
            out_refs[0][...] = preact.astype(dtype)
            out_refs[1][...] = grad_hidden.astype(dtype)
        else:
            out_refs[0][0] = preact.astype(dtype)
            out_refs[0][1] = grad_hidden.astype(dtype)

    if apart:
        outs = [jax.ShapeDtypeStruct((tokens, width), dtype)] * 2
        specs = [pl.BlockSpec((tokens, tile), lambda i, c: (0, i))] * 2
    else:
        outs = [jax.ShapeDtypeStruct((2, tokens, width), dtype)]
        specs = [pl.BlockSpec((2, tokens, tile), lambda i, c: (0, 0, i))]
    return call(
        body,
        core,
        [*units, up, down],
        [whole(units[0].shape)] * len(units)
        + [
            pl.BlockSpec((depth, tile), lambda i, c: (0, first + i)),
            pl.BlockSpec((tile, depth), lambda i, c: (first + i, 0)),
        ],
        outs,
        specs,
        (width // tile,),
        (4 * tokens * depth * width, 4 * depth * width),
        "sums_send" if side else "sums_keep",
        after,
        [pltpu.VMEM((2, tokens, depth), BF16)],
    )


def combine(core, keep, near, row, tokens, column, start, width, after):
    tile = tile_of(width, 256)
    both = pl.BlockSpec((2, tokens, tile), lambda i, c: (0, row // tokens, column // tile + i))
    one = pl.BlockSpec((tokens, tile), lambda i, c: (row // tokens, start // tile + i))

    def body(core_ref, keep_ref, preact_ref, grad_ref, chip_ref):
        chip_ref[0] = (keep_ref[0] + preact_ref[...].astype(F32)).astype(BF16)
        chip_ref[1] = (keep_ref[1] + grad_ref[...].astype(F32)).astype(BF16)

    return call(
        body,
        core,
        [keep, *near],
        [both, one, one],
        jax.ShapeDtypeStruct((2, tokens, width), BF16),
        pl.BlockSpec((2, tokens, tile), lambda i, c: (0, 0, i)),
        (width // tile,),
        (4 * tokens * width, 16 * tokens * width),
        "combine",
        after,
    )


def activations(core, keep, near, far, row, start, near_start, after=()):
    _, tokens, width = far.shape
    tile = tile_of(width, 256)
    first, near_first, block = start // tile, near_start // tile, row // tokens
    both = pl.BlockSpec((2, tokens, tile), lambda i, c: (0, block, first + i))
    both_here = pl.BlockSpec((2, tokens, tile), lambda i, c: (0, 0, i))
    one = pl.BlockSpec((tokens, tile), lambda i, c: (block, near_first + i))

    def body(core_ref, keep_ref, *refs):
        *near_refs, far_ref, act_ref = refs

        def total(which):
            part = near_refs[which][...].astype(F32)
            return keep_ref[which] + part + far_ref[which].astype(F32)

        preact = total(0)
        cdf = 0.5 + 0.5 * lax.erf(preact * (0.5**0.5))
        pdf = jnp.exp(-0.5 * preact * preact) * ((0.5 / math.pi) ** 0.5)
        act_ref[0] = (preact * cdf).astype(BF16)
        act_ref[1] = (total(1) * (cdf + preact * pdf)).astype(BF16)

    return call(
        body,
        core,
        [keep, *near, far],
        [both, one, one, both_here],
        jax.ShapeDtypeStruct(far.shape, BF16),
        both_here,
        (width // tile,),
        (60 * tokens * width, 20 * tokens * width),
        "activations",
        after,
    )


def back(core, acts, ups, start, width, before, row, order, leave, after=()):
    tokens = sum(which[0].shape[1] for which in acts)
    depth = ups[0].shape[0]
    tile = tile_of(depth, 512)
    groups = len(acts)

    def body(core_ref, *refs):
        part = None
        for side in range(2):
            mine = [ref[0] for ref in refs[side * groups : (side + 1) * groups]]
            mine = mine[0] if groups == 1 else jnp.concatenate(mine, axis=0)
            term = contract(mine, refs[2 * groups + side][...], 1, 1)
            part = term if part is None else part + term
        refs = refs[2 * groups + 2 :]
        if before is not None:
            part = part + refs[0][...]
        outs = refs[(before is not None) :]
        if leave is None:
            outs[0][...] = part
        else:
            rows = tokens // len(order)
            part = [part[n * rows : (n + 1) * rows] for n in order]
            outs[0][...] = jnp.concatenate(part[:leave], axis=0) if leave > 1 else part[0]
            outs[1][...] = jnp.concatenate(part[leave:], axis=0).astype(BF16)

    kinds = [(tokens, F32)]
    if leave is not None:
        rows = tokens // len(order)
        kinds = [(leave * rows, F32), (tokens - leave * rows, BF16)]
    operands = [which[side] for side in range(2) for which in acts]
    firsts = [which[2] // width for side in range(2) for which in acts]
    return call(
        body,
        core,
        [*operands, *ups] + ([] if before is None else [before]),
        [
            pl.BlockSpec((1, array.shape[1], width), lambda i, c, first=first: (1, 0, first))
            for array, first in zip(operands, firsts)
        ]
        + [pl.BlockSpec((tile, width), lambda i, c: (i, start // width))] * 2
        + ([] if before is None else [pl.BlockSpec((tokens, tile), lambda i, c: (row // tokens, i))]),
        [jax.ShapeDtypeStruct((rows, depth), dtype) for rows, dtype in kinds],
        [pl.BlockSpec((rows, tile), lambda i, c: (0, i)) for rows, _ in kinds],
        (depth // tile,),
        (4 * tokens * depth * width, 4 * depth * width + 4 * tokens * depth),
        "back",
        after,
    )


def fold(core, stay, near, dtype, after=()):
    rows, depth = stay.shape

    def body(core_ref, stay_ref, near_ref, out_ref):
        out_ref[...] = (stay_ref[...] + near_ref[...].astype(F32)).astype(dtype)

    return call(
        body,
        core,
        [stay, near],
        [whole(stay.shape)] * 2,
        jax.ShapeDtypeStruct(stay.shape, dtype),
        whole(stay.shape),
        (1,),
        (rows * depth, 8 * rows * depth),
        "fold",
        after,
    )


def arrange(core, units, after=()):
    _, rows, depth = units[0].shape
    tokens = rows * len(units)

    def body(core_ref, *refs):
        *unit_refs, inputs_t, cotan = refs
        inputs_t[...] = jnp.concatenate([ref[0] for ref in unit_refs], axis=0).T
        cotan[...] = jnp.concatenate([ref[1] for ref in unit_refs], axis=0)

    return call(
        body,
        core,
        units,
        [whole(units[0].shape)] * len(units),
        [jax.ShapeDtypeStruct((depth, tokens), BF16), jax.ShapeDtypeStruct((tokens, depth), BF16)],
        [whole((depth, tokens)), whole((tokens, depth))],
        (1,),
        (0, 8 * tokens * depth),
        "arrange",
        after,
    )


def weight_grads(core, inputs_t, cotan, sides, acts, start, width, shape, outputs, after=()):
    depth, full = shape
    tokens = cotan.shape[0]
    half = full // 2
    tile = tile_of(width, 256)
    steps = width // tile
    groups = len(acts[0])

    def body(core_ref, inputs_ref, cotan_ref, *refs):
        up_out, down_out, done = refs[-3:]
        done[...] = jnp.zeros_like(done)
        for order in range(len(sides)):
            mine = refs[order * groups : (order + 1) * groups]

            @pl.when(pl.program_id(0) // steps == order)
            def _(mine=mine):
                hidden = jnp.concatenate([ref[0] for ref in mine], axis=0)
                grad = jnp.concatenate([ref[1] for ref in mine], axis=0)
                up_out[...] = contract(inputs_ref[...], grad, 1, 0)
                down_out[...] = contract(hidden, cotan_ref[...], 0, 0)

    def place(i, c):
        which = side_of(c, sides[0])
        if len(sides) > 1:
            which = jnp.where(i // steps == 0, which, 1 - which)
        return which * (half // tile) + start // tile + i % steps

    operands = [inputs_t, cotan]
    specs = [whole(inputs_t.shape), whole(cotan.shape)]
    for order in range(len(sides)):
        for array, offset in acts[order]:

            def index(i, c, order=order, first=offset // tile):
                return (0, 0, first + jnp.clip(i - order * steps, 0, steps - 1))

            operands.append(array)
            specs.append(pl.BlockSpec((2, array.shape[1], tile), index))
    aliases = None
    if outputs is not None:
        aliases = {len(operands) + 1: 0, len(operands) + 2: 1}
        operands += list(outputs)
        specs += [pl.BlockSpec(memory_space=pl.ANY)] * 2
    many = width * len(sides)
    return call(
        body,
        core,
        operands,
        specs,
        [
            jax.ShapeDtypeStruct((depth, full), F32),
            jax.ShapeDtypeStruct((full, depth), F32),
            jax.ShapeDtypeStruct((8, 128), F32),
        ],
        [
            pl.BlockSpec((depth, tile), lambda i, c: (0, place(i, c))),
            pl.BlockSpec((tile, depth), lambda i, c: (place(i, c), 0)),
            whole((8, 128)),
        ],
        (steps * len(sides),),
        (4 * tokens * depth * many, 8 * depth * many),
        "weight_grads",
        after,
        aliases=aliases,
        limit=GRADS_VMEM_LIMIT,
    )


def swap(value, axis, size, bits):
    return lax.ppermute(value, axis, [(i, i ^ bits) for i in range(size)])


def cube_body(inputs, cotangent, up, down):
    rows = inputs.shape[0]
    half = up.shape[1] // 2
    width = half // 2
    core = (lax.axis_index("gy") % 2).astype(jnp.int32).reshape(1)

    unit = {(0, 0): jnp.stack([inputs, cotangent])}
    unit[0, 1] = swap(unit[0, 0], "gx", 2, 1)
    unit[1, 0] = swap(unit[0, 0], "gz", 4, 1)
    z = lax.axis_index("gz")
    middle = (z == 1) | (z == 2)
    across, outward = [(1, 2), (2, 1)], [(1, 0), (2, 3)]
    first = lax.ppermute(unit[0, 0], "gz", across)
    ups, downs = {}, {}
    second = lax.ppermute(unit[1, 0], "gz", across)
    first_on = lax.ppermute(first, "gz", outward)
    second_on = lax.ppermute(second, "gz", outward)
    unit[2, 0] = jnp.where(middle, second, first_on)
    unit[3, 0] = jnp.where(middle, first, second_on)
    for d in (1, 2, 3):
        unit[d, 1] = swap(unit[d, 0], "gx", 2, 1)
    groups = [
        [unit[0, 0], unit[0, 1]],
        [unit[1, 0], unit[1, 1]],
        [unit[2, 0], unit[2, 1], unit[3, 0], unit[3, 1]],
    ]

    pair = 2 * rows
    pieces = [
        (0, 0, pair, 0, half),
        (1, 0, pair, 0, half),
        (2, 0, 2 * pair, 0, width),
        (2, 0, pair, width, width),
        (2, pair, pair, width, width),
    ]
    near, keep, far, act, act_near = {}, {}, {}, {}, {}

    def send(group, after=()):
        if group:
            out = partial_sums(
                core, groups[group], ups[1], downs[1], 1, True, 0, half, after
            )
        else:
            *out, ups[1], downs[1] = bring_and_sum(core, groups[group], 1, up, down, after)
        near[group] = [swap(array, "gy", 4, 1) for array in out]
        return [out[0]]

    def hold(group, start, size, after):
        if group:
            out, = partial_sums(
                core, groups[group], ups[0], downs[0], 0, False, start, size, after
            )
        else:
            out, ups[0], downs[0] = bring_and_sum(core, groups[group], 0, up, down, after)
        keep[group, start] = out
        return [out]

    def kept(group, start):
        return (keep[group, start], 0) if (group, start) in keep else (keep[group, 0], start)

    def cross(n, after=()):
        group, row, count, start, size = pieces[n]
        array, column = kept(group, start)
        if after:
            chip = combine(core, array, near[group], row, count, column, start, size, after)
        else:
            chip = jnp.stack([
                (
                    array[which, row : row + count, column : column + size]
                    + near[group][which][row : row + count, start : start + size].astype(F32)
                ).astype(BF16)
                for which in range(2)
            ])
        far[n] = swap(chip, "gy", 4, 2)
        return [chip]

    def ready(n, after):
        group, row, _, start, _ = pieces[n]
        array, column = kept(group, start)
        act[n] = activations(core, array, near[group], far[n], row, column, start, after)
        act_near[n] = swap(act[n], "gy", 4, 1)
        return [act[n]]

    def inward(which, start, size, part, row, order, leave, after):
        acts = [(act[n], act_near[n], offset) for n, offset in which]
        return back(core, acts, (ups[0], ups[1]), start, size, part, row, order, leave, after)

    outputs = None

    def gradients(j, sides, after):
        acts = [
            [(array[n], j * width) for n in range(2)]
            + ([(array[3], 0), (array[4], 0)] if j else [(array[2], 0)])
            for array in (act, act_near)
        ]
        acts = [acts[side] for side in sides]
        return weight_grads(
            core, inputs_t, cotan, sides, acts, j * width, width, up.shape, outputs, after
        )

    def finish(j, sides, after):
        nonlocal outputs
        *outputs, done = gradients(j, sides, after)
        return [done]

    last = send(0)
    last = hold(0, 0, half, last)
    last = cross(0, [*last, unit[1, 1]])
    last = send(1, [*last, first_on, second])
    last = hold(1, 0, half, [*last, second_on])
    last = ready(0, [*last, unit[2, 1]])
    last = cross(1, last)
    last = send(2, last)
    last = hold(2, 0, half, last)
    last = ready(1, last)
    last = cross(2) + last
    inputs_t, cotan = arrange(core, [u for group in groups for u in group], last)
    stay1, go1 = inward(((0, 0), (1, 0)), 0, half, None, 0, (0, 2, 1, 3), 2, [inputs_t])
    near1 = swap(go1, "gx", 2, 1)

    last = ready(2, [stay1])
    last = cross(3, last)
    last = finish(0, (0,), last)
    last = ready(3, last)
    last = cross(4, last)
    total = fold(core, stay1[:rows], near1[:rows], F32, last)
    back1 = fold(core, stay1[rows:], near1[rows:], BF16, [total])
    far1 = swap(back1, "gz", 4, 1)
    part, = inward(((2, 0),), 0, width, None, 0, None, None, [back1])
    last = finish(0, (1,), [part])
    stay2, go2 = inward(((3, 0),), width, width, part, 0, (0, 1), 1, last)
    near2 = swap(go2, "gx", 2, 1)
    total = fold(core, total, far1, F32, [stay2])
    last = ready(4, [total])
    stay3, go3 = inward(((4, 0),), width, width, part, pair, (0, 1), 1, last)
    near3 = swap(go3, "gx", 2, 1)
    back2 = fold(core, stay2, near2, BF16, [stay3])
    far2 = swap(back2, "gz", 4, 2)
    last = finish(1, (0,), [back2])
    back3 = fold(core, stay3, near3, BF16, last)
    far3 = swap(back3, "gz", 4, 3)
    finish(1, (1,), [back3])
    total = total + far2.astype(F32) + far3.astype(F32)
    return (total.astype(BF16), *outputs)


def solution(mesh):
    placed = (
        P(("gx", "gz"), "gy"),
        P(("gx", "gz"), "gy"),
        P("gy", ("gz", "gx")),
        P(("gz", "gx"), "gy"),
    )
    cube = tuple(mesh.shape[axis] for axis in ("gx", "gy", "gz")) == (2, 4, 4)
    return jax.shard_map(
        cube_body if cube else general_body,
        mesh=mesh,
        in_specs=placed,
        out_specs=(P(("gx", "gz"), "gy"), P("gy", ("gz", "gx")), P(("gz", "gx"), "gy")),
        check_vma=False,
    )
```
